128 devices in a mesh: dp: 4 (over z), tensor: 32 (over y, x, core).
Axes of the slice: x: 4, y: 4, z: 4, core: 2. Of those that a mesh axis runs over, the one named last changes fastest.
Arguments:
- queries: bfloat16 [128, 576, 128], P(('dp', 'tensor')), may hold values from -40 to 40
- cache_pool: bfloat16 [1024, 576, 128], P(('dp', 'tensor')), may hold values from -6 to 6
- holder: int32 [128, 32], P(None, 'tensor'), may hold values from 0 to 3, as said below
- slot_ids: int32 [128, 32], P(None, 'tensor'), may hold values from 0 to 7
- lengths: int32 [128], replicated, may hold values from 1 to 4096, as said below
- residual: bfloat16 [128, 7168], P('dp'), may hold values from -6 to 6
- w_value: bfloat16 [128, 512, 128], P('tensor'), may hold values from -1 to 1
- w_out: bfloat16 [16384, 7168], P('tensor'), may hold values from -0.09375 to 0.09375
- norm_gain: float32 [7168], replicated, may hold values from 0.1 to 1.9
- w_gate: bfloat16 [7168, 12288], P(None, 'tensor'), may hold values from -0.0625 to 0.0625
- w_up: bfloat16 [7168, 12288], P(None, 'tensor'), may hold values from -0.0625 to 0.0625
- w_down: bfloat16 [12288, 7168], P('tensor'), may hold values from -0.0546875 to 0.0546875
Outputs:
- layer_out: float32 [128, 7168], P(('dp', 'tensor'))
The draws below stay inside these ranges and needn't reach their ends.
Inputs may be any that keep to these rules, and one draw needn't show every extreme that they name: `holder`: among the 32 entries of the requests of one data-parallel rank at the block positions of one tensor index, no rank is named more than 12 times, and one rank exactly 12 times. `lengths`: some request has 4096 tokens and some has 1.
All inputs are finite; a program needn't handle non-finite values.
Results may differ from the reference program's by a relative error of at most 0.011.
Values may be sent and summed in bfloat16 or wider, within the bound.
No kernel may reach another device: no remote copies, remote signals or barrier semaphores. Data moves between devices by JAX's collectives and lax.ppermute only.
A program may use at most 576 MiB of HBM per device.

```python
import jax
import jax.numpy as jnp
from jax import lax

H = 128
DL = 512
VH = 128
D = 7168
FF = 12288
CT = 128
NCH = 32
REQ_DEV = 1
SLOTS = 8
E = 576
WIN = 4096
REQS = 128
GROUP_REQS = 32
PC = 1
CAPACITY = 12
N_DP = 4
N_TENSOR = 32
DEVICES = 128


def draw_queries(key, part):
    key = jax.random.fold_in(key, 11)
    base_draw = jax.random.normal(key, (REQS, E, H), jnp.float32)
    return jnp.clip(base_draw, -6.0, 6.0).astype(jnp.bfloat16)


def draw_holder(key, part):
    key = jax.random.fold_in(key, 23)
    item_count = REQ_DEV * NCH
    block_count = N_DP * N_TENSOR
    shuffle_key, heavy_key = jax.random.split(key)
    shuffles = jax.vmap(lambda one_key: jax.random.permutation(one_key, item_count))(jax.random.split(shuffle_key, block_count))
    inverse = jnp.argsort(shuffles, axis=1).astype(jnp.int32)
    heavy = jax.random.randint(heavy_key, (block_count, 1), 0, N_DP)
    extra = jnp.maximum(inverse - CAPACITY, 0) % (N_DP - 1)
    owners = jnp.where(inverse < CAPACITY, heavy, (heavy + 1 + extra) % N_DP)
    owners = owners.reshape(N_DP, N_TENSOR, GROUP_REQS, PC)
    return jnp.transpose(owners, (0, 2, 1, 3)).reshape(REQS, NCH).astype(jnp.int32)


def draw_lengths(key, part):
    key = jax.random.fold_in(key, 37)
    base_key, long_key, short_key = jax.random.split(key, 3)
    base_draw = jax.random.randint(base_key, (REQS,), 1, WIN + 1)
    longest = jax.random.randint(long_key, (), 0, REQS)
    shortest = (longest + 1 + jax.random.randint(short_key, (), 0, REQS - 1)) % REQS
    return base_draw.at[longest].set(WIN).at[shortest].set(1).astype(jnp.int32)


def set_ends(drawn, key, smallest, top_value):
    shape = drawn.shape
    index_at = [jax.random.randint(jax.random.fold_in(key, axis), (), 0, shape[axis]) for axis in range(len(shape))]
    drawn = drawn.at[tuple(index_at)].set(smallest)
    longest = shape.index(max(shape))
    index_at[longest] = (index_at[longest] + 1) % shape[longest]
    return drawn.at[tuple(index_at)].set(top_value)


def steps_of(key, dims, pieces, least, high):
    level = 1.0
    for axis_at, blocks in pieces:
        steps = jax.random.uniform(jax.random.fold_in(jax.random.fold_in(key, 6), axis_at), (blocks,), jnp.float32, least / len(pieces), high / len(pieces))
        level = level * jnp.repeat(jnp.exp(steps), dims[axis_at] // blocks).reshape((-1,) + (1,) * (len(dims) - 1 - axis_at))
    return level


def gaussian(own_key, shape, scale, most, shards=(), kind=jnp.bfloat16):
    values = jax.random.normal(own_key, shape, jnp.float32) * scale
    if len(shards) > 0:
        values = steps_of(own_key, shape, shards, -0.22, 0.18) * values
    return jnp.clip(values, min=-most, max=most).astype(kind)


def setup_inputs(seed: int = 0) -> dict:
    arg_keys = jax.random.split(jax.random.key(seed), 13)
    return {
        "queries": draw_queries(jax.random.fold_in(arg_keys[12], 71), 0),
        "cache_pool": gaussian(arg_keys[1], (SLOTS * DEVICES, E, CT), 1.0, 6.0, ((0, 128),)),
        "holder": draw_holder(jax.random.fold_in(arg_keys[12], 71), 0),
        "slot_ids": set_ends(jax.random.randint(arg_keys[3], (REQS, NCH), 0, SLOTS), jax.random.fold_in(arg_keys[3], 1), 0, SLOTS - 1).astype(jnp.int32),
        "lengths": draw_lengths(jax.random.fold_in(arg_keys[12], 71), 0),
        "residual": gaussian(arg_keys[5], (REQS, D), 1.0, 6.0, ((0, 4),)),
        "w_value": gaussian(arg_keys[6], (H, DL, VH), (DL // 16) ** -0.5, 1.0, ((0, 32),)),
        "w_out": gaussian(arg_keys[7], (H * VH, D), (H * VH // 4) ** -0.5, 0.09375, ((0, 32),)),
        "norm_gain": jnp.clip(1.0 + 0.18 * jax.random.normal(arg_keys[8], (D,), jnp.float32), 0.1, 1.9),
        "w_gate": gaussian(arg_keys[9], (D, FF), D ** -0.5, 0.0625, ((1, 32),)),
        "w_up": gaussian(arg_keys[10], (D, FF), D ** -0.5, 0.0625, ((1, 32),)),
        "w_down": gaussian(arg_keys[11], (FF, D), FF ** -0.5, 0.0546875, ((0, 32),)),
    }


score_scale = 192.0 ** (-0.5)
norm_eps = 1e-06

def attend_request(query_row, holder_row, slot_row, length, cache_pool):
    column = jnp.arange(NCH, dtype=jnp.int32) // PC
    device = holder_row.astype(jnp.int32) * N_TENSOR + column
    pool_rows = (device * SLOTS + slot_row.astype(jnp.int32)).astype(jnp.int32)
    gathered = jnp.take(cache_pool, pool_rows, axis=0)
    key_block = jnp.transpose(gathered, (1, 0, 2)).reshape(E, WIN)
    scores = jnp.dot(query_row.T, key_block, preferred_element_type=jnp.float32) * score_scale
    live_mask = jnp.arange(WIN, dtype=jnp.int32)[None, :] < length
    row_top = lax.optimization_barrier(jnp.max(jnp.where(live_mask, scores, -jnp.inf), axis=1, keepdims=True))
    weights = jnp.exp(jnp.where(live_mask, scores - row_top, -jnp.inf))
    total_sum = lax.optimization_barrier(jnp.sum(weights, axis=1, keepdims=True))
    mixed = jnp.dot(weights.astype(jnp.bfloat16), key_block[:DL].T, preferred_element_type=jnp.float32)
    return (mixed / total_sum).astype(jnp.bfloat16)

def reference(queries, cache_pool, holder, slot_ids, lengths, residual, w_value, w_out, norm_gain, w_gate, w_up, w_down):

    def one_request(packed):
        return attend_request(packed[0], packed[1], packed[2], packed[3], cache_pool)
    attended = lax.map(one_request, (queries, holder, slot_ids, lengths))
    per_head = jnp.einsum('rhd,hdv->rhv', attended.astype(jnp.float32), w_value.astype(jnp.float32)).astype(jnp.bfloat16)
    attention = jnp.dot(per_head.reshape(REQS, H * VH), w_out, preferred_element_type=jnp.float32)
    residual_sum = residual.astype(jnp.float32) + attention
    scale_inv = lax.rsqrt(lax.optimization_barrier(jnp.mean(residual_sum * residual_sum, axis=1, keepdims=True)) + norm_eps)
    normed = (residual_sum * scale_inv * norm_gain[None, :]).astype(jnp.bfloat16)
    gate_val = jnp.dot(normed, w_gate, preferred_element_type=jnp.float32)
    up_val = jnp.dot(normed, w_up, preferred_element_type=jnp.float32)
    activated = (jax.nn.silu(gate_val) * up_val).astype(jnp.bfloat16)
    down_val = jnp.dot(activated, w_down, preferred_element_type=jnp.float32)
    return (residual_sum + down_val).astype(jnp.float32)
```

```python
import functools

import jax
import jax.numpy as jnp
from jax import lax
from jax.experimental import pallas as pl
from jax.experimental.pallas import tpu as pltpu
from jax.sharding import PartitionSpec as P

score_scale = 192.0 ** (-0.5)
norm_eps = 1e-06
far_below = -1e30
CORES = 2
LANES = 128


def attend_kernel(heads, group, latent, head_local, scal_ref, *refs):
    q_hbm = refs[0]
    pieces = refs[1:15]
    out_ref, kbuf, qbuf, acc, lse_buf, sems = refs[15:]
    width = kbuf.shape[2]
    block_len = kbuf.shape[3]
    owners = heads // head_local
    copies = [pltpu.make_async_copy(q_hbm, qbuf, sems.at[14])]
    half = pieces[1].shape[0]
    spots = [(0, 2 * half), (2 * half, half), (3 * half, half), (6 * half, half), (7 * half, half), (4 * half, half), (5 * half, half)]
    for side in range(2):
        for at, (first, count) in enumerate(spots):
            copies.append(
                pltpu.make_async_copy(
                    pieces[side * 7 + at],
                    kbuf.at[side, pl.ds(first, count)],
                    sems.at[side * 7 + at],
                )
            )
    for one in copies:
        one.start()
    lse_buf[...] = jnp.zeros_like(lse_buf)
    for one in copies:
        one.wait()
    base_own = scal_ref[3, 0]
    base_other = scal_ref[3, 1]
    token = lax.broadcasted_iota(jnp.int32, (heads, 2 * block_len), 1)
    position = jnp.where(token < block_len, token + base_own, token - block_len + base_other)
    lane = lax.broadcasted_iota(jnp.int32, (heads, LANES), 1)

    def four(step, carry):
        parts = []
        for i in range(4):
            r = step * 4 + i
            keys = jnp.concatenate([kbuf[0, scal_ref[0, r]], kbuf[1, scal_ref[1, r]]], axis=1)
            scores = jnp.dot(qbuf[r], keys, preferred_element_type=jnp.float32) * score_scale
            live = position < scal_ref[2, r]
            masked = jnp.where(live, scores, far_below)
            top = jnp.max(masked, axis=1, keepdims=True)
            weights = jnp.where(live, jnp.exp(masked - top), 0.0)
            total = jnp.sum(weights, axis=1, keepdims=True)
            mixed = lax.dot_general(
                weights.astype(jnp.bfloat16),
                keys[:latent],
                (((1,), (1,)), ((), ())),
                preferred_element_type=jnp.float32,
            )
            some = total > 0.0
            safe = jnp.where(some, total, 1.0)
            mixed = mixed * jnp.where(some, 1.0 / safe, 0.0)
            lse = jnp.where(some, top + jnp.log(safe), far_below)
            lse_buf[...] = jnp.where(lane == r, lse, lse_buf[...])
            parts.append(mixed)
        rows_at = pl.ds(pl.multiple_of(step * 4 * head_local, 4 * head_local), 4 * head_local)
        for k in range(owners):
            acc[k, rows_at, :] = jnp.concatenate(
                [one[k * head_local : (k + 1) * head_local] for one in parts], axis=0
            )
        return carry

    lax.fori_loop(0, group // 4, four, 0)
    rows = group * head_local
    for piece in range(latent // LANES):
        out_ref[:, piece * rows : (piece + 1) * rows, :] = acc[
            :, :, piece * LANES : (piece + 1) * LANES
        ].astype(jnp.bfloat16)
    lse_all = lse_buf[...]
    high = lse_all.astype(jnp.bfloat16).astype(jnp.float32)
    mid = (lse_all - high).astype(jnp.bfloat16).astype(jnp.float32)
    low = lse_all - high - mid
    tail = latent // LANES * rows
    for k in range(owners):
        own = slice(k * head_local, (k + 1) * head_local)
        out_ref[k, tail:, :] = jnp.concatenate(
            [high[own], mid[own], low[own], jnp.zeros_like(low[own])], axis=0
        ).astype(jnp.bfloat16)


def attend(scalars, q_all, pieces, latent, head_local):
    group, heads, width = q_all.shape
    slots, _, block_len = pieces[0].shape
    owners = heads // head_local
    rows = group * head_local
    out_rows = latent // LANES * rows + 16
    any_spec = pl.BlockSpec(memory_space=pl.ANY)
    return pl.pallas_call(
        functools.partial(attend_kernel, heads, group, latent, head_local),
        out_shape=jax.ShapeDtypeStruct((owners, out_rows, LANES), jnp.bfloat16),
        in_specs=[pl.BlockSpec(memory_space=pltpu.SMEM)] + [any_spec] * 15,
        out_specs=pl.BlockSpec(memory_space=pltpu.VMEM),
        scratch_shapes=[
            pltpu.VMEM((2, 4 * slots, width, block_len), jnp.bfloat16),
            pltpu.VMEM((group, heads, width), jnp.bfloat16),
            pltpu.VMEM((owners, rows, latent), jnp.float32),
            pltpu.VMEM((heads, LANES), jnp.float32),
            pltpu.SemaphoreType.DMA((15,)),
        ],
        compiler_params=pltpu.CompilerParams(vmem_limit_bytes=40 * 1024 * 1024),
        name="attend",
    )(scalars, q_all, *pieces)


def body(
    queries,
    cache_pool,
    holder,
    slot_ids,
    lengths,
    residual,
    w_value,
    w_out,
    norm_gain,
    w_gate,
    w_up,
    w_down,
):
    ranks = lax.axis_size("dp")
    tensors = lax.axis_size("tensor")
    my_rank = lax.axis_index("dp")
    column = lax.axis_index("tensor")
    core = column % CORES
    chips = tensors // CORES
    group = residual.shape[0]
    slots, width, block_len = cache_pool.shape
    head_local, latent, value_width = w_value.shape
    heads = head_local * chips
    features = residual.shape[1]
    tiles = features // LANES
    swap = [(i, i ^ 1) for i in range(tensors)]
    same_core = [[c + CORES * k for k in range(chips)] for c in range(CORES)]
    from_next = [((i + 1) % ranks, i) for i in range(ranks)]
    from_prev = [((i - 1) % ranks, i) for i in range(ranks)]

    def swapped(value):
        return lax.ppermute(value, "tensor", swap)

    half = slots // 2
    lo, hi = cache_pool[:half], cache_pool[half:]
    next_lo = lax.ppermute(lo, "dp", from_next)
    prev_hi = lax.ppermute(hi, "dp", from_prev)
    next_hi = lax.ppermute(hi, "dp", from_next)
    prev_lo = lax.ppermute(lo, "dp", from_prev)
    far_lo = lax.ppermute(next_lo, "dp", from_next)
    far_hi = lax.ppermute(prev_hi, "dp", from_prev)
    mine = [cache_pool, next_lo, next_hi, prev_lo, prev_hi, far_lo, far_hi]
    others = [swapped(one) for one in mine]

    want = jnp.arange(2 * heads, dtype=jnp.int32)
    side, rest = want // heads, want % heads
    chosen_core = jnp.where(side == 0, core, 1 - core)
    head_id = (rest // head_local) * (CORES * head_local) + chosen_core * head_local + rest % head_local
    select = (head_id[:, None] == jnp.arange(2 * heads, dtype=jnp.int32)[None, :]).astype(jnp.bfloat16)
    turned = lax.dot_general(
        select, queries[0], (((1,), (1,)), ((), ())), preferred_element_type=jnp.float32
    ).astype(jnp.bfloat16)
    q_keep, q_send = turned[:heads], turned[heads:]
    q_got = swapped(q_send)
    q_pair = jnp.stack([jnp.where(core == 0, q_keep, q_got), jnp.where(core == 0, q_got, q_keep)])
    q_all = lax.all_gather(q_pair, "tensor", axis=0, tiled=True, axis_index_groups=same_core)

    first = my_rank * group
    own_holder = lax.dynamic_slice_in_dim(holder[:, 0], first, group)
    own_slots = lax.dynamic_slice_in_dim(slot_ids[:, 0], first, group)
    place = ((own_holder - my_rank) % ranks) * slots + own_slots
    place_other = swapped(place)
    group_lengths = lax.dynamic_slice_in_dim(lengths, first, group)
    bases = jnp.zeros((group,), jnp.int32).at[0].set(column * block_len).at[1].set((column ^ 1) * block_len)
    scalars = jnp.stack([place, place_other, group_lengths, bases])

    partial = attend(scalars, q_all, mine + others, latent, head_local)
    parts = lax.all_to_all(
        partial, "tensor", split_axis=0, concat_axis=0, tiled=True, axis_index_groups=same_core
    )
    rows = group * head_local
    pieces = latent // LANES
    lse3 = parts[:, pieces * rows :, :group].astype(jnp.float32).reshape(chips, 4, head_local, group)
    lse = lse3[:, 0] + lse3[:, 1] + lse3[:, 2]
    share = jnp.exp(lse - jnp.max(lse, axis=0, keepdims=True))
    share = share / jnp.sum(share, axis=0, keepdims=True)
    share = jnp.transpose(share, (0, 2, 1)).reshape(chips, 1, rows, 1)
    latents = parts[:, : pieces * rows].astype(jnp.float32).reshape(chips, pieces, rows, LANES)
    attended = jnp.sum(latents * share, axis=0).astype(jnp.bfloat16)
    attended = attended.reshape(pieces, group, head_local, LANES)
    per_head = jnp.einsum(
        "prhd,hpdv->rhv",
        attended,
        w_value.reshape(head_local, pieces, LANES, value_width),
        preferred_element_type=jnp.float32,
    ).astype(jnp.bfloat16)

    def to_rows(value):
        sent = value.astype(jnp.bfloat16).reshape(group, tiles, LANES)
        got = lax.all_to_all(sent, "tensor", split_axis=0, concat_axis=0, tiled=True)
        return jnp.sum(got.astype(jnp.float32), axis=0)

    attention = to_rows(
        jnp.dot(per_head.reshape(group, -1), w_out, preferred_element_type=jnp.float32)
    )
    own_residual = lax.dynamic_index_in_dim(residual, column, 0, keepdims=False)
    residual_sum = own_residual.astype(jnp.float32).reshape(tiles, LANES) + attention
    scale_inv = lax.rsqrt(jnp.mean(residual_sum * residual_sum) + norm_eps)
    normed = (residual_sum * scale_inv * norm_gain.reshape(tiles, LANES)).astype(jnp.bfloat16)
    normed_all = lax.all_to_all(
        jnp.broadcast_to(normed[None], (group, tiles, LANES)),
        "tensor",
        split_axis=0,
        concat_axis=0,
        tiled=True,
    ).reshape(group, features)
    gate_val = jnp.dot(normed_all, w_gate, preferred_element_type=jnp.float32)
    up_val = jnp.dot(normed_all, w_up, preferred_element_type=jnp.float32)
    activated = (jax.nn.silu(gate_val) * up_val).astype(jnp.bfloat16)
    down = to_rows(jnp.dot(activated, w_down, preferred_element_type=jnp.float32))
    return (residual_sum + down).reshape(1, features)


def solution(mesh):
    in_specs = (
        P(("dp", "tensor"), None, None),
        P(("dp", "tensor"), None, None),
        P(None, "tensor"),
        P(None, "tensor"),
        P(),
        P("dp", None),
        P("tensor", None, None),
        P("tensor", None),
        P(),
        P(None, "tensor"),
        P(None, "tensor"),
        P("tensor", None),
    )
    out_specs = P(("dp", "tensor"), None)
    return jax.shard_map(body, mesh=mesh, in_specs=in_specs, out_specs=out_specs, check_vma=False)
```

```python
import functools

import jax
import jax.numpy as jnp
from jax import lax
from jax.experimental import pallas as pl
from jax.experimental.pallas import tpu as pltpu
from jax.sharding import PartitionSpec as P

score_scale = 192.0 ** (-0.5)
norm_eps = 1e-06
far_below = -1e30
CORES = 2
LANES = 128
MIB = 1024 * 1024
hbm_spec = pl.BlockSpec(memory_space=pl.ANY)
vmem_spec = pl.BlockSpec(memory_space=pltpu.VMEM)
smem_spec = pl.BlockSpec(memory_space=pltpu.SMEM)


def in_vmem(value):
    return pltpu.with_memory_space_constraint(value, pltpu.VMEM)


def in_hbm(value):
    return pltpu.with_memory_space_constraint(value, pltpu.HBM)


def split_kernel(pool, low, high, sems):
    half = low.shape[0]
    copies = [
        pltpu.make_async_copy(pool.at[pl.ds(i * half, half)], one, sems.at[i])
        for i, one in enumerate((low, high))
    ]
    for one in copies:
        one.start()
    for one in copies:
        one.wait()


def split_pool(pool):
    half = (pool.shape[0] // 2,) + pool.shape[1:]
    return pl.pallas_call(
        split_kernel,
        out_shape=(pltpu.VMEM(half, pool.dtype), pltpu.VMEM(half, pool.dtype)),
        in_specs=[hbm_spec],
        out_specs=(vmem_spec, vmem_spec),
        scratch_shapes=[pltpu.SemaphoreType.DMA((2,))],
        compiler_params=pltpu.CompilerParams(vmem_limit_bytes=4 * MIB),
        name="split_pool",
    )(in_hbm(pool))


def stage_kernel(count, *refs):
    copies = [
        pltpu.make_async_copy(refs[i], refs[count + i], refs[2 * count].at[i]) for i in range(count)
    ]
    for one in copies:
        one.start()
    for one in copies:
        one.wait()


def stage(*weights):
    count = len(weights)
    size = sum(one.size * one.dtype.itemsize for one in weights)
    return pl.pallas_call(
        functools.partial(stage_kernel, count),
        out_shape=tuple(pltpu.VMEM(one.shape, one.dtype) for one in weights),
        in_specs=[hbm_spec] * count,
        out_specs=(vmem_spec,) * count,
        scratch_shapes=[pltpu.SemaphoreType.DMA((count,))],
        compiler_params=pltpu.CompilerParams(vmem_limit_bytes=4 * MIB),
        cost_estimate=pl.CostEstimate(flops=0, bytes_accessed=2 * size, transcendentals=0),
        name="stage",
    )(*[in_hbm(one) for one in weights])


QUERY_PARTS = 4
UNROLL = 8


def attend_kernel(dims, code_own, code_other, lengths, q_hbm, *refs):
    slots, ranks, head_local, latent, piece_count = dims
    pieces = refs[:piece_count]
    out_ref, kbuf, qraw, qbuf, lse_buf, sems = refs[piece_count:]
    group = q_hbm.shape[0]
    portion, heads, _ = qbuf.shape
    block_len = kbuf.shape[2]
    owners = heads // head_local
    my_rank = lax.axis_index("dp")
    column = lax.axis_index("tensor")
    core = column % CORES
    first = my_rank * group
    q_copies = [
        pltpu.make_async_copy(
            q_hbm.at[pl.ds(i * portion, portion)],
            qraw.at[i % 2],
            sems.at[piece_count + i],
        )
        for i in range(QUERY_PARTS)
    ]
    copies = []
    at = 0
    for i, one in enumerate(pieces):
        copies.append(pltpu.make_async_copy(one, kbuf.at[pl.ds(at, one.shape[0])], sems.at[i]))
        at += one.shape[0]
    for one in q_copies[:2] + copies:
        one.start()
    row = lax.broadcasted_iota(jnp.int32, (heads, CORES * heads), 0)
    wanted = (row // head_local) * (CORES * head_local) + core * head_local + row % head_local
    hit = lax.broadcasted_iota(jnp.int32, (heads, CORES * heads), 1) == wanted
    select = jnp.where(hit, 1.0, 0.0).astype(jnp.bfloat16)
    token = lax.broadcasted_iota(jnp.int32, (1, 2 * block_len), 1)
    partner = column + 1 - 2 * core
    position = jnp.where(
        token < block_len, token + column * block_len, token - block_len + partner * block_len
    )
    lane = lax.broadcasted_iota(jnp.int32, (heads, LANES), 1)
    lse_buf[...] = jnp.zeros_like(lse_buf)
    for one in copies:
        one.wait()

    def place(codes, r):
        code = codes[0, first + r]
        return ((code // slots - my_rank + ranks) % ranks) * slots + code % slots

    def turn(slot, step, carry):
        for i in range(UNROLL):
            r = step * UNROLL + i
            qbuf[r] = lax.dot_general(
                select, qraw[slot, r], (((1,), (1,)), ((), ())), preferred_element_type=jnp.float32
            ).astype(jnp.bfloat16)
        return carry

    def several(step, carry):
        rs = [step * UNROLL + i for i in range(UNROLL)]
        keys = [
            jnp.concatenate(
                [kbuf[place(code_own, r)], kbuf[ranks * slots + place(code_other, r)]], axis=1
            )
            for r in rs
        ]
        scores = [
            jnp.dot(qbuf[r % portion], key, preferred_element_type=jnp.float32) * score_scale
            for r, key in zip(rs, keys)
        ]
        weights, scales, lses = [], [], []
        for r, score in zip(rs, scores):
            live = position < lengths[0, first + r]
            masked = jnp.where(live, score, far_below)
            top = jnp.max(masked, axis=1, keepdims=True)
            weight = jnp.where(live, jnp.exp(masked - top), 0.0)
            total = jnp.sum(weight, axis=1, keepdims=True)
            some = total > 0.0
            safe = jnp.where(some, total, 1.0)
            weights.append(weight.astype(jnp.bfloat16))
            scales.append(jnp.where(some, 1.0 / safe, 0.0))
            lses.append(jnp.where(some, top + jnp.log(safe), far_below))
        mixed = [
            lax.dot_general(
                weight, key[:latent], (((1,), (1,)), ((), ())), preferred_element_type=jnp.float32
            )
            * scale
            for weight, key, scale in zip(weights, keys, scales)
        ]
        lse_all = lse_buf[...]
        for r, lse in zip(rs, lses):
            lse_all = jnp.where(lane == r, lse, lse_all)
        lse_buf[...] = lse_all
        count = UNROLL * head_local
        for k in range(owners):
            both = jnp.concatenate(
                [one[k * head_local : (k + 1) * head_local] for one in mixed], axis=0
            ).astype(jnp.bfloat16)
            for p in range(latent // LANES):
                rows_at = pl.multiple_of(p * group * head_local + step * count, count)
                out_ref[k, pl.ds(rows_at, count), :] = both[:, p * LANES : (p + 1) * LANES]
        return carry

    for i in range(QUERY_PARTS):
        q_copies[i].wait()
        steps = portion // UNROLL
        lax.fori_loop(0, steps, functools.partial(turn, i % 2), 0)
        if i + 2 < QUERY_PARTS:
            q_copies[i + 2].start()
        lax.fori_loop(i * steps, (i + 1) * steps, several, 0)
    lse_all = lse_buf[...]
    high = lse_all.astype(jnp.bfloat16).astype(jnp.float32)
    mid = (lse_all - high).astype(jnp.bfloat16).astype(jnp.float32)
    low = lse_all - high - mid
    tail = latent // LANES * group * head_local
    for k in range(owners):
        own = slice(k * head_local, (k + 1) * head_local)
        out_ref[k, tail:, :] = jnp.concatenate(
            [high[own], mid[own], low[own], jnp.zeros_like(low[own])], axis=0
        ).astype(jnp.bfloat16)


def attend(code_own, code_other, lengths, q_all, pieces, ranks, latent, head_local):
    group, width, head_total = q_all.shape
    heads = head_total // CORES
    block_len = pieces[0].shape[2]
    blocks = sum(one.shape[0] for one in pieces)
    owners = heads // head_local
    rows = group * head_local
    out_rows = latent // LANES * rows + 16
    count = len(pieces)
    dims = (blocks // ranks // CORES, ranks, head_local, latent, count)
    return pl.pallas_call(
        functools.partial(attend_kernel, dims),
        out_shape=pltpu.VMEM((owners, out_rows, LANES), jnp.bfloat16),
        in_specs=[smem_spec] * 3 + [hbm_spec] + [vmem_spec] * count,
        out_specs=vmem_spec,
        scratch_shapes=[
            pltpu.VMEM((blocks, width, block_len), jnp.bfloat16),
            pltpu.VMEM((2, group // QUERY_PARTS, width, head_total), jnp.bfloat16),
            pltpu.VMEM((group // QUERY_PARTS, heads, width), jnp.bfloat16),
            pltpu.VMEM((heads, LANES), jnp.float32),
            pltpu.SemaphoreType.DMA((count + QUERY_PARTS,)),
        ],
        compiler_params=pltpu.CompilerParams(vmem_limit_bytes=24 * MIB),
        name="attend",
    )(code_own, code_other, lengths, in_hbm(q_all), *[in_vmem(one) for one in pieces])


def scatter_tiles(flat, value, first_tile, group, tiles):
    for n in range(value.shape[1] // LANES):
        flat[pl.ds(first_tile + n, group, stride=tiles), :] = value[:, n * LANES : (n + 1) * LANES]


def project_kernel(dims, parts, w_value, w_out, sent, att_buf, flat):
    group, head_local, latent, chunk = dims
    sources = parts.shape[0]
    rows = group * head_local
    pieces = latent // LANES
    tiles = w_out.shape[1] // LANES
    tail = pieces * rows
    lses = []
    for s in range(sources):
        three = parts[s, tail:, :].astype(jnp.float32)
        lses.append(
            three[:head_local]
            + three[head_local : 2 * head_local]
            + three[2 * head_local : 3 * head_local]
        )
    peak = functools.reduce(jnp.maximum, lses)
    shares = [jnp.exp(one - peak) for one in lses]
    inverse = 1.0 / functools.reduce(jnp.add, shares)
    share_all = jnp.concatenate([one * inverse for one in shares], axis=0)
    count = sources * head_local
    pick_request = jnp.where(
        lax.broadcasted_iota(jnp.int32, (rows, LANES), 0) // head_local
        == lax.broadcasted_iota(jnp.int32, (rows, LANES), 1),
        1.0,
        0.0,
    )
    valid = lax.broadcasted_iota(jnp.int32, (count, LANES), 1) < group
    spread = lax.dot_general(
        pick_request,
        jnp.where(valid, share_all, 0.0),
        (((1,), (1,)), ((), ())),
        precision=lax.Precision.HIGHEST,
        preferred_element_type=jnp.float32,
    )
    own_head = (
        lax.broadcasted_iota(jnp.int32, (rows, count), 0) % head_local
        == lax.broadcasted_iota(jnp.int32, (rows, count), 1) % head_local
    )
    pick_source = jnp.where(
        lax.broadcasted_iota(jnp.int32, (count, LANES), 0) // head_local
        == lax.broadcasted_iota(jnp.int32, (count, LANES), 1),
        1.0,
        0.0,
    )
    share = jnp.dot(
        jnp.where(own_head, spread, 0.0),
        pick_source,
        precision=lax.Precision.HIGHEST,
        preferred_element_type=jnp.float32,
    )
    totals = [None] * pieces
    for s in range(sources):
        factor = jnp.broadcast_to(share[:, s : s + 1], (rows, LANES))
        for p in range(pieces):
            term = parts[s, p * rows : (p + 1) * rows, :].astype(jnp.float32) * factor
            totals[p] = term if s == 0 else totals[p] + term
    for p in range(pieces):
        att_buf[p] = totals[p]
    heads = []
    for j in range(head_local):
        attended = jnp.concatenate(
            [att_buf[p, pl.ds(j, group, stride=head_local), :] for p in range(pieces)], axis=1
        ).astype(jnp.bfloat16)
        heads.append(
            jnp.dot(attended, w_value[j], preferred_element_type=jnp.float32).astype(jnp.bfloat16)
        )
    per_head = jnp.concatenate(heads, axis=1)
    for c in range(w_out.shape[1] // chunk):
        value = jnp.dot(
            per_head, w_out[:, c * chunk : (c + 1) * chunk], preferred_element_type=jnp.float32
        )
        scatter_tiles(flat, value, c * chunk // LANES, group, tiles)
    for r in range(group):
        sent[r] = flat[r * tiles : (r + 1) * tiles, :].astype(jnp.bfloat16)


def project(parts, w_value, w_out, group):
    head_local, latent, _ = w_value.shape
    features = w_out.shape[1]
    tiles = features // LANES
    dims = (group, head_local, latent, features // 7)
    return pl.pallas_call(
        functools.partial(project_kernel, dims),
        out_shape=pltpu.VMEM((group, tiles, LANES), jnp.bfloat16),
        in_specs=[vmem_spec] * 3,
        out_specs=vmem_spec,
        scratch_shapes=[
            pltpu.VMEM((latent // LANES, group * head_local, LANES), jnp.float32),
            pltpu.VMEM((group * tiles, LANES), jnp.float32),
        ],
        compiler_params=pltpu.CompilerParams(vmem_limit_bytes=12 * MIB),
        name="project",
    )(in_vmem(parts), w_value, w_out)


def norm_kernel(got, residual, gain, kept, normed):
    total = residual[...]
    for s in range(got.shape[0]):
        total = total + got[s].astype(jnp.float32)
    kept[...] = total
    mean = jnp.sum(total * total) * (1.0 / total.size)
    value = (total * lax.rsqrt(mean + norm_eps) * gain[...]).astype(jnp.bfloat16)
    for s in range(normed.shape[0]):
        normed[s] = value


def norm(got, residual, gain):
    return pl.pallas_call(
        norm_kernel,
        out_shape=(pltpu.VMEM(residual.shape, jnp.float32), pltpu.VMEM(got.shape, got.dtype)),
        in_specs=[vmem_spec] * 3,
        out_specs=(vmem_spec, vmem_spec),
        compiler_params=pltpu.CompilerParams(vmem_limit_bytes=8 * MIB),
        name="norm",
    )(in_vmem(got), in_vmem(residual), in_vmem(gain))


def ffn_kernel(chunk, normed, w_gate, w_up, w_down, sent, flat, wide):
    group, tiles, _ = normed.shape
    for r in range(group):
        flat[r * tiles : (r + 1) * tiles, :] = normed[r].astype(jnp.float32)
    for n in range(tiles):
        wide[:, n * LANES : (n + 1) * LANES] = flat[pl.ds(n, group, stride=tiles), :].astype(
            jnp.bfloat16
        )
    gate = jnp.dot(wide[...], w_gate[...], preferred_element_type=jnp.float32)
    up = jnp.dot(wide[...], w_up[...], preferred_element_type=jnp.float32)
    activated = (gate / (1.0 + jnp.exp(-gate)) * up).astype(jnp.bfloat16)
    for c in range(w_down.shape[1] // chunk):
        value = jnp.dot(
            activated, w_down[:, c * chunk : (c + 1) * chunk], preferred_element_type=jnp.float32
        )
        scatter_tiles(flat, value, c * chunk // LANES, group, tiles)
    for r in range(group):
        sent[r] = flat[r * tiles : (r + 1) * tiles, :].astype(jnp.bfloat16)


def ffn(normed, w_gate, w_up, w_down):
    group, tiles, _ = normed.shape
    features = tiles * LANES
    return pl.pallas_call(
        functools.partial(ffn_kernel, features // 7),
        out_shape=pltpu.VMEM(normed.shape, jnp.bfloat16),
        in_specs=[vmem_spec] * 4,
        out_specs=vmem_spec,
        scratch_shapes=[
            pltpu.VMEM((group * tiles, LANES), jnp.float32),
            pltpu.VMEM((group, features), jnp.bfloat16),
        ],
        compiler_params=pltpu.CompilerParams(vmem_limit_bytes=12 * MIB),
        name="ffn",
    )(in_vmem(normed), w_gate, w_up, w_down)


def body(
    queries,
    cache_pool,
    holder,
    slot_ids,
    lengths,
    residual,
    w_value,
    w_out,
    norm_gain,
    w_gate,
    w_up,
    w_down,
):
    ranks = lax.axis_size("dp")
    tensors = lax.axis_size("tensor")
    column = lax.axis_index("tensor")
    chips = tensors // CORES
    group = residual.shape[0]
    slots = cache_pool.shape[0]
    head_local, latent, _ = w_value.shape
    features = residual.shape[1]
    tiles = features // LANES
    requests = lengths.shape[0]
    swap = [(i, i ^ 1) for i in range(tensors)]
    same_core = [[c + CORES * k for k in range(chips)] for c in range(CORES)]
    from_next = [((i + 1) % ranks, i) for i in range(ranks)]
    from_prev = [((i - 1) % ranks, i) for i in range(ranks)]

    def swapped(value):
        return lax.ppermute(value, "tensor", swap)

    q_all = lax.all_gather(queries, "tensor", axis=0, tiled=True)
    low, high = split_pool(cache_pool)
    next_low = lax.ppermute(low, "dp", from_next)
    prev_high = lax.ppermute(high, "dp", from_prev)
    next_high = lax.ppermute(high, "dp", from_next)
    prev_low = lax.ppermute(low, "dp", from_prev)
    far_low = lax.ppermute(next_low, "dp", from_next)
    far_high = lax.ppermute(prev_high, "dp", from_prev)
    mine = [low, high, next_low, next_high, far_low, far_high, prev_low, prev_high]
    code = (holder * slots + slot_ids).reshape(1, requests)
    code_other = swapped(code)
    own_residual = (
        lax.dynamic_index_in_dim(residual, column, 0, keepdims=False)
        .astype(jnp.float32)
        .reshape(tiles, LANES)
    )
    gain = norm_gain.reshape(tiles, LANES)
    w_value, w_out, w_gate, w_up, w_down = [
        in_vmem(one) for one in (w_value, w_out, w_gate, w_up, w_down)
    ]
    others = [swapped(one) for one in mine]

    q_all, own_residual, gain = lax.optimization_barrier((q_all, own_residual, gain))
    partial = attend(
        code, code_other, lengths.reshape(1, requests), q_all, mine + others, ranks, latent, head_local
    )
    parts = lax.all_to_all(
        partial, "tensor", split_axis=0, concat_axis=0, tiled=True, axis_index_groups=same_core
    )

    def exchange(value):
        return lax.all_to_all(value, "tensor", split_axis=0, concat_axis=0, tiled=True)

    residual_sum, normed = norm(exchange(project(parts, w_value, w_out, group)), own_residual, gain)
    down = exchange(ffn(exchange(normed), w_gate, w_up, w_down))
    return (residual_sum + jnp.sum(down.astype(jnp.float32), axis=0)).reshape(1, features)


def solution(mesh):
    in_specs = (
        P(("dp", "tensor"), None, None),
        P(("dp", "tensor"), None, None),
        P(None, "tensor"),
        P(None, "tensor"),
        P(),
        P("dp", None),
        P("tensor", None, None),
        P("tensor", None),
        P(),
        P(None, "tensor"),
        P(None, "tensor"),
        P("tensor", None),
    )
    out_specs = P(("dp", "tensor"), None)
    return jax.shard_map(body, mesh=mesh, in_specs=in_specs, out_specs=out_specs, check_vma=False)
```

```python
import functools

import jax
import jax.numpy as jnp
from jax import lax
from jax.experimental import pallas as pl
from jax.experimental.pallas import tpu as pltpu
from jax.sharding import PartitionSpec as P

score_scale = 192.0 ** (-0.5)
norm_eps = 1e-06
far_below = -1e30
CORES = 2
LANES = 128
HEAD_LOCAL = 4
QUERY_PARTS = 4
QUERY_ROWS = (576,)
MIB = 1024 * 1024
hbm_spec = pl.BlockSpec(memory_space=pl.ANY)
vmem_spec = pl.BlockSpec(memory_space=pltpu.VMEM)
smem_spec = pl.BlockSpec(memory_space=pltpu.SMEM)


def in_vmem(value):
    return pltpu.with_memory_space_constraint(value, pltpu.VMEM)


def in_hbm(value):
    return pltpu.with_memory_space_constraint(value, pltpu.HBM)


def split_kernel(pool, *refs):
    low, high, sems = refs[-3:]
    half = low.shape[0]
    copies = [
        pltpu.make_async_copy(pool.at[pl.ds(i * half, half)], one, sems.at[i])
        for i, one in enumerate((low, high))
    ]
    for one in copies:
        one.start()
    for one in copies:
        one.wait()


def split(pool, *after):
    half = (pool.shape[0] // 2,) + pool.shape[1:]
    return pl.pallas_call(
        split_kernel,
        out_shape=(pltpu.VMEM(half, pool.dtype), pltpu.VMEM(half, pool.dtype)),
        in_specs=[hbm_spec] * (1 + len(after)),
        out_specs=(vmem_spec, vmem_spec),
        scratch_shapes=[pltpu.SemaphoreType.DMA((2,))],
        compiler_params=pltpu.CompilerParams(vmem_limit_bytes=12 * MIB),
        name="split",
    )(in_hbm(pool), *after)


def turn_kernel(own, other, *outs):
    width, head_total = own.shape
    heads = head_total // CORES
    head_local, tail = HEAD_LOCAL, width // LANES * LANES
    core = lax.axis_index("tensor") % CORES
    row = lax.broadcasted_iota(jnp.int32, (heads, head_total), 0)
    wanted = (row // head_local) * (CORES * head_local) + core * head_local + row % head_local
    hit = lax.broadcasted_iota(jnp.int32, (heads, head_total), 1) == wanted
    select = jnp.where(hit, 1.0, 0.0).astype(jnp.bfloat16)
    turned = [
        lax.dot_general(select, one[...], (((1,), (1,)), ((), ())), preferred_element_type=jnp.float32)
        for one in (own, other)
    ]
    pair = [
        jnp.where(core == 0, turned[0], turned[1]).astype(jnp.bfloat16),
        jnp.where(core == 0, turned[1], turned[0]).astype(jnp.bfloat16),
    ]
    rows = [
        pair[i][:, p * LANES : (p + 1) * LANES] for p in range(tail // LANES) for i in range(CORES)
    ]
    rows = jnp.concatenate(
        rows + [jnp.concatenate([one[:, tail:] for one in pair], axis=1)], axis=0
    )
    at = 0
    for out in outs:
        out[0] = rows[at : at + out.shape[1], :]
        at += out.shape[1]


def turn(own, other):
    return pl.pallas_call(
        turn_kernel,
        out_shape=tuple(
            jax.ShapeDtypeStruct((1, rows, own.shape[1]), own.dtype) for rows in QUERY_ROWS
        ),
        in_specs=[vmem_spec] * 2,
        out_specs=(vmem_spec,) * len(QUERY_ROWS),
        compiler_params=pltpu.CompilerParams(vmem_limit_bytes=4 * MIB),
        name="turn",
    )(own, other)


def attend_kernel(dims, code_own, code_other, lengths, *refs):
    slots, ranks, head_local, latent, count = dims
    q_refs = refs[: len(QUERY_ROWS)]
    pieces = refs[len(QUERY_ROWS) : len(QUERY_ROWS) + count]
    out_ref, kbuf, qbuf, lse_buf, sems = refs[len(QUERY_ROWS) + count :]
    pairs, width, _ = qbuf.shape
    group = CORES * pairs
    heads = lse_buf.shape[0]
    block_len = kbuf.shape[2]
    owners = heads // head_local
    my_rank = lax.axis_index("dp")
    column = lax.axis_index("tensor")
    core = column % CORES
    first = my_rank * group
    portion = pairs // QUERY_PARTS

    def q_copies(step):
        made, at = [], 0
        for i, one in enumerate(q_refs):
            rows = one.shape[1]
            made.append(
                pltpu.make_async_copy(
                    one.at[pl.ds(step * portion, portion)],
                    qbuf.at[pl.ds(step * portion, portion), pl.ds(at, rows)],
                    sems.at[count + step * len(q_refs) + i],
                )
            )
            at += rows
        return made

    copies, at = [], 0
    for i, one in enumerate(pieces):
        copies.append(pltpu.make_async_copy(one, kbuf.at[pl.ds(at, one.shape[0])], sems.at[i]))
        at += one.shape[0]
    for one in q_copies(0) + copies:
        one.start()
    for step in range(1, QUERY_PARTS):
        for one in q_copies(step):
            one.start()
    token = lax.broadcasted_iota(jnp.int32, (1, 2 * block_len), 1)
    partner = column + 1 - 2 * core
    position = jnp.where(
        token < block_len, token + column * block_len, token - block_len + partner * block_len
    )
    lane = lax.broadcasted_iota(jnp.int32, (heads, LANES), 1)
    lse_buf[...] = jnp.zeros_like(lse_buf)
    for one in copies:
        one.wait()

    def place(codes, r):
        code = codes[0, first + r]
        return ((code // slots - my_rank + ranks) % ranks) * slots + code % slots

    unroll = CORES * portion

    def several(step):
        rs = [step * unroll + i for i in range(unroll)]
        keys = [
            jnp.concatenate(
                [kbuf[place(code_own, r)], kbuf[ranks * slots + place(code_other, r)]], axis=1
            )
            for r in rs
        ]
        asked = []
        for i in range(unroll):
            at = step * portion + i // CORES
            side = i % CORES
            rotary = qbuf[at, latent:, :]
            mine = (lane < LANES // CORES) if side == 0 else (lane >= LANES // CORES)
            rows = [
                qbuf[at, (p * CORES + side) * heads : (p * CORES + side + 1) * heads, :]
                for p in range(latent // LANES)
            ]
            asked.append(
                jnp.concatenate(rows + [jnp.where(mine, rotary, jnp.zeros_like(rotary))], axis=1)
            )
        scores = [
            jnp.dot(
                q,
                jnp.concatenate([key, key[latent:]], axis=0),
                preferred_element_type=jnp.float32,
            )
            * score_scale
            for q, key in zip(asked, keys)
        ]
        weights, scales, lses = [], [], []
        for r, score in zip(rs, scores):
            live = position < lengths[0, first + r]
            masked = jnp.where(live, score, far_below)
            top = jnp.max(masked, axis=1, keepdims=True)
            weight = jnp.where(live, jnp.exp(masked - top), 0.0)
            total = jnp.sum(weight, axis=1, keepdims=True)
            some = total > 0.0
            safe = jnp.where(some, total, 1.0)
            weights.append(weight.astype(jnp.bfloat16))
            scales.append(jnp.where(some, 1.0 / safe, 0.0))
            lses.append(jnp.where(some, top + jnp.log(safe), far_below))
        mixed = [
            lax.dot_general(
                weight, key[:latent], (((1,), (1,)), ((), ())), preferred_element_type=jnp.float32
            )
            * scale
            for weight, key, scale in zip(weights, keys, scales)
        ]
        lse_all = lse_buf[...]
        for r, lse in zip(rs, lses):
            lse_all = jnp.where(lane == r, lse, lse_all)
        lse_buf[...] = lse_all
        rows_count = unroll * head_local
        for k in range(owners):
            both = jnp.concatenate(
                [one[k * head_local : (k + 1) * head_local] for one in mixed], axis=0
            ).astype(jnp.bfloat16)
            for p in range(latent // LANES):
                rows_at = pl.multiple_of(p * group * head_local + step * rows_count, rows_count)
                out_ref[k, pl.ds(rows_at, rows_count), :] = both[:, p * LANES : (p + 1) * LANES]

    def one_step(step, carry):
        for one in q_copies(step):
            one.wait()
        several(step)
        return carry

    lax.fori_loop(0, QUERY_PARTS, one_step, 0)
    lse_all = lse_buf[...]
    high = lse_all.astype(jnp.bfloat16).astype(jnp.float32)
    mid = (lse_all - high).astype(jnp.bfloat16).astype(jnp.float32)
    low = lse_all - high - mid
    tail = latent // LANES * group * head_local
    for k in range(owners):
        own = slice(k * head_local, (k + 1) * head_local)
        out_ref[k, tail:, :] = jnp.concatenate(
            [high[own], mid[own], low[own], jnp.zeros_like(low[own])], axis=0
        ).astype(jnp.bfloat16)


def attend(code_own, code_other, lengths, q_all, pieces, ranks, latent, head_local):
    pairs, _, head_total = q_all[0].shape
    width, block_len = pieces[0].shape[1:]
    heads = head_total // CORES
    blocks = sum(one.shape[0] for one in pieces)
    owners = heads // head_local
    out_rows = latent // LANES * pairs * CORES * head_local + 16
    count = len(pieces)
    dims = (blocks // ranks // CORES, ranks, head_local, latent, count)
    return pl.pallas_call(
        functools.partial(attend_kernel, dims),
        out_shape=pltpu.VMEM((owners, out_rows, LANES), jnp.bfloat16),
        in_specs=[smem_spec] * 3 + [hbm_spec] * (len(q_all) + count),
        out_specs=vmem_spec,
        scratch_shapes=[
            pltpu.VMEM((blocks, width, block_len), jnp.bfloat16),
            pltpu.VMEM((pairs, width, head_total), jnp.bfloat16),
            pltpu.VMEM((heads, LANES), jnp.float32),
            pltpu.SemaphoreType.DMA((count + QUERY_PARTS * len(q_all),)),
        ],
        compiler_params=pltpu.CompilerParams(vmem_limit_bytes=20 * MIB),
        name="attend",
    )(code_own, code_other, lengths, *[in_hbm(one) for one in q_all], *pieces)


def scatter_tiles(flat, value, first_tile, group, tiles):
    for n in range(value.shape[1] // LANES):
        flat[pl.ds(first_tile + n, group, stride=tiles), :] = value[:, n * LANES : (n + 1) * LANES]


def project_kernel(dims, parts, w_value, w_out, sent, att_buf, flat):
    group, head_local, latent, chunk = dims
    sources = parts.shape[0]
    rows = group * head_local
    pieces = latent // LANES
    tiles = w_out.shape[1] // LANES
    tail = pieces * rows
    lses = []
    for s in range(sources):
        three = parts[s, tail:, :].astype(jnp.float32)
        lses.append(
            three[:head_local]
            + three[head_local : 2 * head_local]
            + three[2 * head_local : 3 * head_local]
        )
    peak = functools.reduce(jnp.maximum, lses)
    shares = [jnp.exp(one - peak) for one in lses]
    inverse = 1.0 / functools.reduce(jnp.add, shares)
    share_all = jnp.concatenate([one * inverse for one in shares], axis=0)
    count = sources * head_local
    pick_request = jnp.where(
        lax.broadcasted_iota(jnp.int32, (rows, LANES), 0) // head_local
        == lax.broadcasted_iota(jnp.int32, (rows, LANES), 1),
        1.0,
        0.0,
    )
    valid = lax.broadcasted_iota(jnp.int32, (count, LANES), 1) < group
    spread = lax.dot_general(
        pick_request,
        jnp.where(valid, share_all, 0.0),
        (((1,), (1,)), ((), ())),
        precision=lax.Precision.HIGHEST,
        preferred_element_type=jnp.float32,
    )
    own_head = (
        lax.broadcasted_iota(jnp.int32, (rows, count), 0) % head_local
        == lax.broadcasted_iota(jnp.int32, (rows, count), 1) % head_local
    )
    pick_source = jnp.where(
        lax.broadcasted_iota(jnp.int32, (count, LANES), 0) // head_local
        == lax.broadcasted_iota(jnp.int32, (count, LANES), 1),
        1.0,
        0.0,
    )
    share = jnp.dot(
        jnp.where(own_head, spread, 0.0),
        pick_source,
        precision=lax.Precision.HIGHEST,
        preferred_element_type=jnp.float32,
    )
    totals = [None] * pieces
    for s in range(sources):
        factor = jnp.broadcast_to(share[:, s : s + 1], (rows, LANES))
        for p in range(pieces):
            term = parts[s, p * rows : (p + 1) * rows, :].astype(jnp.float32) * factor
            totals[p] = term if s == 0 else totals[p] + term
    for p in range(pieces):
        att_buf[p] = totals[p]
    heads = []
    for j in range(head_local):
        attended = jnp.concatenate(
            [att_buf[p, pl.ds(j, group, stride=head_local), :] for p in range(pieces)], axis=1
        ).astype(jnp.bfloat16)
        heads.append(
            jnp.dot(attended, w_value[j], preferred_element_type=jnp.float32).astype(jnp.bfloat16)
        )
    per_head = jnp.concatenate(heads, axis=1)
    for c in range(w_out.shape[1] // chunk):
        value = jnp.dot(
            per_head, w_out[:, c * chunk : (c + 1) * chunk], preferred_element_type=jnp.float32
        )
        scatter_tiles(flat, value, c * chunk // LANES, group, tiles)
    for r in range(group):
        sent[r] = flat[r * tiles : (r + 1) * tiles, :].astype(jnp.bfloat16)


def project(parts, w_value, w_out, group):
    head_local, latent, _ = w_value.shape
    features = w_out.shape[1]
    tiles = features // LANES
    dims = (group, head_local, latent, features // 7)
    return pl.pallas_call(
        functools.partial(project_kernel, dims),
        out_shape=pltpu.VMEM((group, tiles, LANES), jnp.bfloat16),
        in_specs=[vmem_spec] * 3,
        out_specs=vmem_spec,
        scratch_shapes=[
            pltpu.VMEM((latent // LANES, group * head_local, LANES), jnp.float32),
            pltpu.VMEM((group * tiles, LANES), jnp.float32),
        ],
        compiler_params=pltpu.CompilerParams(vmem_limit_bytes=12 * MIB),
        name="project",
    )(in_vmem(parts), w_value, w_out)


def norm_kernel(got, residual, gain, kept, normed):
    total = residual[...]
    for s in range(got.shape[0]):
        total = total + got[s].astype(jnp.float32)
    kept[...] = total
    mean = jnp.sum(total * total) * (1.0 / total.size)
    value = (total * lax.rsqrt(mean + norm_eps) * gain[...]).astype(jnp.bfloat16)
    for s in range(normed.shape[0]):
        normed[s] = value


def norm(got, residual, gain):
    return pl.pallas_call(
        norm_kernel,
        out_shape=(pltpu.VMEM(residual.shape, jnp.float32), pltpu.VMEM(got.shape, got.dtype)),
        in_specs=[vmem_spec] * 3,
        out_specs=(vmem_spec, vmem_spec),
        compiler_params=pltpu.CompilerParams(vmem_limit_bytes=8 * MIB),
        name="norm",
    )(in_vmem(got), in_vmem(residual), in_vmem(gain))


def ffn_kernel(chunk, normed, w_gate, w_up, w_down, sent, flat, wide):
    group, tiles, _ = normed.shape
    for r in range(group):
        flat[r * tiles : (r + 1) * tiles, :] = normed[r].astype(jnp.float32)
    for n in range(tiles):
        wide[:, n * LANES : (n + 1) * LANES] = flat[pl.ds(n, group, stride=tiles), :].astype(
            jnp.bfloat16
        )
    gate = jnp.dot(wide[...], w_gate[...], preferred_element_type=jnp.float32)
    up = jnp.dot(wide[...], w_up[...], preferred_element_type=jnp.float32)
    activated = (gate / (1.0 + jnp.exp(-gate)) * up).astype(jnp.bfloat16)
    for c in range(w_down.shape[1] // chunk):
        value = jnp.dot(
            activated, w_down[:, c * chunk : (c + 1) * chunk], preferred_element_type=jnp.float32
        )
        scatter_tiles(flat, value, c * chunk // LANES, group, tiles)
    for r in range(group):
        sent[r] = flat[r * tiles : (r + 1) * tiles, :].astype(jnp.bfloat16)


def ffn(normed, w_gate, w_up, w_down):
    group, tiles, _ = normed.shape
    features = tiles * LANES
    return pl.pallas_call(
        functools.partial(ffn_kernel, features // 7),
        out_shape=pltpu.VMEM(normed.shape, jnp.bfloat16),
        in_specs=[vmem_spec] * 4,
        out_specs=vmem_spec,
        scratch_shapes=[
            pltpu.VMEM((group * tiles, LANES), jnp.float32),
            pltpu.VMEM((group, features), jnp.bfloat16),
        ],
        compiler_params=pltpu.CompilerParams(vmem_limit_bytes=12 * MIB),
        name="ffn",
    )(in_vmem(normed), w_gate, w_up, w_down)


def body(
    queries,
    cache_pool,
    holder,
    slot_ids,
    lengths,
    residual,
    w_value,
    w_out,
    norm_gain,
    w_gate,
    w_up,
    w_down,
):
    ranks = lax.axis_size("dp")
    tensors = lax.axis_size("tensor")
    column = lax.axis_index("tensor")
    chips = tensors // CORES
    group = residual.shape[0]
    slots = cache_pool.shape[0]
    head_local, latent, _ = w_value.shape
    features = residual.shape[1]
    tiles = features // LANES
    requests = lengths.shape[0]
    swap = [(i, i ^ 1) for i in range(tensors)]
    same_core = [[c + CORES * k for k in range(chips)] for c in range(CORES)]
    from_next = [((i + 1) % ranks, i) for i in range(ranks)]
    from_prev = [((i - 1) % ranks, i) for i in range(ranks)]

    def swapped(value):
        return lax.ppermute(value, "tensor", swap)

    own_queries = queries[0]
    (q_pair,) = turn(own_queries, swapped(own_queries))
    q_gather = lax.all_gather(q_pair, "tensor", axis=0, tiled=True, axis_index_groups=same_core)
    low, high = split(cache_pool)
    next_low = lax.ppermute(low, "dp", from_next)
    prev_high = lax.ppermute(high, "dp", from_prev)
    low, high = split(cache_pool, q_pair)
    next_high = lax.ppermute(high, "dp", from_next)
    prev_low = lax.ppermute(low, "dp", from_prev)
    own_residual = (
        lax.dynamic_index_in_dim(residual, column, 0, keepdims=False)
        .astype(jnp.float32)
        .reshape(tiles, LANES)
    )
    far_low = lax.ppermute(next_low, "dp", from_next)
    far_high = lax.ppermute(prev_high, "dp", from_prev)
    mine = [next_low, next_high, far_low, far_high, prev_low, prev_high]
    moved = [in_vmem(swapped(one)) for one in mine]
    mine = [in_vmem(one) for one in mine]
    pieces = [in_hbm(cache_pool)] + mine + [in_hbm(swapped(cache_pool))] + moved
    code = (holder * slots + slot_ids).reshape(1, requests)
    code_other = swapped(code)
    gain = norm_gain.reshape(tiles, LANES)
    q_gather, own_residual, gain = lax.optimization_barrier((q_gather, own_residual, gain))
    w_value, w_out, w_gate, w_up, w_down = [
        in_vmem(one) for one in (w_value, w_out, w_gate, w_up, w_down)
    ]
    partial = attend(
        code,
        code_other,
        lengths.reshape(1, requests),
        (q_gather,),
        pieces,
        ranks,
        latent,
        head_local,
    )
    parts = lax.all_to_all(
        partial, "tensor", split_axis=0, concat_axis=0, tiled=True, axis_index_groups=same_core
    )

    def exchange(value):
        return lax.all_to_all(value, "tensor", split_axis=0, concat_axis=0, tiled=True)

    residual_sum, normed = norm(exchange(project(parts, w_value, w_out, group)), own_residual, gain)
    down = exchange(ffn(exchange(normed), w_gate, w_up, w_down))
    return (residual_sum + jnp.sum(down.astype(jnp.float32), axis=0)).reshape(1, features)


def solution(mesh):
    in_specs = (
        P(("dp", "tensor"), None, None),
        P(("dp", "tensor"), None, None),
        P(None, "tensor"),
        P(None, "tensor"),
        P(),
        P("dp", None),
        P("tensor", None, None),
        P("tensor", None),
        P(),
        P(None, "tensor"),
        P(None, "tensor"),
        P("tensor", None),
    )
    out_specs = P(("dp", "tensor"), None)
    return jax.shard_map(body, mesh=mesh, in_specs=in_specs, out_specs=out_specs, check_vma=False)
```

```python
import functools

import jax
import jax.numpy as jnp
from jax import lax
from jax.experimental import pallas as pl
from jax.experimental.pallas import tpu as pltpu
from jax.sharding import PartitionSpec as P

score_scale = 192.0 ** (-0.5)
norm_eps = 1e-06
far_below = -1e30
CORES = 2
LANES = 128
HEAD_LOCAL = 4
SIDE = 4
MIB = 1024 * 1024
hbm_spec = pl.BlockSpec(memory_space=pl.ANY)
vmem_spec = pl.BlockSpec(memory_space=pltpu.VMEM)
smem_spec = pl.BlockSpec(memory_space=pltpu.SMEM)


def in_vmem(value):
    return pltpu.with_memory_space_constraint(value, pltpu.VMEM)


def in_hbm(value):
    return pltpu.with_memory_space_constraint(value, pltpu.HBM)


def split_kernel(pool, *refs):
    low, high, sems = refs[-3:]
    half = low.shape[0]
    copies = [
        pltpu.make_async_copy(pool.at[pl.ds(i * half, half)], one, sems.at[i])
        for i, one in enumerate((low, high))
    ]
    for one in copies:
        one.start()
    for one in copies:
        one.wait()


def split(pool, *after):
    half = (pool.shape[0] // 2,) + pool.shape[1:]
    return pl.pallas_call(
        split_kernel,
        out_shape=(pltpu.VMEM(half, pool.dtype), pltpu.VMEM(half, pool.dtype)),
        in_specs=[hbm_spec] * (1 + len(after)),
        out_specs=(vmem_spec, vmem_spec),
        scratch_shapes=[pltpu.SemaphoreType.DMA((2,))],
        compiler_params=pltpu.CompilerParams(vmem_limit_bytes=12 * MIB),
        name="split",
    )(in_hbm(pool), *after)


def turn_kernel(own, other, out):
    width, head_total = own.shape
    heads = head_total // CORES
    head_local, tail = HEAD_LOCAL, width // LANES * LANES
    core = lax.axis_index("tensor") % CORES
    row = lax.broadcasted_iota(jnp.int32, (heads, head_total), 0)
    wanted = (row // head_local) * (CORES * head_local) + core * head_local + row % head_local
    hit = lax.broadcasted_iota(jnp.int32, (heads, head_total), 1) == wanted
    select = jnp.where(hit, 1.0, 0.0).astype(jnp.bfloat16)
    turned = [
        lax.dot_general(select, one[...], (((1,), (1,)), ((), ())), preferred_element_type=jnp.float32)
        for one in (own, other)
    ]
    pair = [
        jnp.where(core == 0, turned[0], turned[1]).astype(jnp.bfloat16),
        jnp.where(core == 0, turned[1], turned[0]).astype(jnp.bfloat16),
    ]
    rows = [
        pair[i][:, p * LANES : (p + 1) * LANES] for p in range(tail // LANES) for i in range(CORES)
    ]
    out[0] = jnp.concatenate(
        rows + [jnp.concatenate([one[:, tail:] for one in pair], axis=1)], axis=0
    )


def turn(own, other):
    return pl.pallas_call(
        turn_kernel,
        out_shape=jax.ShapeDtypeStruct((1,) + own.shape, own.dtype),
        in_specs=[vmem_spec] * 2,
        out_specs=vmem_spec,
        compiler_params=pltpu.CompilerParams(vmem_limit_bytes=4 * MIB),
        name="turn",
    )(own, other)


def join_kernel(*refs):
    count = len(refs) - 2
    out, sems = refs[count:]
    copies = [
        pltpu.make_async_copy(one, out.at[pl.ds(i, 1)], sems.at[i])
        for i, one in enumerate(refs[:count])
    ]
    for one in copies:
        one.start()
    for one in copies:
        one.wait()


def join(pieces):
    count = len(pieces)
    return pl.pallas_call(
        join_kernel,
        out_shape=jax.ShapeDtypeStruct((count,) + pieces[0].shape[1:], pieces[0].dtype),
        in_specs=[hbm_spec] * count,
        out_specs=hbm_spec,
        scratch_shapes=[pltpu.SemaphoreType.DMA((count,))],
        compiler_params=pltpu.CompilerParams(vmem_limit_bytes=4 * MIB),
        name="join",
    )(*pieces)


def by_core(core, chip):
    x, y = chip % SIDE, chip // SIDE
    return jnp.where(core == 0, x, y), jnp.where(core == 0, y, x)


def shifts(tensors, first, distance):
    pairs = []
    for i in range(tensors):
        core, chip = i % CORES, i // CORES
        x, y = chip % SIDE, chip // SIDE
        if (core == 0) == first:
            x = (x + distance) % SIDE
        else:
            y = (y + distance) % SIDE
        pairs.append((i, (y * SIDE + x) * CORES + core))
    return pairs


def attend_kernel(dims, code_own, code_other, lengths, *refs):
    slots, ranks, head_local, latent, count = dims
    q_refs, pieces = refs[:SIDE], refs[SIDE : SIDE + count]
    outs = refs[SIDE + count : 2 * SIDE + count]
    kbuf, qbuf, obuf, lse_buf, sems = refs[2 * SIDE + count :]
    group = CORES * SIDE * SIDE
    heads = lse_buf.shape[0]
    block_len = kbuf.shape[2]
    owners = heads // head_local
    my_rank = lax.axis_index("dp")
    column = lax.axis_index("tensor")
    core = column % CORES
    own_first, own_second = by_core(core, column // CORES)
    first = my_rank * group
    q_copies = [
        pltpu.make_async_copy(one, qbuf.at[pl.ds(e * SIDE, SIDE)], sems.at[count + e])
        for e, one in enumerate(q_refs)
    ]
    copies, at = [], 0
    for i, one in enumerate(pieces):
        copies.append(pltpu.make_async_copy(one, kbuf.at[pl.ds(at, one.shape[0])], sems.at[i]))
        at += one.shape[0]
    for one in q_copies + copies:
        one.start()
    token = lax.broadcasted_iota(jnp.int32, (1, 2 * block_len), 1)
    partner = column + 1 - 2 * core
    position = jnp.where(
        token < block_len, token + column * block_len, token - block_len + partner * block_len
    )
    lane = lax.broadcasted_iota(jnp.int32, (heads, LANES), 1)
    lse_buf[...] = jnp.zeros_like(lse_buf)
    spots = []
    for k in range(owners):
        k_first, k_second = by_core(core, k)
        spots.append(
            (k_first - own_first + SIDE) % SIDE * SIDE + (k_second - own_second + SIDE) % SIDE
        )
    for one in q_copies + copies:
        one.wait()

    def place(codes, r):
        code = codes[0, first + r]
        return ((code // slots - my_rank + ranks) % ranks) * slots + code % slots

    unroll = CORES * SIDE

    def several(e, carry):
        second = (own_second - e + SIDE) % SIDE
        rs, asked = [], []
        for i in range(SIDE):
            chip = jnp.where(core == 0, second * SIDE + i, i * SIDE + second)
            at = e * SIDE + (own_first - i + SIDE) % SIDE
            for side in range(CORES):
                rs.append(chip * CORES + side)
                rotary = qbuf[at, latent:, :]
                mine = (lane < LANES // CORES) if side == 0 else (lane >= LANES // CORES)
                rows = [
                    qbuf[at, (p * CORES + side) * heads : (p * CORES + side + 1) * heads, :]
                    for p in range(latent // LANES)
                ]
                asked.append(
                    jnp.concatenate(
                        rows + [jnp.where(mine, rotary, jnp.zeros_like(rotary))], axis=1
                    )
                )
        keys = [
            jnp.concatenate(
                [kbuf[place(code_own, r)], kbuf[ranks * slots + place(code_other, r)]], axis=1
            )
            for r in rs
        ]
        scores = [
            jnp.dot(
                q,
                jnp.concatenate([key, key[latent:]], axis=0),
                preferred_element_type=jnp.float32,
            )
            * score_scale
            for q, key in zip(asked, keys)
        ]
        weights, scales, lses = [], [], []
        for r, score in zip(rs, scores):
            live = position < lengths[0, first + r]
            masked = jnp.where(live, score, far_below)
            top = jnp.max(masked, axis=1, keepdims=True)
            weight = jnp.where(live, jnp.exp(masked - top), 0.0)
            total = jnp.sum(weight, axis=1, keepdims=True)
            some = total > 0.0
            safe = jnp.where(some, total, 1.0)
            weights.append(weight.astype(jnp.bfloat16))
            scales.append(jnp.where(some, 1.0 / safe, 0.0))
            lses.append(jnp.where(some, top + jnp.log(safe), far_below))
        mixed = [
            lax.dot_general(
                weight, key[:latent], (((1,), (1,)), ((), ())), preferred_element_type=jnp.float32
            )
            * scale
            for weight, key, scale in zip(weights, keys, scales)
        ]
        lse_all = lse_buf[...]
        for i, lse in enumerate(lses):
            lse_all = jnp.where(lane == second * unroll + i, lse, lse_all)
        lse_buf[...] = lse_all
        rows_count = unroll * head_local
        for k in range(owners):
            both = jnp.concatenate(
                [one[k * head_local : (k + 1) * head_local] for one in mixed], axis=0
            ).astype(jnp.bfloat16)
            for p in range(latent // LANES):
                rows_at = pl.multiple_of(p * group * head_local + second * rows_count, rows_count)
                obuf[spots[k], pl.ds(rows_at, rows_count), :] = both[:, p * LANES : (p + 1) * LANES]
        return carry

    lax.fori_loop(0, SIDE, several, 0)
    tail = latent // LANES * group * head_local
    parts = lse_parts(lse_buf[...])
    for k in range(owners):
        own = slice(k * head_local, (k + 1) * head_local)
        obuf[spots[k], tail:, :] = jnp.concatenate(
            [one[own] for one in parts] + [jnp.zeros_like(parts[0][own])], axis=0
        ).astype(jnp.bfloat16)
    copies = [
        pltpu.make_async_copy(obuf.at[pl.ds(d * SIDE, SIDE)], outs[d], sems.at[d])
        for d in range(SIDE)
    ]
    for one in copies:
        one.start()
    for one in copies:
        one.wait()


def lse_parts(value):
    high = value.astype(jnp.bfloat16).astype(jnp.float32)
    mid = (value - high).astype(jnp.bfloat16).astype(jnp.float32)
    return [high, mid, value - high - mid]


def attend(code_own, code_other, lengths, q_all, pieces, ranks, latent, head_local):
    per, _, head_total = q_all[0].shape
    width, block_len = pieces[0].shape[1:]
    heads = head_total // CORES
    blocks = sum(one.shape[0] for one in pieces)
    chips = SIDE * SIDE
    out_rows = latent // LANES * chips * CORES * head_local + 16
    count = len(pieces)
    dims = (blocks // ranks // CORES, ranks, head_local, latent, count)
    return pl.pallas_call(
        functools.partial(attend_kernel, dims),
        out_shape=(pltpu.VMEM((SIDE, out_rows, LANES), jnp.bfloat16),) * SIDE,
        in_specs=[smem_spec] * 3 + [hbm_spec] * (SIDE + count),
        out_specs=(vmem_spec,) * SIDE,
        scratch_shapes=[
            pltpu.VMEM((blocks, width, block_len), jnp.bfloat16),
            pltpu.VMEM((chips, width, head_total), jnp.bfloat16),
            pltpu.VMEM((chips, out_rows, LANES), jnp.bfloat16),
            pltpu.VMEM((heads, LANES), jnp.float32),
            pltpu.SemaphoreType.DMA((count + SIDE,)),
        ],
        compiler_params=pltpu.CompilerParams(vmem_limit_bytes=22 * MIB),
        name="attend",
    )(code_own, code_other, lengths, *[in_hbm(one) for one in q_all], *pieces)


def combine_shares(lses, sets, rows, group, head_local):
    merged, scaled = [], [None] * len(lses)
    for one_set in sets:
        peak = functools.reduce(jnp.maximum, [lses[s] for s in one_set])
        shares = [jnp.exp(lses[s] - peak) for s in one_set]
        total = functools.reduce(jnp.add, shares)
        merged.append(peak + jnp.log(total))
        inverse = 1.0 / total
        for s, share in zip(one_set, shares):
            scaled[s] = share * inverse
    share_all = jnp.concatenate(scaled, axis=0)
    count = len(lses) * head_local
    pick_request = jnp.where(
        lax.broadcasted_iota(jnp.int32, (rows, LANES), 0) // head_local
        == lax.broadcasted_iota(jnp.int32, (rows, LANES), 1),
        1.0,
        0.0,
    )
    valid = lax.broadcasted_iota(jnp.int32, (count, LANES), 1) < group
    spread = lax.dot_general(
        pick_request,
        jnp.where(valid, share_all, 0.0),
        (((1,), (1,)), ((), ())),
        precision=lax.Precision.HIGHEST,
        preferred_element_type=jnp.float32,
    )
    own_head = (
        lax.broadcasted_iota(jnp.int32, (rows, count), 0) % head_local
        == lax.broadcasted_iota(jnp.int32, (rows, count), 1) % head_local
    )
    pick_source = jnp.where(
        lax.broadcasted_iota(jnp.int32, (count, LANES), 0) // head_local
        == lax.broadcasted_iota(jnp.int32, (count, LANES), 1),
        1.0,
        0.0,
    )
    share = jnp.dot(
        jnp.where(own_head, spread, 0.0),
        pick_source,
        precision=lax.Precision.HIGHEST,
        preferred_element_type=jnp.float32,
    )
    return share, merged


def read_lse(tile, head_local):
    three = tile.astype(jnp.float32)
    return functools.reduce(
        jnp.add, [three[i * head_local : (i + 1) * head_local] for i in range(3)]
    )


def merge_kernel(dims, *refs):
    group, head_local, latent = dims
    ins, outs = refs[:SIDE], refs[SIDE:]
    rows = group * head_local
    pieces = latent // LANES
    tail = pieces * rows
    lses = [read_lse(one[e, tail:, :], head_local) for e in range(SIDE) for one in ins]
    sets = [[e * SIDE + s for s in range(SIDE)] for e in range(SIDE)]
    share, merged = combine_shares(lses, sets, rows, group, head_local)
    for e in range(SIDE):
        totals = [None] * pieces
        for s in range(SIDE):
            at = e * SIDE + s
            factor = jnp.broadcast_to(share[:, at : at + 1], (rows, LANES))
            for p in range(pieces):
                term = ins[s][e, p * rows : (p + 1) * rows, :].astype(jnp.float32) * factor
                totals[p] = term if s == 0 else totals[p] + term
        for p in range(pieces):
            outs[e][p * rows : (p + 1) * rows, :] = totals[p].astype(jnp.bfloat16)
        parts = lse_parts(merged[e])
        outs[e][tail:, :] = jnp.concatenate(parts + [jnp.zeros_like(parts[0])], axis=0).astype(
            jnp.bfloat16
        )


def merge(arrived, group, head_local, latent):
    shape = arrived[0].shape[1:]
    return pl.pallas_call(
        functools.partial(merge_kernel, (group, head_local, latent)),
        out_shape=(pltpu.VMEM(shape, jnp.bfloat16),) * SIDE,
        in_specs=[vmem_spec] * SIDE,
        out_specs=(vmem_spec,) * SIDE,
        compiler_params=pltpu.CompilerParams(vmem_limit_bytes=8 * MIB),
        name="merge",
    )(*[in_vmem(one) for one in arrived])


def scatter_tiles(flat, value, first_tile, group, tiles):
    for n in range(value.shape[1] // LANES):
        flat[pl.ds(first_tile + n, group, stride=tiles), :] = value[:, n * LANES : (n + 1) * LANES]


def project_kernel(dims, *refs):
    group, head_local, latent, chunk = dims
    parts = refs[:SIDE]
    w_value, w_out, sent, att_buf, flat = refs[SIDE:]
    rows = group * head_local
    pieces = latent // LANES
    tiles = w_out.shape[1] // LANES
    tail = pieces * rows
    lses = [read_lse(one[tail:, :], head_local) for one in parts]
    share, _ = combine_shares(lses, [list(range(SIDE))], rows, group, head_local)
    totals = [None] * pieces
    for s in range(SIDE):
        factor = jnp.broadcast_to(share[:, s : s + 1], (rows, LANES))
        for p in range(pieces):
            term = parts[s][p * rows : (p + 1) * rows, :].astype(jnp.float32) * factor
            totals[p] = term if s == 0 else totals[p] + term
    for p in range(pieces):
        att_buf[p] = totals[p]
    heads = []
    for j in range(head_local):
        attended = jnp.concatenate(
            [att_buf[p, pl.ds(j, group, stride=head_local), :] for p in range(pieces)], axis=1
        ).astype(jnp.bfloat16)
        heads.append(
            jnp.dot(attended, w_value[j], preferred_element_type=jnp.float32).astype(jnp.bfloat16)
        )
    per_head = jnp.concatenate(heads, axis=1)
    for c in range(w_out.shape[1] // chunk):
        value = jnp.dot(
            per_head, w_out[:, c * chunk : (c + 1) * chunk], preferred_element_type=jnp.float32
        )
        scatter_tiles(flat, value, c * chunk // LANES, group, tiles)
    core = lax.axis_index("tensor") % CORES
    for i in range(group):
        pair, side = i // CORES, i % CORES
        second, place = pair // SIDE, pair % SIDE
        r = jnp.where(core == 0, pair, place * SIDE + second) * CORES + side
        sent[r] = flat[i * tiles : (i + 1) * tiles, :].astype(jnp.bfloat16)


def project(parts, w_value, w_out, group):
    head_local, latent, _ = w_value.shape
    features = w_out.shape[1]
    tiles = features // LANES
    dims = (group, head_local, latent, features // 7)
    return pl.pallas_call(
        functools.partial(project_kernel, dims),
        out_shape=pltpu.VMEM((group, tiles, LANES), jnp.bfloat16),
        in_specs=[vmem_spec] * (SIDE + 2),
        out_specs=vmem_spec,
        scratch_shapes=[
            pltpu.VMEM((latent // LANES, group * head_local, LANES), jnp.float32),
            pltpu.VMEM((group * tiles, LANES), jnp.float32),
        ],
        compiler_params=pltpu.CompilerParams(vmem_limit_bytes=12 * MIB),
        name="project",
    )(*[in_vmem(one) for one in parts], w_value, w_out)


def norm_kernel(got, residual, gain, kept, normed):
    total = residual[...]
    for s in range(got.shape[0]):
        total = total + got[s].astype(jnp.float32)
    kept[...] = total
    mean = jnp.sum(total * total) * (1.0 / total.size)
    value = (total * lax.rsqrt(mean + norm_eps) * gain[...]).astype(jnp.bfloat16)
    for s in range(normed.shape[0]):
        normed[s] = value


def norm(got, residual, gain):
    return pl.pallas_call(
        norm_kernel,
        out_shape=(pltpu.VMEM(residual.shape, jnp.float32), pltpu.VMEM(got.shape, got.dtype)),
        in_specs=[vmem_spec] * 3,
        out_specs=(vmem_spec, vmem_spec),
        compiler_params=pltpu.CompilerParams(vmem_limit_bytes=8 * MIB),
        name="norm",
    )(in_vmem(got), in_vmem(residual), in_vmem(gain))


def ffn_kernel(chunk, normed, w_gate, w_up, w_down, sent, flat, wide):
    group, tiles, _ = normed.shape
    for r in range(group):
        flat[r * tiles : (r + 1) * tiles, :] = normed[r].astype(jnp.float32)
    for n in range(tiles):
        wide[:, n * LANES : (n + 1) * LANES] = flat[pl.ds(n, group, stride=tiles), :].astype(
            jnp.bfloat16
        )
    gate = jnp.dot(wide[...], w_gate[...], preferred_element_type=jnp.float32)
    up = jnp.dot(wide[...], w_up[...], preferred_element_type=jnp.float32)
    activated = (gate / (1.0 + jnp.exp(-gate)) * up).astype(jnp.bfloat16)
    for c in range(w_down.shape[1] // chunk):
        value = jnp.dot(
            activated, w_down[:, c * chunk : (c + 1) * chunk], preferred_element_type=jnp.float32
        )
        scatter_tiles(flat, value, c * chunk // LANES, group, tiles)
    for r in range(group):
        sent[r] = flat[r * tiles : (r + 1) * tiles, :].astype(jnp.bfloat16)


def ffn(normed, w_gate, w_up, w_down):
    group, tiles, _ = normed.shape
    features = tiles * LANES
    return pl.pallas_call(
        functools.partial(ffn_kernel, features // 7),
        out_shape=pltpu.VMEM(normed.shape, jnp.bfloat16),
        in_specs=[vmem_spec] * 4,
        out_specs=vmem_spec,
        scratch_shapes=[
            pltpu.VMEM((group * tiles, LANES), jnp.float32),
            pltpu.VMEM((group, features), jnp.bfloat16),
        ],
        compiler_params=pltpu.CompilerParams(vmem_limit_bytes=12 * MIB),
        name="ffn",
    )(in_vmem(normed), w_gate, w_up, w_down)


def body(
    queries,
    cache_pool,
    holder,
    slot_ids,
    lengths,
    residual,
    w_value,
    w_out,
    norm_gain,
    w_gate,
    w_up,
    w_down,
):
    ranks = lax.axis_size("dp")
    tensors = lax.axis_size("tensor")
    column = lax.axis_index("tensor")
    group = residual.shape[0]
    slots = cache_pool.shape[0]
    head_local, latent, _ = w_value.shape
    features = residual.shape[1]
    tiles = features // LANES
    requests = lengths.shape[0]
    swap = [(i, i ^ 1) for i in range(tensors)]
    from_next = [((i + 1) % ranks, i) for i in range(ranks)]
    from_prev = [((i - 1) % ranks, i) for i in range(ranks)]

    def swapped(value):
        return lax.ppermute(value, "tensor", swap)

    def along(value, first, distance):
        return lax.ppermute(value, "tensor", shifts(tensors, first, distance))

    own_queries = queries[0]
    q_pair = turn(own_queries, swapped(own_queries))
    low, high = split(cache_pool)
    next_low = lax.ppermute(low, "dp", from_next)
    prev_high = lax.ppermute(high, "dp", from_prev)
    low, high = split(cache_pool, q_pair)
    next_high = lax.ppermute(high, "dp", from_next)
    prev_low = lax.ppermute(low, "dp", from_prev)
    own_residual = (
        lax.dynamic_index_in_dim(residual, column, 0, keepdims=False)
        .astype(jnp.float32)
        .reshape(tiles, LANES)
    )
    q_line = join([q_pair] + [along(q_pair, True, d) for d in range(1, SIDE)])
    q_all = [q_line] + [along(q_line, False, e) for e in range(1, SIDE)]
    far_low = lax.ppermute(next_low, "dp", from_next)
    far_high = lax.ppermute(prev_high, "dp", from_prev)
    mine = [next_low, next_high, far_low, far_high, prev_low, prev_high]
    moved = [in_vmem(swapped(one)) for one in mine]
    mine = [in_vmem(one) for one in mine]
    pieces = [in_hbm(cache_pool)] + mine + [in_hbm(swapped(cache_pool))] + moved
    code = (holder * slots + slot_ids).reshape(1, requests)
    code_other = swapped(code)
    gain = norm_gain.reshape(tiles, LANES)
    q_all, own_residual, gain = lax.optimization_barrier((q_all, own_residual, gain))
    w_value, w_out, w_gate, w_up, w_down = [
        in_vmem(one) for one in (w_value, w_out, w_gate, w_up, w_down)
    ]
    partial = attend(
        code,
        code_other,
        lengths.reshape(1, requests),
        q_all,
        pieces,
        ranks,
        latent,
        head_local,
    )
    arrived = [partial[0]] + [along(partial[d], True, d) for d in range(1, SIDE)]
    merged = merge(arrived, group, head_local, latent)
    parts = [merged[0]] + [along(merged[e], False, e) for e in range(1, SIDE)]

    def exchange(value):
        return lax.all_to_all(value, "tensor", split_axis=0, concat_axis=0, tiled=True)

    residual_sum, normed = norm(exchange(project(parts, w_value, w_out, group)), own_residual, gain)
    down = exchange(ffn(exchange(normed), w_gate, w_up, w_down))
    return (residual_sum + jnp.sum(down.astype(jnp.float32), axis=0)).reshape(1, features)


def solution(mesh):
    in_specs = (
        P(("dp", "tensor"), None, None),
        P(("dp", "tensor"), None, None),
        P(None, "tensor"),
        P(None, "tensor"),
        P(),
        P("dp", None),
        P("tensor", None, None),
        P("tensor", None),
        P(),
        P(None, "tensor"),
        P(None, "tensor"),
        P("tensor", None),
    )
    out_specs = P(("dp", "tensor"), None)
    return jax.shard_map(body, mesh=mesh, in_specs=in_specs, out_specs=out_specs, check_vma=False)
```

```python
import functools

import jax
import jax.numpy as jnp
from jax import lax
from jax.experimental import pallas as pl
from jax.experimental.pallas import tpu as pltpu
from jax.sharding import PartitionSpec as P

score_scale = 192.0 ** (-0.5)
norm_eps = 1e-06
far_below = -1e30
CORES = 2
LANES = 128
HEAD_LOCAL = 4
SIDE = 4
MIB = 1024 * 1024
hbm_spec = pl.BlockSpec(memory_space=pl.ANY)
vmem_spec = pl.BlockSpec(memory_space=pltpu.VMEM)
smem_spec = pl.BlockSpec(memory_space=pltpu.SMEM)


def in_vmem(value):
    return pltpu.with_memory_space_constraint(value, pltpu.VMEM)


def in_hbm(value):
    return pltpu.with_memory_space_constraint(value, pltpu.HBM)


def split_kernel(following, previous, low, high, sems):
    half = low.shape[0]
    copies = [
        pltpu.make_async_copy(following.at[pl.ds(0, half)], low, sems.at[0]),
        pltpu.make_async_copy(previous.at[pl.ds(half, half)], high, sems.at[1]),
    ]
    for one in copies:
        one.start()
    for one in copies:
        one.wait()


def split(following, previous):
    half = (following.shape[0] // 2,) + following.shape[1:]
    return pl.pallas_call(
        split_kernel,
        out_shape=(pltpu.VMEM(half, following.dtype), pltpu.VMEM(half, following.dtype)),
        in_specs=[hbm_spec] * 2,
        out_specs=(vmem_spec, vmem_spec),
        scratch_shapes=[pltpu.SemaphoreType.DMA((2,))],
        compiler_params=pltpu.CompilerParams(vmem_limit_bytes=12 * MIB),
        name="split",
    )(following, previous)


def turn_kernel(own, other, out):
    width, head_total = own.shape
    heads = head_total // CORES
    head_local, tail = HEAD_LOCAL, width // LANES * LANES
    core = lax.axis_index("tensor") % CORES
    row = lax.broadcasted_iota(jnp.int32, (heads, head_total), 0)
    wanted = (row // head_local) * (CORES * head_local) + core * head_local + row % head_local
    hit = lax.broadcasted_iota(jnp.int32, (heads, head_total), 1) == wanted
    select = jnp.where(hit, 1.0, 0.0).astype(jnp.bfloat16)
    turned = [
        lax.dot_general(select, one[...], (((1,), (1,)), ((), ())), preferred_element_type=jnp.float32)
        for one in (own, other)
    ]
    pair = [
        jnp.where(core == 0, turned[0], turned[1]).astype(jnp.bfloat16),
        jnp.where(core == 0, turned[1], turned[0]).astype(jnp.bfloat16),
    ]
    rows = [
        pair[i][:, p * LANES : (p + 1) * LANES] for p in range(tail // LANES) for i in range(CORES)
    ]
    out[0] = jnp.concatenate(
        rows + [jnp.concatenate([one[:, tail:] for one in pair], axis=1)], axis=0
    )


def turn(own, other):
    return pl.pallas_call(
        turn_kernel,
        out_shape=jax.ShapeDtypeStruct((1,) + own.shape, own.dtype),
        in_specs=[vmem_spec] * 2,
        out_specs=vmem_spec,
        compiler_params=pltpu.CompilerParams(vmem_limit_bytes=4 * MIB),
        name="turn",
    )(own, other)


def join_kernel(*refs):
    count = len(refs) - 2
    out, sems = refs[count:]
    copies = [
        pltpu.make_async_copy(one, out.at[pl.ds(i, 1)], sems.at[i])
        for i, one in enumerate(refs[:count])
    ]
    for one in copies:
        one.start()
    for one in copies:
        one.wait()


def join(pieces):
    count = len(pieces)
    return pl.pallas_call(
        join_kernel,
        out_shape=jax.ShapeDtypeStruct((count,) + pieces[0].shape[1:], pieces[0].dtype),
        in_specs=[hbm_spec] * count,
        out_specs=hbm_spec,
        scratch_shapes=[pltpu.SemaphoreType.DMA((count,))],
        compiler_params=pltpu.CompilerParams(vmem_limit_bytes=4 * MIB),
        name="join",
    )(*pieces)


def by_core(core, chip):
    x, y = chip % SIDE, chip // SIDE
    return jnp.where(core == 0, x, y), jnp.where(core == 0, y, x)


def shifts(tensors, first, distance):
    pairs = []
    for i in range(tensors):
        core, chip = i % CORES, i // CORES
        x, y = chip % SIDE, chip // SIDE
        if (core == 0) == first:
            x = (x + distance) % SIDE
        else:
            y = (y + distance) % SIDE
        pairs.append((i, (y * SIDE + x) * CORES + core))
    return pairs


def attend_kernel(dims, code_own, code_other, lengths, *refs):
    slots, ranks, head_local, latent, count = dims
    q_refs, pieces = refs[:SIDE], refs[SIDE : SIDE + count]
    outs = refs[SIDE + count : 2 * SIDE + count]
    kbuf, qbuf, obuf, lse_buf, sems = refs[2 * SIDE + count :]
    group = CORES * SIDE * SIDE
    heads = lse_buf.shape[0]
    block_len = kbuf.shape[2]
    owners = heads // head_local
    my_rank = lax.axis_index("dp")
    column = lax.axis_index("tensor")
    core = column % CORES
    own_first, own_second = by_core(core, column // CORES)
    first = my_rank * group
    q_copies = [
        pltpu.make_async_copy(one, qbuf.at[pl.ds(e * SIDE, SIDE)], sems.at[count + e])
        for e, one in enumerate(q_refs)
    ]
    copies, at = [], 0
    for i, one in enumerate(pieces):
        copies.append(pltpu.make_async_copy(one, kbuf.at[pl.ds(at, one.shape[0])], sems.at[i]))
        at += one.shape[0]
    for one in q_copies + copies:
        one.start()
    token = lax.broadcasted_iota(jnp.int32, (1, 2 * block_len), 1)
    partner = column + 1 - 2 * core
    position = jnp.where(
        token < block_len, token + column * block_len, token - block_len + partner * block_len
    )
    lane = lax.broadcasted_iota(jnp.int32, (heads, LANES), 1)
    lse_buf[...] = jnp.zeros_like(lse_buf)
    spots = []
    for k in range(owners):
        k_first, k_second = by_core(core, k)
        spots.append(
            (k_first - own_first + SIDE) % SIDE * SIDE + (k_second - own_second + SIDE) % SIDE
        )
    for one in q_copies + copies:
        one.wait()

    def place(codes, r):
        code = codes[0, first + r]
        return ((code // slots - my_rank + ranks) % ranks) * slots + code % slots

    unroll = CORES * SIDE

    def several(e, carry):
        second = (own_second - e + SIDE) % SIDE
        rs, asked = [], []
        for i in range(SIDE):
            chip = jnp.where(core == 0, second * SIDE + i, i * SIDE + second)
            at = e * SIDE + (own_first - i + SIDE) % SIDE
            for side in range(CORES):
                rs.append(chip * CORES + side)
                rotary = qbuf[at, latent:, :]
                mine = (lane < LANES // CORES) if side == 0 else (lane >= LANES // CORES)
                rows = [
                    qbuf[at, (p * CORES + side) * heads : (p * CORES + side + 1) * heads, :]
                    for p in range(latent // LANES)
                ]
                asked.append(
                    jnp.concatenate(
                        rows + [jnp.where(mine, rotary, jnp.zeros_like(rotary))], axis=1
                    )
                )
        keys = [
            jnp.concatenate(
                [kbuf[place(code_own, r)], kbuf[ranks * slots + place(code_other, r)]], axis=1
            )
            for r in rs
        ]
        scores = [
            jnp.dot(
                q,
                jnp.concatenate([key, key[latent:]], axis=0),
                preferred_element_type=jnp.float32,
            )
            * score_scale
            for q, key in zip(asked, keys)
        ]
        weights, scales, lses = [], [], []
        for r, score in zip(rs, scores):
            live = position < lengths[0, first + r]
            masked = jnp.where(live, score, far_below)
            top = jnp.max(masked, axis=1, keepdims=True)
            weight = jnp.where(live, jnp.exp(masked - top), 0.0)
            total = jnp.sum(weight, axis=1, keepdims=True)
            some = total > 0.0
            safe = jnp.where(some, total, 1.0)
            weights.append(weight.astype(jnp.bfloat16))
            scales.append(jnp.where(some, 1.0 / safe, 0.0))
            lses.append(jnp.where(some, top + jnp.log(safe), far_below))
        mixed = [
            lax.dot_general(
                weight, key[:latent], (((1,), (1,)), ((), ())), preferred_element_type=jnp.float32
            )
            * scale
            for weight, key, scale in zip(weights, keys, scales)
        ]
        lse_all = lse_buf[...]
        for i, lse in enumerate(lses):
            lse_all = jnp.where(lane == second * unroll + i, lse, lse_all)
        lse_buf[...] = lse_all
        rows_count = unroll * head_local
        for k in range(owners):
            both = jnp.concatenate(
                [one[k * head_local : (k + 1) * head_local] for one in mixed], axis=0
            ).astype(jnp.bfloat16)
            for p in range(latent // LANES):
                rows_at = pl.multiple_of(p * group * head_local + second * rows_count, rows_count)
                obuf[spots[k], pl.ds(rows_at, rows_count), :] = both[:, p * LANES : (p + 1) * LANES]
        return carry

    lax.fori_loop(0, SIDE, several, 0)
    tail = latent // LANES * group * head_local
    parts = lse_parts(lse_buf[...])
    for k in range(owners):
        own = slice(k * head_local, (k + 1) * head_local)
        obuf[spots[k], tail:, :] = jnp.concatenate(
            [one[own] for one in parts] + [jnp.zeros_like(parts[0][own])], axis=0
        ).astype(jnp.bfloat16)
    copies = [
        pltpu.make_async_copy(obuf.at[pl.ds(d * SIDE, SIDE)], outs[d], sems.at[d])
        for d in range(SIDE)
    ]
    for one in copies:
        one.start()
    for one in copies:
        one.wait()


def lse_parts(value):
    high = value.astype(jnp.bfloat16).astype(jnp.float32)
    mid = (value - high).astype(jnp.bfloat16).astype(jnp.float32)
    return [high, mid, value - high - mid]


def attend(code_own, code_other, lengths, q_all, pieces, ranks, latent, head_local):
    per, _, head_total = q_all[0].shape
    width, block_len = pieces[0].shape[1:]
    heads = head_total // CORES
    blocks = sum(one.shape[0] for one in pieces)
    chips = SIDE * SIDE
    out_rows = latent // LANES * chips * CORES * head_local + 16
    count = len(pieces)
    dims = (blocks // ranks // CORES, ranks, head_local, latent, count)
    return pl.pallas_call(
        functools.partial(attend_kernel, dims),
        out_shape=(pltpu.VMEM((SIDE, out_rows, LANES), jnp.bfloat16),) * SIDE,
        in_specs=[smem_spec] * 3 + [hbm_spec] * (SIDE + count),
        out_specs=(vmem_spec,) * SIDE,
        scratch_shapes=[
            pltpu.VMEM((blocks, width, block_len), jnp.bfloat16),
            pltpu.VMEM((chips, width, head_total), jnp.bfloat16),
            pltpu.VMEM((chips, out_rows, LANES), jnp.bfloat16),
            pltpu.VMEM((heads, LANES), jnp.float32),
            pltpu.SemaphoreType.DMA((count + SIDE,)),
        ],
        compiler_params=pltpu.CompilerParams(vmem_limit_bytes=22 * MIB),
        name="attend",
    )(code_own, code_other, lengths, *[in_hbm(one) for one in q_all], *pieces)


def combine_shares(lses, sets, rows, group, head_local):
    merged, scaled = [], [None] * len(lses)
    for one_set in sets:
        peak = functools.reduce(jnp.maximum, [lses[s] for s in one_set])
        shares = [jnp.exp(lses[s] - peak) for s in one_set]
        total = functools.reduce(jnp.add, shares)
        merged.append(peak + jnp.log(total))
        inverse = 1.0 / total
        for s, share in zip(one_set, shares):
            scaled[s] = share * inverse
    share_all = jnp.concatenate(scaled, axis=0)
    count = len(lses) * head_local
    pick_request = jnp.where(
        lax.broadcasted_iota(jnp.int32, (rows, LANES), 0) // head_local
        == lax.broadcasted_iota(jnp.int32, (rows, LANES), 1),
        1.0,
        0.0,
    )
    valid = lax.broadcasted_iota(jnp.int32, (count, LANES), 1) < group
    spread = lax.dot_general(
        pick_request,
        jnp.where(valid, share_all, 0.0),
        (((1,), (1,)), ((), ())),
        precision=lax.Precision.HIGHEST,
        preferred_element_type=jnp.float32,
    )
    own_head = (
        lax.broadcasted_iota(jnp.int32, (rows, count), 0) % head_local
        == lax.broadcasted_iota(jnp.int32, (rows, count), 1) % head_local
    )
    pick_source = jnp.where(
        lax.broadcasted_iota(jnp.int32, (count, LANES), 0) // head_local
        == lax.broadcasted_iota(jnp.int32, (count, LANES), 1),
        1.0,
        0.0,
    )
    share = jnp.dot(
        jnp.where(own_head, spread, 0.0),
        pick_source,
        precision=lax.Precision.HIGHEST,
        preferred_element_type=jnp.float32,
    )
    return share, merged


def read_lse(tile, head_local):
    three = tile.astype(jnp.float32)
    return functools.reduce(
        jnp.add, [three[i * head_local : (i + 1) * head_local] for i in range(3)]
    )


def merge_kernel(dims, *refs):
    group, head_local, latent = dims
    ins, outs = refs[:SIDE], refs[SIDE:]
    rows = group * head_local
    pieces = latent // LANES
    tail = pieces * rows
    lses = [read_lse(one[e, tail:, :], head_local) for e in range(SIDE) for one in ins]
    sets = [[e * SIDE + s for s in range(SIDE)] for e in range(SIDE)]
    share, merged = combine_shares(lses, sets, rows, group, head_local)
    for e in range(SIDE):
        totals = [None] * pieces
        for s in range(SIDE):
            at = e * SIDE + s
            factor = jnp.broadcast_to(share[:, at : at + 1], (rows, LANES))
            for p in range(pieces):
                term = ins[s][e, p * rows : (p + 1) * rows, :].astype(jnp.float32) * factor
                totals[p] = term if s == 0 else totals[p] + term
        for p in range(pieces):
            outs[e][p * rows : (p + 1) * rows, :] = totals[p].astype(jnp.bfloat16)
        parts = lse_parts(merged[e])
        outs[e][tail:, :] = jnp.concatenate(parts + [jnp.zeros_like(parts[0])], axis=0).astype(
            jnp.bfloat16
        )


def merge(arrived, group, head_local, latent):
    shape = arrived[0].shape[1:]
    return pl.pallas_call(
        functools.partial(merge_kernel, (group, head_local, latent)),
        out_shape=(pltpu.VMEM(shape, jnp.bfloat16),) * SIDE,
        in_specs=[vmem_spec] * SIDE,
        out_specs=(vmem_spec,) * SIDE,
        compiler_params=pltpu.CompilerParams(vmem_limit_bytes=8 * MIB),
        name="merge",
    )(*[in_vmem(one) for one in arrived])


def scatter_tiles(flat, value, first_tile, group, tiles):
    for n in range(value.shape[1] // LANES):
        flat[pl.ds(first_tile + n, group, stride=tiles), :] = value[:, n * LANES : (n + 1) * LANES]


def project_kernel(dims, *refs):
    group, head_local, latent, chunk = dims
    parts = refs[:SIDE]
    w_value, w_out, sent, att_buf, flat = refs[SIDE:]
    rows = group * head_local
    pieces = latent // LANES
    tiles = w_out.shape[1] // LANES
    tail = pieces * rows
    lses = [read_lse(one[tail:, :], head_local) for one in parts]
    share, _ = combine_shares(lses, [list(range(SIDE))], rows, group, head_local)
    totals = [None] * pieces
    for s in range(SIDE):
        factor = jnp.broadcast_to(share[:, s : s + 1], (rows, LANES))
        for p in range(pieces):
            term = parts[s][p * rows : (p + 1) * rows, :].astype(jnp.float32) * factor
            totals[p] = term if s == 0 else totals[p] + term
    for p in range(pieces):
        att_buf[p] = totals[p]
    heads = []
    for j in range(head_local):
        attended = jnp.concatenate(
            [att_buf[p, pl.ds(j, group, stride=head_local), :] for p in range(pieces)], axis=1
        ).astype(jnp.bfloat16)
        heads.append(
            jnp.dot(attended, w_value[j], preferred_element_type=jnp.float32).astype(jnp.bfloat16)
        )
    per_head = jnp.concatenate(heads, axis=1)
    for c in range(w_out.shape[1] // chunk):
        value = jnp.dot(
            per_head, w_out[:, c * chunk : (c + 1) * chunk], preferred_element_type=jnp.float32
        )
        scatter_tiles(flat, value, c * chunk // LANES, group, tiles)
    core = lax.axis_index("tensor") % CORES
    for i in range(group):
        pair, side = i // CORES, i % CORES
        second, place = pair // SIDE, pair % SIDE
        r = jnp.where(core == 0, pair, place * SIDE + second) * CORES + side
        sent[r] = flat[i * tiles : (i + 1) * tiles, :].astype(jnp.bfloat16)


def project(parts, w_value, w_out, group):
    head_local, latent, _ = w_value.shape
    features = w_out.shape[1]
    tiles = features // LANES
    dims = (group, head_local, latent, features // 7)
    return pl.pallas_call(
        functools.partial(project_kernel, dims),
        out_shape=pltpu.VMEM((group, tiles, LANES), jnp.bfloat16),
        in_specs=[vmem_spec] * (SIDE + 2),
        out_specs=vmem_spec,
        scratch_shapes=[
            pltpu.VMEM((latent // LANES, group * head_local, LANES), jnp.float32),
            pltpu.VMEM((group * tiles, LANES), jnp.float32),
        ],
        compiler_params=pltpu.CompilerParams(vmem_limit_bytes=12 * MIB),
        name="project",
    )(*[in_vmem(one) for one in parts], w_value, w_out)


def norm_kernel(got, residual, gain, kept, normed):
    total = residual[...]
    for s in range(got.shape[0]):
        total = total + got[s].astype(jnp.float32)
    kept[...] = total
    mean = jnp.sum(total * total) * (1.0 / total.size)
    value = (total * lax.rsqrt(mean + norm_eps) * gain[...]).astype(jnp.bfloat16)
    for s in range(normed.shape[0]):
        normed[s] = value


def norm(got, residual, gain):
    return pl.pallas_call(
        norm_kernel,
        out_shape=(pltpu.VMEM(residual.shape, jnp.float32), pltpu.VMEM(got.shape, got.dtype)),
        in_specs=[vmem_spec] * 3,
        out_specs=(vmem_spec, vmem_spec),
        compiler_params=pltpu.CompilerParams(vmem_limit_bytes=8 * MIB),
        name="norm",
    )(in_vmem(got), in_vmem(residual), in_vmem(gain))


def ffn_kernel(chunk, normed, w_gate, w_up, w_down, sent, flat, wide):
    group, tiles, _ = normed.shape
    for r in range(group):
        flat[r * tiles : (r + 1) * tiles, :] = normed[r].astype(jnp.float32)
    for n in range(tiles):
        wide[:, n * LANES : (n + 1) * LANES] = flat[pl.ds(n, group, stride=tiles), :].astype(
            jnp.bfloat16
        )
    gate = jnp.dot(wide[...], w_gate[...], preferred_element_type=jnp.float32)
    up = jnp.dot(wide[...], w_up[...], preferred_element_type=jnp.float32)
    activated = (gate / (1.0 + jnp.exp(-gate)) * up).astype(jnp.bfloat16)
    for c in range(w_down.shape[1] // chunk):
        value = jnp.dot(
            activated, w_down[:, c * chunk : (c + 1) * chunk], preferred_element_type=jnp.float32
        )
        scatter_tiles(flat, value, c * chunk // LANES, group, tiles)
    for r in range(group):
        sent[r] = flat[r * tiles : (r + 1) * tiles, :].astype(jnp.bfloat16)


def ffn(normed, w_gate, w_up, w_down):
    group, tiles, _ = normed.shape
    features = tiles * LANES
    return pl.pallas_call(
        functools.partial(ffn_kernel, features // 7),
        out_shape=pltpu.VMEM(normed.shape, jnp.bfloat16),
        in_specs=[vmem_spec] * 4,
        out_specs=vmem_spec,
        scratch_shapes=[
            pltpu.VMEM((group * tiles, LANES), jnp.float32),
            pltpu.VMEM((group, features), jnp.bfloat16),
        ],
        compiler_params=pltpu.CompilerParams(vmem_limit_bytes=12 * MIB),
        name="ffn",
    )(in_vmem(normed), w_gate, w_up, w_down)


def body(
    queries,
    cache_pool,
    holder,
    slot_ids,
    lengths,
    residual,
    w_value,
    w_out,
    norm_gain,
    w_gate,
    w_up,
    w_down,
):
    ranks = lax.axis_size("dp")
    tensors = lax.axis_size("tensor")
    column = lax.axis_index("tensor")
    group = residual.shape[0]
    slots = cache_pool.shape[0]
    head_local, latent, _ = w_value.shape
    features = residual.shape[1]
    tiles = features // LANES
    requests = lengths.shape[0]
    swap = [(i, i ^ 1) for i in range(tensors)]
    from_next = [((i + 1) % ranks, i) for i in range(ranks)]
    from_prev = [((i - 1) % ranks, i) for i in range(ranks)]

    def swapped(value):
        return lax.ppermute(value, "tensor", swap)

    def along(value, first, distance):
        return lax.ppermute(value, "tensor", shifts(tensors, first, distance))

    own_queries = queries[0]
    other_queries = swapped(own_queries)
    q_pair = turn(own_queries, other_queries)
    following = lax.ppermute(cache_pool, "dp", from_next)
    previous = lax.ppermute(cache_pool, "dp", from_prev)
    q_line = join([q_pair] + [along(q_pair, True, d) for d in range(1, SIDE)])
    q_all = [q_line] + [along(q_line, False, e) for e in range(1, SIDE)]
    passed = split(following, previous)
    far_low = lax.ppermute(passed[0], "dp", from_next)
    far_high = lax.ppermute(passed[1], "dp", from_prev)
    mine = [following, far_low, far_high, previous]
    moved = [in_vmem(swapped(one)) for one in mine]
    mine = [in_vmem(one) for one in mine]
    pieces = [in_hbm(cache_pool)] + mine + [in_hbm(swapped(cache_pool))] + moved
    code = (holder * slots + slot_ids).reshape(1, requests)
    code_other = swapped(code)
    own_residual = (
        lax.dynamic_index_in_dim(residual, column, 0, keepdims=False)
        .astype(jnp.float32)
        .reshape(tiles, LANES)
    )
    gain = norm_gain.reshape(tiles, LANES)
    q_all, own_residual, gain = lax.optimization_barrier((q_all, own_residual, gain))
    w_value, w_out, w_gate, w_up, w_down = [
        in_vmem(one) for one in (w_value, w_out, w_gate, w_up, w_down)
    ]
    partial = attend(
        code,
        code_other,
        lengths.reshape(1, requests),
        q_all,
        pieces,
        ranks,
        latent,
        head_local,
    )
    arrived = [partial[0]] + [along(partial[d], True, d) for d in range(1, SIDE)]
    merged = merge(arrived, group, head_local, latent)
    parts = [merged[0]] + [along(merged[e], False, e) for e in range(1, SIDE)]

    def exchange(value):
        return lax.all_to_all(value, "tensor", split_axis=0, concat_axis=0, tiled=True)

    residual_sum, normed = norm(exchange(project(parts, w_value, w_out, group)), own_residual, gain)
    down = exchange(ffn(exchange(normed), w_gate, w_up, w_down))
    return (residual_sum + jnp.sum(down.astype(jnp.float32), axis=0)).reshape(1, features)


def solution(mesh):
    in_specs = (
        P(("dp", "tensor"), None, None),
        P(("dp", "tensor"), None, None),
        P(None, "tensor"),
        P(None, "tensor"),
        P(),
        P("dp", None),
        P("tensor", None, None),
        P("tensor", None),
        P(),
        P(None, "tensor"),
        P(None, "tensor"),
        P("tensor", None),
    )
    out_specs = P(("dp", "tensor"), None)
    return jax.shard_map(body, mesh=mesh, in_specs=in_specs, out_specs=out_specs, check_vma=False)
```

```python
import functools

import jax
import jax.numpy as jnp
from jax import lax
from jax.experimental import pallas as pl
from jax.experimental.pallas import tpu as pltpu
from jax.sharding import PartitionSpec as P

score_scale = 192.0 ** (-0.5)
norm_eps = 1e-06
far_below = -1e30
CORES = 2
LANES = 128
HEAD_LOCAL = 4
SIDE = 4
MIB = 1024 * 1024
hbm_spec = pl.BlockSpec(memory_space=pl.ANY)
vmem_spec = pl.BlockSpec(memory_space=pltpu.VMEM)
smem_spec = pl.BlockSpec(memory_space=pltpu.SMEM)


def in_vmem(value):
    return pltpu.with_memory_space_constraint(value, pltpu.VMEM)


def in_hbm(value):
    return pltpu.with_memory_space_constraint(value, pltpu.HBM)


def split_kernel(following, previous, low, high, sems):
    half = low.shape[0]
    copies = [
        pltpu.make_async_copy(following.at[pl.ds(0, half)], low, sems.at[0]),
        pltpu.make_async_copy(previous.at[pl.ds(half, half)], high, sems.at[1]),
    ]
    for one in copies:
        one.start()
    for one in copies:
        one.wait()


def split(following, previous):
    half = (following.shape[0] // 2,) + following.shape[1:]
    return pl.pallas_call(
        split_kernel,
        out_shape=(pltpu.VMEM(half, following.dtype), pltpu.VMEM(half, following.dtype)),
        in_specs=[hbm_spec] * 2,
        out_specs=(vmem_spec, vmem_spec),
        scratch_shapes=[pltpu.SemaphoreType.DMA((2,))],
        compiler_params=pltpu.CompilerParams(vmem_limit_bytes=12 * MIB),
        name="split",
    )(following, previous)


def turn_kernel(own, other, out):
    width, head_total = own.shape
    heads = head_total // CORES
    head_local, tail = HEAD_LOCAL, width // LANES * LANES
    core = lax.axis_index("tensor") % CORES
    row = lax.broadcasted_iota(jnp.int32, (heads, head_total), 0)
    wanted = (row // head_local) * (CORES * head_local) + core * head_local + row % head_local
    hit = lax.broadcasted_iota(jnp.int32, (heads, head_total), 1) == wanted
    select = jnp.where(hit, 1.0, 0.0).astype(jnp.bfloat16)
    turned = [
        lax.dot_general(select, one[...], (((1,), (1,)), ((), ())), preferred_element_type=jnp.float32)
        for one in (own, other)
    ]
    pair = [
        jnp.where(core == 0, turned[0], turned[1]).astype(jnp.bfloat16),
        jnp.where(core == 0, turned[1], turned[0]).astype(jnp.bfloat16),
    ]
    rows = [
        pair[i][:, p * LANES : (p + 1) * LANES] for p in range(tail // LANES) for i in range(CORES)
    ]
    out[0] = jnp.concatenate(
        rows + [jnp.concatenate([one[:, tail:] for one in pair], axis=1)], axis=0
    )


def turn(own, other):
    return pl.pallas_call(
        turn_kernel,
        out_shape=jax.ShapeDtypeStruct((1,) + own.shape, own.dtype),
        in_specs=[vmem_spec] * 2,
        out_specs=vmem_spec,
        compiler_params=pltpu.CompilerParams(vmem_limit_bytes=4 * MIB),
        name="turn",
    )(own, other)


def join_kernel(*refs):
    count = len(refs) - 2
    out, sems = refs[count:]
    copies = [
        pltpu.make_async_copy(one, out.at[pl.ds(i, 1)], sems.at[i])
        for i, one in enumerate(refs[:count])
    ]
    for one in copies:
        one.start()
    for one in copies:
        one.wait()


def join(pieces):
    count = len(pieces)
    return pl.pallas_call(
        join_kernel,
        out_shape=jax.ShapeDtypeStruct((count,) + pieces[0].shape[1:], pieces[0].dtype),
        in_specs=[hbm_spec] * count,
        out_specs=hbm_spec,
        scratch_shapes=[pltpu.SemaphoreType.DMA((count,))],
        compiler_params=pltpu.CompilerParams(vmem_limit_bytes=4 * MIB),
        name="join",
    )(*pieces)


def by_core(core, chip):
    x, y = chip % SIDE, chip // SIDE
    return jnp.where(core == 0, x, y), jnp.where(core == 0, y, x)


def shifts(tensors, first, distance):
    pairs = []
    for i in range(tensors):
        core, chip = i % CORES, i // CORES
        x, y = chip % SIDE, chip // SIDE
        if (core == 0) == first:
            x = (x + distance) % SIDE
        else:
            y = (y + distance) % SIDE
        pairs.append((i, (y * SIDE + x) * CORES + core))
    return pairs


def attend_kernel(dims, code_own, code_other, lengths, *refs):
    slots, ranks, head_local, latent, count = dims
    q_refs, pieces = refs[:SIDE], refs[SIDE : SIDE + count]
    outs = refs[SIDE + count : 2 * SIDE + count]
    kbuf, qbuf, obuf, lse_buf, sems = refs[2 * SIDE + count :]
    group = CORES * SIDE * SIDE
    heads = lse_buf.shape[0]
    block_len = kbuf.shape[2]
    owners = heads // head_local
    my_rank = lax.axis_index("dp")
    column = lax.axis_index("tensor")
    core = column % CORES
    own_first, own_second = by_core(core, column // CORES)
    first = my_rank * group
    q_copies = [
        pltpu.make_async_copy(one, qbuf.at[pl.ds(e * SIDE, SIDE)], sems.at[count + e])
        for e, one in enumerate(q_refs)
    ]
    copies, at = [], 0
    for i, one in enumerate(pieces):
        copies.append(pltpu.make_async_copy(one, kbuf.at[pl.ds(at, one.shape[0])], sems.at[i]))
        at += one.shape[0]
    for one in q_copies + copies:
        one.start()
    token = lax.broadcasted_iota(jnp.int32, (1, 2 * block_len), 1)
    partner = column + 1 - 2 * core
    position = jnp.where(
        token < block_len, token + column * block_len, token - block_len + partner * block_len
    )
    lane = lax.broadcasted_iota(jnp.int32, (heads, LANES), 1)
    lse_buf[...] = jnp.zeros_like(lse_buf)
    spots = []
    for k in range(owners):
        k_first, k_second = by_core(core, k)
        spots.append(
            (k_first - own_first + SIDE) % SIDE * SIDE + (k_second - own_second + SIDE) % SIDE
        )
    for one in q_copies + copies:
        one.wait()

    def place(codes, r):
        code = codes[0, first + r]
        return ((code // slots - my_rank + ranks) % ranks) * slots + code % slots

    unroll = CORES * SIDE

    def several(e, carry):
        second = (own_second - e + SIDE) % SIDE
        rs, asked = [], []
        for i in range(SIDE):
            chip = jnp.where(core == 0, second * SIDE + i, i * SIDE + second)
            at = e * SIDE + (own_first - i + SIDE) % SIDE
            for side in range(CORES):
                rs.append(chip * CORES + side)
                rotary = qbuf[at, latent:, :]
                mine = (lane < LANES // CORES) if side == 0 else (lane >= LANES // CORES)
                rows = [
                    qbuf[at, (p * CORES + side) * heads : (p * CORES + side + 1) * heads, :]
                    for p in range(latent // LANES)
                ]
                asked.append(
                    jnp.concatenate(
                        rows + [jnp.where(mine, rotary, jnp.zeros_like(rotary))], axis=1
                    )
                )
        keys = [
            jnp.concatenate(
                [kbuf[place(code_own, r)], kbuf[ranks * slots + place(code_other, r)]], axis=1
            )
            for r in rs
        ]
        scores = [
            jnp.dot(
                q,
                jnp.concatenate([key, key[latent:]], axis=0),
                preferred_element_type=jnp.float32,
            )
            * score_scale
            for q, key in zip(asked, keys)
        ]
        weights, scales, lses = [], [], []
        for r, score in zip(rs, scores):
            live = position < lengths[0, first + r]
            masked = jnp.where(live, score, far_below)
            top = jnp.max(masked, axis=1, keepdims=True)
            weight = jnp.where(live, jnp.exp(masked - top), 0.0)
            total = jnp.sum(weight, axis=1, keepdims=True)
            some = total > 0.0
            safe = jnp.where(some, total, 1.0)
            weights.append(weight.astype(jnp.bfloat16))
            scales.append(jnp.where(some, 1.0 / safe, 0.0))
            lses.append(jnp.where(some, top + jnp.log(safe), far_below))
        mixed = [
            lax.dot_general(
                weight, key[:latent], (((1,), (1,)), ((), ())), preferred_element_type=jnp.float32
            )
            * scale
            for weight, key, scale in zip(weights, keys, scales)
        ]
        lse_all = lse_buf[...]
        for i, lse in enumerate(lses):
            lse_all = jnp.where(lane == second * unroll + i, lse, lse_all)
        lse_buf[...] = lse_all
        rows_count = unroll * head_local
        for k in range(owners):
            both = jnp.concatenate(
                [one[k * head_local : (k + 1) * head_local] for one in mixed], axis=0
            ).astype(jnp.bfloat16)
            for p in range(latent // LANES):
                rows_at = pl.multiple_of(p * group * head_local + second * rows_count, rows_count)
                obuf[spots[k], pl.ds(rows_at, rows_count), :] = both[:, p * LANES : (p + 1) * LANES]
        return carry

    lax.fori_loop(0, SIDE, several, 0)
    tail = latent // LANES * group * head_local
    parts = lse_parts(lse_buf[...])
    for k in range(owners):
        own = slice(k * head_local, (k + 1) * head_local)
        obuf[spots[k], tail:, :] = jnp.concatenate(
            [one[own] for one in parts] + [jnp.zeros_like(parts[0][own])], axis=0
        ).astype(jnp.bfloat16)
    copies = [
        pltpu.make_async_copy(obuf.at[pl.ds(d * SIDE, SIDE)], outs[d], sems.at[d])
        for d in range(SIDE)
    ]
    for one in copies:
        one.start()
    for one in copies:
        one.wait()


def lse_parts(value):
    high = value.astype(jnp.bfloat16).astype(jnp.float32)
    mid = (value - high).astype(jnp.bfloat16).astype(jnp.float32)
    return [high, mid, value - high - mid]


def attend(code_own, code_other, lengths, q_all, pieces, ranks, latent, head_local):
    per, _, head_total = q_all[0].shape
    width, block_len = pieces[0].shape[1:]
    heads = head_total // CORES
    blocks = sum(one.shape[0] for one in pieces)
    chips = SIDE * SIDE
    out_rows = latent // LANES * chips * CORES * head_local + 16
    count = len(pieces)
    dims = (blocks // ranks // CORES, ranks, head_local, latent, count)
    return pl.pallas_call(
        functools.partial(attend_kernel, dims),
        out_shape=(pltpu.VMEM((SIDE, out_rows, LANES), jnp.bfloat16),) * SIDE,
        in_specs=[smem_spec] * 3 + [hbm_spec] * (SIDE + count),
        out_specs=(vmem_spec,) * SIDE,
        scratch_shapes=[
            pltpu.VMEM((blocks, width, block_len), jnp.bfloat16),
            pltpu.VMEM((chips, width, head_total), jnp.bfloat16),
            pltpu.VMEM((chips, out_rows, LANES), jnp.bfloat16),
            pltpu.VMEM((heads, LANES), jnp.float32),
            pltpu.SemaphoreType.DMA((count + SIDE,)),
        ],
        compiler_params=pltpu.CompilerParams(vmem_limit_bytes=22 * MIB),
        name="attend",
    )(code_own, code_other, lengths, *[in_hbm(one) for one in q_all], *pieces)


def combine_shares(lses, sets, rows, group, head_local):
    merged, scaled = [], [None] * len(lses)
    for one_set in sets:
        peak = functools.reduce(jnp.maximum, [lses[s] for s in one_set])
        shares = [jnp.exp(lses[s] - peak) for s in one_set]
        total = functools.reduce(jnp.add, shares)
        merged.append(peak + jnp.log(total))
        inverse = 1.0 / total
        for s, share in zip(one_set, shares):
            scaled[s] = share * inverse
    share_all = jnp.concatenate(scaled, axis=0)
    count = len(lses) * head_local
    pick_request = jnp.where(
        lax.broadcasted_iota(jnp.int32, (rows, LANES), 0) // head_local
        == lax.broadcasted_iota(jnp.int32, (rows, LANES), 1),
        1.0,
        0.0,
    )
    valid = lax.broadcasted_iota(jnp.int32, (count, LANES), 1) < group
    spread = lax.dot_general(
        pick_request,
        jnp.where(valid, share_all, 0.0),
        (((1,), (1,)), ((), ())),
        precision=lax.Precision.HIGHEST,
        preferred_element_type=jnp.float32,
    )
    own_head = (
        lax.broadcasted_iota(jnp.int32, (rows, count), 0) % head_local
        == lax.broadcasted_iota(jnp.int32, (rows, count), 1) % head_local
    )
    pick_source = jnp.where(
        lax.broadcasted_iota(jnp.int32, (count, LANES), 0) // head_local
        == lax.broadcasted_iota(jnp.int32, (count, LANES), 1),
        1.0,
        0.0,
    )
    share = jnp.dot(
        jnp.where(own_head, spread, 0.0),
        pick_source,
        precision=lax.Precision.HIGHEST,
        preferred_element_type=jnp.float32,
    )
    return share, merged


def read_lse(tile, head_local):
    three = tile.astype(jnp.float32)
    return functools.reduce(
        jnp.add, [three[i * head_local : (i + 1) * head_local] for i in range(3)]
    )


def merge_kernel(dims, *refs):
    group, head_local, latent = dims
    ins, outs = refs[:SIDE], refs[SIDE:]
    rows = group * head_local
    pieces = latent // LANES
    tail = pieces * rows
    lses = [read_lse(one[e, tail:, :], head_local) for e in range(SIDE) for one in ins]
    sets = [[e * SIDE + s for s in range(SIDE)] for e in range(SIDE)]
    share, merged = combine_shares(lses, sets, rows, group, head_local)
    for e in range(SIDE):
        totals = [None] * pieces
        for s in range(SIDE):
            at = e * SIDE + s
            factor = jnp.broadcast_to(share[:, at : at + 1], (rows, LANES))
            for p in range(pieces):
                term = ins[s][e, p * rows : (p + 1) * rows, :].astype(jnp.float32) * factor
                totals[p] = term if s == 0 else totals[p] + term
        for p in range(pieces):
            outs[e][p * rows : (p + 1) * rows, :] = totals[p].astype(jnp.bfloat16)
        parts = lse_parts(merged[e])
        outs[e][tail:, :] = jnp.concatenate(parts + [jnp.zeros_like(parts[0])], axis=0).astype(
            jnp.bfloat16
        )


def merge(arrived, group, head_local, latent):
    shape = arrived[0].shape[1:]
    return pl.pallas_call(
        functools.partial(merge_kernel, (group, head_local, latent)),
        out_shape=(pltpu.VMEM(shape, jnp.bfloat16),) * SIDE,
        in_specs=[vmem_spec] * SIDE,
        out_specs=(vmem_spec,) * SIDE,
        compiler_params=pltpu.CompilerParams(vmem_limit_bytes=8 * MIB),
        name="merge",
    )(*[in_vmem(one) for one in arrived])


def scatter_tiles(flat, value, first_tile, group, tiles):
    for n in range(value.shape[1] // LANES):
        flat[pl.ds(first_tile + n, group, stride=tiles), :] = value[:, n * LANES : (n + 1) * LANES]


def project_kernel(dims, *refs):
    group, head_local, latent, chunk = dims
    parts = refs[:SIDE]
    w_value, w_out, kept, passed, att_buf, flat = refs[SIDE:]
    rows = group * head_local
    pieces = latent // LANES
    tiles = w_out.shape[1] // LANES
    tail = pieces * rows
    lses = [read_lse(one[tail:, :], head_local) for one in parts]
    share, _ = combine_shares(lses, [list(range(SIDE))], rows, group, head_local)
    totals = [None] * pieces
    for s in range(SIDE):
        factor = jnp.broadcast_to(share[:, s : s + 1], (rows, LANES))
        for p in range(pieces):
            term = parts[s][p * rows : (p + 1) * rows, :].astype(jnp.float32) * factor
            totals[p] = term if s == 0 else totals[p] + term
    for p in range(pieces):
        att_buf[p] = totals[p]
    heads = []
    for j in range(head_local):
        attended = jnp.concatenate(
            [att_buf[p, pl.ds(j, group, stride=head_local), :] for p in range(pieces)], axis=1
        ).astype(jnp.bfloat16)
        heads.append(
            jnp.dot(attended, w_value[j], preferred_element_type=jnp.float32).astype(jnp.bfloat16)
        )
    per_head = jnp.concatenate(heads, axis=1)
    for c in range(w_out.shape[1] // chunk):
        value = jnp.dot(
            per_head, w_out[:, c * chunk : (c + 1) * chunk], preferred_element_type=jnp.float32
        )
        scatter_tiles(flat, value, c * chunk // LANES, group, tiles)
    core = lax.axis_index("tensor") % CORES
    for chip in range(SIDE * SIDE):
        pair = jnp.where(core == 0, chip, chip % SIDE * SIDE + chip // SIDE)
        for out, side in ((kept, core), (passed, 1 - core)):
            at = pl.multiple_of((pair * CORES + side) * tiles, 8)
            out[chip] = flat[pl.ds(at, tiles), :].astype(jnp.bfloat16)


def project(parts, w_value, w_out, group):
    head_local, latent, _ = w_value.shape
    features = w_out.shape[1]
    tiles = features // LANES
    dims = (group, head_local, latent, features // 7)
    return pl.pallas_call(
        functools.partial(project_kernel, dims),
        out_shape=(pltpu.VMEM((group // CORES, tiles, LANES), jnp.bfloat16),) * CORES,
        in_specs=[vmem_spec] * (SIDE + 2),
        out_specs=(vmem_spec,) * CORES,
        scratch_shapes=[
            pltpu.VMEM((latent // LANES, group * head_local, LANES), jnp.float32),
            pltpu.VMEM((group * tiles, LANES), jnp.float32),
        ],
        compiler_params=pltpu.CompilerParams(vmem_limit_bytes=12 * MIB),
        name="project",
    )(*[in_vmem(one) for one in parts], w_value, w_out)


def add_kernel(one, other, out):
    for s in range(out.shape[0]):
        out[s] = (one[s].astype(jnp.float32) + other[s].astype(jnp.float32)).astype(out.dtype)


def add(one, other):
    return pl.pallas_call(
        add_kernel,
        out_shape=pltpu.VMEM(one.shape, one.dtype),
        in_specs=[vmem_spec] * 2,
        out_specs=vmem_spec,
        compiler_params=pltpu.CompilerParams(vmem_limit_bytes=4 * MIB),
        name="add",
    )(in_vmem(one), in_vmem(other))


def norm_kernel(got, residual, gain, kept, normed):
    total = residual[...]
    for s in range(got.shape[0]):
        total = total + got[s].astype(jnp.float32)
    kept[...] = total
    mean = jnp.sum(total * total) * (1.0 / total.size)
    value = (total * lax.rsqrt(mean + norm_eps) * gain[...]).astype(jnp.bfloat16)
    for s in range(normed.shape[0]):
        normed[s] = value


def norm(got, residual, gain):
    return pl.pallas_call(
        norm_kernel,
        out_shape=(pltpu.VMEM(residual.shape, jnp.float32), pltpu.VMEM(got.shape, got.dtype)),
        in_specs=[vmem_spec] * 3,
        out_specs=(vmem_spec, vmem_spec),
        compiler_params=pltpu.CompilerParams(vmem_limit_bytes=8 * MIB),
        name="norm",
    )(in_vmem(got), in_vmem(residual), in_vmem(gain))


def ffn_kernel(chunk, *refs):
    normed, (w_gate, w_up, w_down) = refs[:CORES], refs[CORES : CORES + 3]
    outs, (flat, wide) = refs[CORES + 3 : 2 * CORES + 3], refs[2 * CORES + 3 :]
    half, tiles, _ = normed[0].shape
    group = CORES * half
    for c in range(CORES):
        for r in range(half):
            at = (c * half + r) * tiles
            flat[at : at + tiles, :] = normed[c][r].astype(jnp.float32)
    for n in range(tiles):
        wide[:, n * LANES : (n + 1) * LANES] = flat[pl.ds(n, group, stride=tiles), :].astype(
            jnp.bfloat16
        )
    gate = jnp.dot(wide[...], w_gate[...], preferred_element_type=jnp.float32)
    up = jnp.dot(wide[...], w_up[...], preferred_element_type=jnp.float32)
    activated = (gate / (1.0 + jnp.exp(-gate)) * up).astype(jnp.bfloat16)
    for c in range(w_down.shape[1] // chunk):
        value = jnp.dot(
            activated, w_down[:, c * chunk : (c + 1) * chunk], preferred_element_type=jnp.float32
        )
        scatter_tiles(flat, value, c * chunk // LANES, group, tiles)
    for c in range(CORES):
        for r in range(half):
            at = (c * half + r) * tiles
            outs[c][r] = flat[at : at + tiles, :].astype(jnp.bfloat16)


def ffn(normed, w_gate, w_up, w_down):
    half, tiles, _ = normed[0].shape
    group, features = CORES * half, tiles * LANES
    return pl.pallas_call(
        functools.partial(ffn_kernel, features // 7),
        out_shape=(pltpu.VMEM(normed[0].shape, jnp.bfloat16),) * CORES,
        in_specs=[vmem_spec] * (CORES + 3),
        out_specs=(vmem_spec,) * CORES,
        scratch_shapes=[
            pltpu.VMEM((group * tiles, LANES), jnp.float32),
            pltpu.VMEM((group, features), jnp.bfloat16),
        ],
        compiler_params=pltpu.CompilerParams(vmem_limit_bytes=12 * MIB),
        name="ffn",
    )(*[in_vmem(one) for one in normed], w_gate, w_up, w_down)


def body(
    queries,
    cache_pool,
    holder,
    slot_ids,
    lengths,
    residual,
    w_value,
    w_out,
    norm_gain,
    w_gate,
    w_up,
    w_down,
):
    ranks = lax.axis_size("dp")
    tensors = lax.axis_size("tensor")
    column = lax.axis_index("tensor")
    group = residual.shape[0]
    slots = cache_pool.shape[0]
    head_local, latent, _ = w_value.shape
    features = residual.shape[1]
    tiles = features // LANES
    requests = lengths.shape[0]
    swap = [(i, i ^ 1) for i in range(tensors)]
    from_next = [((i + 1) % ranks, i) for i in range(ranks)]
    from_prev = [((i - 1) % ranks, i) for i in range(ranks)]

    def swapped(value):
        return lax.ppermute(value, "tensor", swap)

    def along(value, first, distance):
        return lax.ppermute(value, "tensor", shifts(tensors, first, distance))

    own_queries = queries[0]
    other_queries = swapped(own_queries)
    q_pair = turn(own_queries, other_queries)
    following = lax.ppermute(cache_pool, "dp", from_next)
    previous = lax.ppermute(cache_pool, "dp", from_prev)
    q_line = join([q_pair] + [along(q_pair, True, d) for d in range(1, SIDE)])
    q_all = [q_line] + [along(q_line, False, e) for e in range(1, SIDE)]
    passed = split(following, previous)
    far_low = lax.ppermute(passed[0], "dp", from_next)
    far_high = lax.ppermute(passed[1], "dp", from_prev)
    mine = [following, far_low, far_high, previous]
    moved = [in_vmem(swapped(one)) for one in mine]
    mine = [in_vmem(one) for one in mine]
    pieces = [in_hbm(cache_pool)] + mine + [in_hbm(swapped(cache_pool))] + moved
    code = (holder * slots + slot_ids).reshape(1, requests)
    code_other = swapped(code)
    own_residual = (
        lax.dynamic_index_in_dim(residual, column, 0, keepdims=False)
        .astype(jnp.float32)
        .reshape(tiles, LANES)
    )
    gain = norm_gain.reshape(tiles, LANES)
    q_all, own_residual, gain = lax.optimization_barrier((q_all, own_residual, gain))
    w_value, w_out, w_gate, w_up, w_down = [
        in_vmem(one) for one in (w_value, w_out, w_gate, w_up, w_down)
    ]
    partial = attend(
        code,
        code_other,
        lengths.reshape(1, requests),
        q_all,
        pieces,
        ranks,
        latent,
        head_local,
    )
    arrived = [partial[0]] + [along(partial[d], True, d) for d in range(1, SIDE)]
    merged = merge(arrived, group, head_local, latent)
    parts = [merged[0]] + [along(merged[e], False, e) for e in range(1, SIDE)]

    chips = SIDE * SIDE
    same_core = [[c + CORES * k for k in range(chips)] for c in range(CORES)]

    def exchange(value):
        return lax.all_to_all(
            value, "tensor", split_axis=0, concat_axis=0, tiled=True, axis_index_groups=same_core
        )

    def to_rows(kept, passed):
        return exchange(add(kept, swapped(passed)))

    residual_sum, normed = norm(
        to_rows(*project(parts, w_value, w_out, group)), own_residual, gain
    )
    rows = exchange(normed)
    down = to_rows(*ffn((rows, swapped(rows)), w_gate, w_up, w_down))
    return (residual_sum + jnp.sum(down.astype(jnp.float32), axis=0)).reshape(1, features)


def solution(mesh):
    in_specs = (
        P(("dp", "tensor"), None, None),
        P(("dp", "tensor"), None, None),
        P(None, "tensor"),
        P(None, "tensor"),
        P(),
        P("dp", None),
        P("tensor", None, None),
        P("tensor", None),
        P(),
        P(None, "tensor"),
        P(None, "tensor"),
        P("tensor", None),
    )
    out_specs = P(("dp", "tensor"), None)
    return jax.shard_map(body, mesh=mesh, in_specs=in_specs, out_specs=out_specs, check_vma=False)
```

```python
import functools

import jax
import jax.numpy as jnp
from jax import lax
from jax.experimental import pallas as pl
from jax.experimental.pallas import tpu as pltpu
from jax.sharding import PartitionSpec as P

score_scale = 192.0 ** (-0.5)
norm_eps = 1e-06
far_below = -1e30
CORES = 2
LANES = 128
HEAD_LOCAL = 4
SIDE = 4
MIB = 1024 * 1024
hbm_spec = pl.BlockSpec(memory_space=pl.ANY)
vmem_spec = pl.BlockSpec(memory_space=pltpu.VMEM)
smem_spec = pl.BlockSpec(memory_space=pltpu.SMEM)


def in_vmem(value):
    return pltpu.with_memory_space_constraint(value, pltpu.VMEM)


def moves(size):
    return pl.CostEstimate(flops=0, bytes_accessed=size, transcendentals=0)


def in_hbm(value):
    return pltpu.with_memory_space_constraint(value, pltpu.HBM)


def cut_kernel(first, blocks, out, sem):
    copy = pltpu.make_async_copy(blocks.at[pl.ds(first, out.shape[0])], out, sem)
    copy.start()
    copy.wait()


def cut(blocks, first):
    half = (blocks.shape[0] // 2,) + blocks.shape[1:]
    return pl.pallas_call(
        functools.partial(cut_kernel, first),
        out_shape=pltpu.VMEM(half, blocks.dtype),
        in_specs=[hbm_spec],
        out_specs=vmem_spec,
        scratch_shapes=[pltpu.SemaphoreType.DMA],
        compiler_params=pltpu.CompilerParams(vmem_limit_bytes=4 * MIB),
        cost_estimate=moves(1200000),
        name="cut",
    )(blocks)


def fetch_kernel(weight, _, out, sem):
    copy = pltpu.make_async_copy(weight, out, sem)
    copy.start()
    copy.wait()


def fetch(weight, after):
    return pl.pallas_call(
        fetch_kernel,
        out_shape=pltpu.VMEM(weight.shape, weight.dtype),
        in_specs=[hbm_spec, vmem_spec],
        out_specs=vmem_spec,
        scratch_shapes=[pltpu.SemaphoreType.DMA],
        compiler_params=pltpu.CompilerParams(vmem_limit_bytes=4 * MIB),
        cost_estimate=moves(2 * weight.size * weight.dtype.itemsize),
        name="fetch",
    )(in_hbm(weight), in_vmem(after))


def turn_kernel(own, other, out):
    width, head_total = own.shape
    heads = head_total // CORES
    head_local, tail = HEAD_LOCAL, width // LANES * LANES
    core = lax.axis_index("tensor") % CORES
    row = lax.broadcasted_iota(jnp.int32, (heads, head_total), 0)
    wanted = (row // head_local) * (CORES * head_local) + core * head_local + row % head_local
    hit = lax.broadcasted_iota(jnp.int32, (heads, head_total), 1) == wanted
    select = jnp.where(hit, 1.0, 0.0).astype(jnp.bfloat16)
    turned = [
        lax.dot_general(select, one[...], (((1,), (1,)), ((), ())), preferred_element_type=jnp.float32)
        for one in (own, other)
    ]
    pair = [
        jnp.where(core == 0, turned[0], turned[1]).astype(jnp.bfloat16),
        jnp.where(core == 0, turned[1], turned[0]).astype(jnp.bfloat16),
    ]
    rows = [
        pair[i][:, p * LANES : (p + 1) * LANES] for p in range(tail // LANES) for i in range(CORES)
    ]
    out[0] = jnp.concatenate(
        rows + [jnp.concatenate([one[:, tail:] for one in pair], axis=1)], axis=0
    )


def turn(own, other):
    return pl.pallas_call(
        turn_kernel,
        out_shape=jax.ShapeDtypeStruct((1,) + own.shape, own.dtype),
        in_specs=[vmem_spec] * 2,
        out_specs=vmem_spec,
        compiler_params=pltpu.CompilerParams(vmem_limit_bytes=4 * MIB),
        cost_estimate=moves(450000),
        name="turn",
    )(own, other)


def join_kernel(*refs):
    count = len(refs) - 2
    out, sems = refs[count:]
    copies = [
        pltpu.make_async_copy(one, out.at[pl.ds(i, 1)], sems.at[i])
        for i, one in enumerate(refs[:count])
    ]
    for one in copies:
        one.start()
    for one in copies:
        one.wait()


def join(pieces):
    count = len(pieces)
    return pl.pallas_call(
        join_kernel,
        out_shape=jax.ShapeDtypeStruct((count,) + pieces[0].shape[1:], pieces[0].dtype),
        in_specs=[hbm_spec] * count,
        out_specs=hbm_spec,
        scratch_shapes=[pltpu.SemaphoreType.DMA((count,))],
        compiler_params=pltpu.CompilerParams(vmem_limit_bytes=4 * MIB),
        cost_estimate=moves(1200000),
        name="join",
    )(*pieces)


def by_core(core, chip):
    x, y = chip % SIDE, chip // SIDE
    return jnp.where(core == 0, x, y), jnp.where(core == 0, y, x)


def shifts(tensors, first, distance):
    pairs = []
    for i in range(tensors):
        core, chip = i % CORES, i // CORES
        x, y = chip % SIDE, chip // SIDE
        if (core == 0) == first:
            x = (x + distance) % SIDE
        else:
            y = (y + distance) % SIDE
        pairs.append((i, (y * SIDE + x) * CORES + core))
    return pairs


def attend_kernel(dims, code_own, code_other, lengths, *refs):
    slots, ranks, head_local, latent, count = dims
    q_refs, pieces = refs[:SIDE], refs[SIDE : SIDE + count]
    outs = refs[SIDE + count : 2 * SIDE + count]
    kbuf, qbuf, obuf, lse_buf, sems = refs[2 * SIDE + count :]
    group = CORES * SIDE * SIDE
    heads = lse_buf.shape[0]
    block_len = kbuf.shape[2]
    owners = heads // head_local
    my_rank = lax.axis_index("dp")
    column = lax.axis_index("tensor")
    core = column % CORES
    own_first, own_second = by_core(core, column // CORES)
    first = my_rank * group
    q_copies = [
        pltpu.make_async_copy(one, qbuf.at[pl.ds(e * SIDE, SIDE)], sems.at[count + e])
        for e, one in enumerate(q_refs)
    ]
    copies, at = [], 0
    for i, one in enumerate(pieces):
        copies.append(pltpu.make_async_copy(one, kbuf.at[pl.ds(at, one.shape[0])], sems.at[i]))
        at += one.shape[0]
    for one in q_copies + copies:
        one.start()
    token = lax.broadcasted_iota(jnp.int32, (1, 2 * block_len), 1)
    partner = column + 1 - 2 * core
    position = jnp.where(
        token < block_len, token + column * block_len, token - block_len + partner * block_len
    )
    lane = lax.broadcasted_iota(jnp.int32, (heads, LANES), 1)
    lse_buf[...] = jnp.zeros_like(lse_buf)
    spots = []
    for k in range(owners):
        k_first, k_second = by_core(core, k)
        spots.append(
            (k_first - own_first + SIDE) % SIDE * SIDE + (k_second - own_second + SIDE) % SIDE
        )
    for one in q_copies + copies:
        one.wait()

    def place(codes, r):
        code = codes[0, first + r]
        return ((code // slots - my_rank + ranks) % ranks) * slots + code % slots

    unroll = CORES * SIDE

    def several(e, carry):
        second = (own_second - e + SIDE) % SIDE
        rs, asked = [], []
        for i in range(SIDE):
            chip = jnp.where(core == 0, second * SIDE + i, i * SIDE + second)
            at = e * SIDE + (own_first - i + SIDE) % SIDE
            for side in range(CORES):
                rs.append(chip * CORES + side)
                rotary = qbuf[at, latent:, :]
                mine = (lane < LANES // CORES) if side == 0 else (lane >= LANES // CORES)
                rows = [
                    qbuf[at, (p * CORES + side) * heads : (p * CORES + side + 1) * heads, :]
                    for p in range(latent // LANES)
                ]
                asked.append(
                    jnp.concatenate(
                        rows + [jnp.where(mine, rotary, jnp.zeros_like(rotary))], axis=1
                    )
                )
        keys = [
            jnp.concatenate(
                [kbuf[place(code_own, r)], kbuf[ranks * slots + place(code_other, r)]], axis=1
            )
            for r in rs
        ]
        scores = [
            jnp.dot(
                q,
                jnp.concatenate([key, key[latent:]], axis=0),
                preferred_element_type=jnp.float32,
            )
            * score_scale
            for q, key in zip(asked, keys)
        ]
        weights, scales, lses = [], [], []
        for r, score in zip(rs, scores):
            live = position < lengths[0, first + r]
            masked = jnp.where(live, score, far_below)
            top = jnp.max(masked, axis=1, keepdims=True)
            weight = jnp.where(live, jnp.exp(masked - top), 0.0)
            total = jnp.sum(weight, axis=1, keepdims=True)
            some = total > 0.0
            safe = jnp.where(some, total, 1.0)
            weights.append(weight.astype(jnp.bfloat16))
            scales.append(jnp.where(some, 1.0 / safe, 0.0))
            lses.append(jnp.where(some, top + jnp.log(safe), far_below))
        mixed = [
            lax.dot_general(
                weight, key[:latent], (((1,), (1,)), ((), ())), preferred_element_type=jnp.float32
            )
            * scale
            for weight, key, scale in zip(weights, keys, scales)
        ]
        lse_all = lse_buf[...]
        for i, lse in enumerate(lses):
            lse_all = jnp.where(lane == second * unroll + i, lse, lse_all)
        lse_buf[...] = lse_all
        rows_count = unroll * head_local
        for k in range(owners):
            both = jnp.concatenate(
                [one[k * head_local : (k + 1) * head_local] for one in mixed], axis=0
            ).astype(jnp.bfloat16)
            for p in range(latent // LANES):
                rows_at = pl.multiple_of(p * group * head_local + second * rows_count, rows_count)
                obuf[spots[k], pl.ds(rows_at, rows_count), :] = both[:, p * LANES : (p + 1) * LANES]
        return carry

    lax.fori_loop(0, SIDE, several, 0)
    tail = latent // LANES * group * head_local
    parts = lse_parts(lse_buf[...])
    for k in range(owners):
        own = slice(k * head_local, (k + 1) * head_local)
        obuf[spots[k], tail:, :] = jnp.concatenate(
            [one[own] for one in parts] + [jnp.zeros_like(parts[0][own])], axis=0
        ).astype(jnp.bfloat16)
    copies = [
        pltpu.make_async_copy(obuf.at[pl.ds(d * SIDE, SIDE)], outs[d], sems.at[d])
        for d in range(SIDE)
    ]
    for one in copies:
        one.start()
    for one in copies:
        one.wait()


def lse_parts(value):
    high = value.astype(jnp.bfloat16).astype(jnp.float32)
    mid = (value - high).astype(jnp.bfloat16).astype(jnp.float32)
    return [high, mid, value - high - mid]


def attend(code_own, code_other, lengths, q_all, pieces, ranks, latent, head_local):
    per, _, head_total = q_all[0].shape
    width, block_len = pieces[0].shape[1:]
    heads = head_total // CORES
    blocks = sum(one.shape[0] for one in pieces)
    chips = SIDE * SIDE
    out_rows = latent // LANES * chips * CORES * head_local + 16
    count = len(pieces)
    dims = (blocks // ranks // CORES, ranks, head_local, latent, count)
    return pl.pallas_call(
        functools.partial(attend_kernel, dims),
        out_shape=(pltpu.VMEM((SIDE, out_rows, LANES), jnp.bfloat16),) * SIDE,
        in_specs=[smem_spec] * 3 + [hbm_spec] * (SIDE + count),
        out_specs=(vmem_spec,) * SIDE,
        scratch_shapes=[
            pltpu.VMEM((blocks, width, block_len), jnp.bfloat16),
            pltpu.VMEM((chips, width, head_total), jnp.bfloat16),
            pltpu.VMEM((chips, out_rows, LANES), jnp.bfloat16),
            pltpu.VMEM((heads, LANES), jnp.float32),
            pltpu.SemaphoreType.DMA((count + SIDE,)),
        ],
        compiler_params=pltpu.CompilerParams(vmem_limit_bytes=22 * MIB),
        cost_estimate=moves(20000000),
        name="attend",
    )(code_own, code_other, lengths, *[in_hbm(one) for one in q_all], *pieces)


def combine_shares(lses, sets, rows, group, head_local):
    merged, scaled = [], [None] * len(lses)
    for one_set in sets:
        peak = functools.reduce(jnp.maximum, [lses[s] for s in one_set])
        shares = [jnp.exp(lses[s] - peak) for s in one_set]
        total = functools.reduce(jnp.add, shares)
        merged.append(peak + jnp.log(total))
        inverse = 1.0 / total
        for s, share in zip(one_set, shares):
            scaled[s] = share * inverse
    share_all = jnp.concatenate(scaled, axis=0)
    count = len(lses) * head_local
    pick_request = jnp.where(
        lax.broadcasted_iota(jnp.int32, (rows, LANES), 0) // head_local
        == lax.broadcasted_iota(jnp.int32, (rows, LANES), 1),
        1.0,
        0.0,
    )
    valid = lax.broadcasted_iota(jnp.int32, (count, LANES), 1) < group
    spread = lax.dot_general(
        pick_request,
        jnp.where(valid, share_all, 0.0),
        (((1,), (1,)), ((), ())),
        precision=lax.Precision.HIGHEST,
        preferred_element_type=jnp.float32,
    )
    own_head = (
        lax.broadcasted_iota(jnp.int32, (rows, count), 0) % head_local
        == lax.broadcasted_iota(jnp.int32, (rows, count), 1) % head_local
    )
    pick_source = jnp.where(
        lax.broadcasted_iota(jnp.int32, (count, LANES), 0) // head_local
        == lax.broadcasted_iota(jnp.int32, (count, LANES), 1),
        1.0,
        0.0,
    )
    share = jnp.dot(
        jnp.where(own_head, spread, 0.0),
        pick_source,
        precision=lax.Precision.HIGHEST,
        preferred_element_type=jnp.float32,
    )
    return share, merged


def read_lse(tile, head_local):
    three = tile.astype(jnp.float32)
    return functools.reduce(
        jnp.add, [three[i * head_local : (i + 1) * head_local] for i in range(3)]
    )


def merge_kernel(dims, *refs):
    group, head_local, latent = dims
    ins, outs = refs[:SIDE], refs[SIDE:]
    rows = group * head_local
    pieces = latent // LANES
    tail = pieces * rows
    lses = [read_lse(one[e, tail:, :], head_local) for e in range(SIDE) for one in ins]
    sets = [[e * SIDE + s for s in range(SIDE)] for e in range(SIDE)]
    share, merged = combine_shares(lses, sets, rows, group, head_local)
    for e in range(SIDE):
        totals = [None] * pieces
        for s in range(SIDE):
            at = e * SIDE + s
            factor = jnp.broadcast_to(share[:, at : at + 1], (rows, LANES))
            for p in range(pieces):
                term = ins[s][e, p * rows : (p + 1) * rows, :].astype(jnp.float32) * factor
                totals[p] = term if s == 0 else totals[p] + term
        for p in range(pieces):
            outs[e][p * rows : (p + 1) * rows, :] = totals[p].astype(jnp.bfloat16)
        parts = lse_parts(merged[e])
        outs[e][tail:, :] = jnp.concatenate(parts + [jnp.zeros_like(parts[0])], axis=0).astype(
            jnp.bfloat16
        )


def merge(arrived, group, head_local, latent):
    shape = arrived[0].shape[1:]
    return pl.pallas_call(
        functools.partial(merge_kernel, (group, head_local, latent)),
        out_shape=(pltpu.VMEM(shape, jnp.bfloat16),) * SIDE,
        in_specs=[vmem_spec] * SIDE,
        out_specs=(vmem_spec,) * SIDE,
        compiler_params=pltpu.CompilerParams(vmem_limit_bytes=8 * MIB),
        cost_estimate=moves(4500000),
        name="merge",
    )(*[in_vmem(one) for one in arrived])


def scatter_tiles(flat, value, first_tile, group, tiles):
    for n in range(value.shape[1] // LANES):
        flat[pl.ds(first_tile + n, group, stride=tiles), :] = value[:, n * LANES : (n + 1) * LANES]


def project_kernel(dims, *refs):
    group, head_local, latent, chunk = dims
    parts = refs[:SIDE]
    w_value, w_out, kept, passed, att_buf, flat = refs[SIDE:]
    rows = group * head_local
    pieces = latent // LANES
    tiles = w_out.shape[1] // LANES
    tail = pieces * rows
    lses = [read_lse(one[tail:, :], head_local) for one in parts]
    share, _ = combine_shares(lses, [list(range(SIDE))], rows, group, head_local)
    totals = [None] * pieces
    for s in range(SIDE):
        factor = jnp.broadcast_to(share[:, s : s + 1], (rows, LANES))
        for p in range(pieces):
            term = parts[s][p * rows : (p + 1) * rows, :].astype(jnp.float32) * factor
            totals[p] = term if s == 0 else totals[p] + term
    for p in range(pieces):
        att_buf[p] = totals[p]
    heads = []
    for j in range(head_local):
        attended = jnp.concatenate(
            [att_buf[p, pl.ds(j, group, stride=head_local), :] for p in range(pieces)], axis=1
        ).astype(jnp.bfloat16)
        heads.append(
            jnp.dot(attended, w_value[j], preferred_element_type=jnp.float32).astype(jnp.bfloat16)
        )
    per_head = jnp.concatenate(heads, axis=1)
    for c in range(w_out.shape[1] // chunk):
        value = jnp.dot(
            per_head, w_out[:, c * chunk : (c + 1) * chunk], preferred_element_type=jnp.float32
        )
        scatter_tiles(flat, value, c * chunk // LANES, group, tiles)
    core = lax.axis_index("tensor") % CORES
    for chip in range(SIDE * SIDE):
        pair = jnp.where(core == 0, chip, chip % SIDE * SIDE + chip // SIDE)
        for out, side in ((kept, core), (passed, 1 - core)):
            at = pl.multiple_of((pair * CORES + side) * tiles, 8)
            out[chip] = flat[pl.ds(at, tiles), :].astype(jnp.bfloat16)


def project(parts, w_value, w_out, group):
    head_local, latent, _ = w_value.shape
    features = w_out.shape[1]
    tiles = features // LANES
    dims = (group, head_local, latent, features // 7)
    return pl.pallas_call(
        functools.partial(project_kernel, dims),
        out_shape=(pltpu.VMEM((group // CORES, tiles, LANES), jnp.bfloat16),) * CORES,
        in_specs=[vmem_spec] * (SIDE + 2),
        out_specs=(vmem_spec,) * CORES,
        scratch_shapes=[
            pltpu.VMEM((latent // LANES, group * head_local, LANES), jnp.float32),
            pltpu.VMEM((group * tiles, LANES), jnp.float32),
        ],
        compiler_params=pltpu.CompilerParams(vmem_limit_bytes=12 * MIB),
        cost_estimate=moves(9000000),
        name="project",
    )(*[in_vmem(one) for one in parts], w_value, w_out)


def add_kernel(one, other, out):
    for s in range(out.shape[0]):
        out[s] = (one[s].astype(jnp.float32) + other[s].astype(jnp.float32)).astype(out.dtype)


def add(one, other):
    return pl.pallas_call(
        add_kernel,
        out_shape=pltpu.VMEM(one.shape, one.dtype),
        in_specs=[vmem_spec] * 2,
        out_specs=vmem_spec,
        compiler_params=pltpu.CompilerParams(vmem_limit_bytes=4 * MIB),
        cost_estimate=moves(700000),
        name="add",
    )(in_vmem(one), in_vmem(other))


def norm_kernel(got, residual, gain, kept, normed):
    total = residual[...]
    for s in range(got.shape[0]):
        total = total + got[s].astype(jnp.float32)
    kept[...] = total
    mean = jnp.sum(total * total) * (1.0 / total.size)
    value = (total * lax.rsqrt(mean + norm_eps) * gain[...]).astype(jnp.bfloat16)
    for s in range(normed.shape[0]):
        normed[s] = value


def norm(got, residual, gain):
    return pl.pallas_call(
        norm_kernel,
        out_shape=(pltpu.VMEM(residual.shape, jnp.float32), pltpu.VMEM(got.shape, got.dtype)),
        in_specs=[vmem_spec] * 3,
        out_specs=(vmem_spec, vmem_spec),
        compiler_params=pltpu.CompilerParams(vmem_limit_bytes=8 * MIB),
        cost_estimate=moves(700000),
        name="norm",
    )(in_vmem(got), in_vmem(residual), in_vmem(gain))


def ffn_kernel(chunk, *refs):
    normed, (w_gate, w_up, w_down) = refs[:CORES], refs[CORES : CORES + 3]
    outs, (flat, wide) = refs[CORES + 3 : 2 * CORES + 3], refs[2 * CORES + 3 :]
    half, tiles, _ = normed[0].shape
    group = CORES * half
    for c in range(CORES):
        for r in range(half):
            at = (c * half + r) * tiles
            flat[at : at + tiles, :] = normed[c][r].astype(jnp.float32)
    for n in range(tiles):
        wide[:, n * LANES : (n + 1) * LANES] = flat[pl.ds(n, group, stride=tiles), :].astype(
            jnp.bfloat16
        )
    gate = jnp.dot(wide[...], w_gate[...], preferred_element_type=jnp.float32)
    up = jnp.dot(wide[...], w_up[...], preferred_element_type=jnp.float32)
    activated = (gate / (1.0 + jnp.exp(-gate)) * up).astype(jnp.bfloat16)
    for c in range(w_down.shape[1] // chunk):
        value = jnp.dot(
            activated, w_down[:, c * chunk : (c + 1) * chunk], preferred_element_type=jnp.float32
        )
        scatter_tiles(flat, value, c * chunk // LANES, group, tiles)
    for c in range(CORES):
        for r in range(half):
            at = (c * half + r) * tiles
            outs[c][r] = flat[at : at + tiles, :].astype(jnp.bfloat16)


def ffn(normed, w_gate, w_up, w_down):
    half, tiles, _ = normed[0].shape
    group, features = CORES * half, tiles * LANES
    return pl.pallas_call(
        functools.partial(ffn_kernel, features // 7),
        out_shape=(pltpu.VMEM(normed[0].shape, jnp.bfloat16),) * CORES,
        in_specs=[vmem_spec] * (CORES + 3),
        out_specs=(vmem_spec,) * CORES,
        scratch_shapes=[
            pltpu.VMEM((group * tiles, LANES), jnp.float32),
            pltpu.VMEM((group, features), jnp.bfloat16),
        ],
        compiler_params=pltpu.CompilerParams(vmem_limit_bytes=12 * MIB),
        cost_estimate=moves(17000000),
        name="ffn",
    )(*[in_vmem(one) for one in normed], w_gate, w_up, w_down)


def body(
    queries,
    cache_pool,
    holder,
    slot_ids,
    lengths,
    residual,
    w_value,
    w_out,
    norm_gain,
    w_gate,
    w_up,
    w_down,
):
    ranks = lax.axis_size("dp")
    tensors = lax.axis_size("tensor")
    column = lax.axis_index("tensor")
    group = residual.shape[0]
    slots = cache_pool.shape[0]
    head_local, latent, _ = w_value.shape
    features = residual.shape[1]
    tiles = features // LANES
    requests = lengths.shape[0]
    swap = [(i, i ^ 1) for i in range(tensors)]
    from_next = [((i + 1) % ranks, i) for i in range(ranks)]
    from_prev = [((i - 1) % ranks, i) for i in range(ranks)]

    def swapped(value):
        return lax.ppermute(value, "tensor", swap)

    def along(value, first, distance):
        return lax.ppermute(value, "tensor", shifts(tensors, first, distance))

    own_queries = queries[0]
    other_queries = swapped(own_queries)
    q_pair = turn(own_queries, other_queries)
    following = lax.ppermute(cache_pool, "dp", from_next)
    previous = lax.ppermute(cache_pool, "dp", from_prev)
    q_line = join([q_pair] + [along(q_pair, True, d) for d in range(1, SIDE)])
    q_all = [q_line] + [along(q_line, False, e) for e in range(1, SIDE)]
    far_low = lax.ppermute(cut(following, 0), "dp", from_next)
    far_high = lax.ppermute(cut(previous, slots // 2), "dp", from_prev)
    mine = [following, far_low, far_high, previous]
    moved = [in_vmem(swapped(one)) for one in mine]
    mine = [in_vmem(one) for one in mine]
    pieces = [in_hbm(cache_pool)] + mine + [in_hbm(swapped(cache_pool))] + moved
    code = (holder * slots + slot_ids).reshape(1, requests)
    code_other = swapped(code)
    own_residual = (
        lax.dynamic_index_in_dim(residual, column, 0, keepdims=False)
        .astype(jnp.float32)
        .reshape(tiles, LANES)
    )
    gain = norm_gain.reshape(tiles, LANES)
    q_all, own_residual, gain = lax.optimization_barrier((q_all, own_residual, gain))
    w_value, w_gate, w_up, w_down = [
        in_vmem(one) for one in (w_value, w_gate, w_up, w_down)
    ]
    partial = attend(
        code,
        code_other,
        lengths.reshape(1, requests),
        q_all,
        pieces,
        ranks,
        latent,
        head_local,
    )
    w_out = fetch(w_out, partial[0])
    arrived = [partial[0]] + [along(partial[d], True, d) for d in range(1, SIDE)]
    merged = merge(arrived, group, head_local, latent)
    parts = [merged[0]] + [along(merged[e], False, e) for e in range(1, SIDE)]

    chips = SIDE * SIDE
    same_core = [[c + CORES * k for k in range(chips)] for c in range(CORES)]

    def exchange(value):
        return lax.all_to_all(
            value, "tensor", split_axis=0, concat_axis=0, tiled=True, axis_index_groups=same_core
        )

    def to_rows(kept, passed):
        return exchange(add(kept, swapped(passed)))

    residual_sum, normed = norm(
        to_rows(*project(parts, w_value, w_out, group)), own_residual, gain
    )
    rows = exchange(normed)
    down = to_rows(*ffn((rows, swapped(rows)), w_gate, w_up, w_down))
    return (residual_sum + jnp.sum(down.astype(jnp.float32), axis=0)).reshape(1, features)


def solution(mesh):
    in_specs = (
        P(("dp", "tensor"), None, None),
        P(("dp", "tensor"), None, None),
        P(None, "tensor"),
        P(None, "tensor"),
        P(),
        P("dp", None),
        P("tensor", None, None),
        P("tensor", None),
        P(),
        P(None, "tensor"),
        P(None, "tensor"),
        P("tensor", None),
    )
    out_specs = P(("dp", "tensor"), None)
    return jax.shard_map(body, mesh=mesh, in_specs=in_specs, out_specs=out_specs, check_vma=False)
```

```python
import functools

import jax
import jax.numpy as jnp
from jax import lax
from jax.experimental import pallas as pl
from jax.experimental.pallas import tpu as pltpu
from jax.sharding import PartitionSpec as P

score_scale = 192.0 ** (-0.5)
norm_eps = 1e-06
far_below = -1e30
CORES = 2
LANES = 128
HEAD_LOCAL = 4
SIDE = 4
MIB = 1024 * 1024
hbm_spec = pl.BlockSpec(memory_space=pl.ANY)
vmem_spec = pl.BlockSpec(memory_space=pltpu.VMEM)
smem_spec = pl.BlockSpec(memory_space=pltpu.SMEM)


def in_vmem(value):
    return pltpu.with_memory_space_constraint(value, pltpu.VMEM)


def moves(size):
    return pl.CostEstimate(flops=0, bytes_accessed=size, transcendentals=0)


def in_hbm(value):
    return pltpu.with_memory_space_constraint(value, pltpu.HBM)


def cut_kernel(first, blocks, out, sem):
    copy = pltpu.make_async_copy(blocks.at[pl.ds(first, out.shape[0])], out, sem)
    copy.start()
    copy.wait()


def cut(blocks, first):
    half = (blocks.shape[0] // 2,) + blocks.shape[1:]
    return pl.pallas_call(
        functools.partial(cut_kernel, first),
        out_shape=pltpu.VMEM(half, blocks.dtype),
        in_specs=[hbm_spec],
        out_specs=vmem_spec,
        scratch_shapes=[pltpu.SemaphoreType.DMA],
        compiler_params=pltpu.CompilerParams(vmem_limit_bytes=4 * MIB),
        cost_estimate=moves(1200000),
        name="cut",
    )(blocks)


def fetch_kernel(weight, _, out, sem):
    copy = pltpu.make_async_copy(weight, out, sem)
    copy.start()
    copy.wait()


def fetch(weight, after):
    return pl.pallas_call(
        fetch_kernel,
        out_shape=pltpu.VMEM(weight.shape, weight.dtype),
        in_specs=[hbm_spec, vmem_spec],
        out_specs=vmem_spec,
        scratch_shapes=[pltpu.SemaphoreType.DMA],
        compiler_params=pltpu.CompilerParams(vmem_limit_bytes=4 * MIB),
        cost_estimate=moves(2 * weight.size * weight.dtype.itemsize),
        name="fetch",
    )(in_hbm(weight), in_vmem(after))


def turn_kernel(own, other, out):
    width, head_total = own.shape
    heads = head_total // CORES
    head_local, tail = HEAD_LOCAL, width // LANES * LANES
    core = lax.axis_index("tensor") % CORES
    row = lax.broadcasted_iota(jnp.int32, (heads, head_total), 0)
    wanted = (row // head_local) * (CORES * head_local) + core * head_local + row % head_local
    hit = lax.broadcasted_iota(jnp.int32, (heads, head_total), 1) == wanted
    select = jnp.where(hit, 1.0, 0.0).astype(jnp.bfloat16)
    turned = [
        lax.dot_general(select, one[...], (((1,), (1,)), ((), ())), preferred_element_type=jnp.float32)
        for one in (own, other)
    ]
    pair = [
        jnp.where(core == 0, turned[0], turned[1]).astype(jnp.bfloat16),
        jnp.where(core == 0, turned[1], turned[0]).astype(jnp.bfloat16),
    ]
    rows = [
        pair[i][:, p * LANES : (p + 1) * LANES] for p in range(tail // LANES) for i in range(CORES)
    ]
    out[0] = jnp.concatenate(
        rows + [jnp.concatenate([one[:, tail:] for one in pair], axis=1)], axis=0
    )


def turn(own, other):
    return pl.pallas_call(
        turn_kernel,
        out_shape=jax.ShapeDtypeStruct((1,) + own.shape, own.dtype),
        in_specs=[vmem_spec] * 2,
        out_specs=vmem_spec,
        compiler_params=pltpu.CompilerParams(vmem_limit_bytes=4 * MIB),
        cost_estimate=moves(450000),
        name="turn",
    )(own, other)


def join_kernel(*refs):
    count = len(refs) - 2
    out, sems = refs[count:]
    copies = [
        pltpu.make_async_copy(one, out.at[pl.ds(i, 1)], sems.at[i])
        for i, one in enumerate(refs[:count])
    ]
    for one in copies:
        one.start()
    for one in copies:
        one.wait()


def join(pieces):
    count = len(pieces)
    return pl.pallas_call(
        join_kernel,
        out_shape=jax.ShapeDtypeStruct((count,) + pieces[0].shape[1:], pieces[0].dtype),
        in_specs=[hbm_spec] * count,
        out_specs=hbm_spec,
        scratch_shapes=[pltpu.SemaphoreType.DMA((count,))],
        compiler_params=pltpu.CompilerParams(vmem_limit_bytes=4 * MIB),
        cost_estimate=moves(1200000),
        name="join",
    )(*pieces)


def by_core(core, chip):
    x, y = chip % SIDE, chip // SIDE
    return jnp.where(core == 0, x, y), jnp.where(core == 0, y, x)


def shifts(tensors, first, distance):
    pairs = []
    for i in range(tensors):
        core, chip = i % CORES, i // CORES
        x, y = chip % SIDE, chip // SIDE
        if (core == 0) == first:
            x = (x + distance) % SIDE
        else:
            y = (y + distance) % SIDE
        pairs.append((i, (y * SIDE + x) * CORES + core))
    return pairs


def attend_kernel(dims, code_own, code_other, lengths, *refs):
    slots, ranks, head_local, latent, count = dims
    q_refs, pieces = refs[:SIDE], refs[SIDE : SIDE + count]
    outs = refs[SIDE + count : 2 * SIDE + count]
    kbuf, qbuf, obuf, lse_buf, sems = refs[2 * SIDE + count :]
    group = CORES * SIDE * SIDE
    heads = lse_buf.shape[0]
    block_len = kbuf.shape[2]
    owners = heads // head_local
    my_rank = lax.axis_index("dp")
    column = lax.axis_index("tensor")
    core = column % CORES
    own_first, own_second = by_core(core, column // CORES)
    first = my_rank * group
    q_copies = [
        pltpu.make_async_copy(one, qbuf.at[pl.ds(e * SIDE, SIDE)], sems.at[count + e])
        for e, one in enumerate(q_refs)
    ]
    copies, at = [], 0
    for i, one in enumerate(pieces):
        copies.append(pltpu.make_async_copy(one, kbuf.at[pl.ds(at, one.shape[0])], sems.at[i]))
        at += one.shape[0]
    for one in copies[:1] + copies[count // 2 : count // 2 + 1] + q_copies[:1]:
        one.start()
    for one in copies[1 : count // 2] + copies[count // 2 + 1 :] + q_copies[1:]:
        one.start()
    token = lax.broadcasted_iota(jnp.int32, (1, 2 * block_len), 1)
    partner = column + 1 - 2 * core
    position = jnp.where(
        token < block_len, token + column * block_len, token - block_len + partner * block_len
    )
    lane = lax.broadcasted_iota(jnp.int32, (heads, LANES), 1)
    lse_buf[...] = jnp.zeros_like(lse_buf)
    spots = []
    for k in range(owners):
        k_first, k_second = by_core(core, k)
        spots.append(
            (k_first - own_first + SIDE) % SIDE * SIDE + (k_second - own_second + SIDE) % SIDE
        )
    for one in copies:
        one.wait()

    def place(codes, r):
        code = codes[0, first + r]
        return ((code // slots - my_rank + ranks) % ranks) * slots + code % slots

    unroll = CORES * SIDE

    def several(e, carry):
        for i, one in enumerate(q_copies):
            pl.when(e == i)(one.wait)
        second = (own_second - e + SIDE) % SIDE
        rs, asked = [], []
        for i in range(SIDE):
            chip = jnp.where(core == 0, second * SIDE + i, i * SIDE + second)
            at = e * SIDE + (own_first - i + SIDE) % SIDE
            for side in range(CORES):
                rs.append(chip * CORES + side)
                rotary = qbuf[at, latent:, :]
                mine = (lane < LANES // CORES) if side == 0 else (lane >= LANES // CORES)
                rows = [
                    qbuf[at, (p * CORES + side) * heads : (p * CORES + side + 1) * heads, :]
                    for p in range(latent // LANES)
                ]
                asked.append(
                    jnp.concatenate(
                        rows + [jnp.where(mine, rotary, jnp.zeros_like(rotary))], axis=1
                    )
                )
        keys = [
            jnp.concatenate(
                [kbuf[place(code_own, r)], kbuf[ranks * slots + place(code_other, r)]], axis=1
            )
            for r in rs
        ]
        scores = [
            jnp.dot(
                q,
                jnp.concatenate([key, key[latent:]], axis=0),
                preferred_element_type=jnp.float32,
            )
            * score_scale
            for q, key in zip(asked, keys)
        ]
        weights, scales, lses = [], [], []
        for r, score in zip(rs, scores):
            live = position < lengths[0, first + r]
            masked = jnp.where(live, score, far_below)
            top = jnp.max(masked, axis=1, keepdims=True)
            weight = jnp.where(live, jnp.exp(masked - top), 0.0)
            total = jnp.sum(weight, axis=1, keepdims=True)
            some = total > 0.0
            safe = jnp.where(some, total, 1.0)
            weights.append(weight.astype(jnp.bfloat16))
            scales.append(jnp.where(some, 1.0 / safe, 0.0))
            lses.append(jnp.where(some, top + jnp.log(safe), far_below))
        mixed = [
            lax.dot_general(
                weight, key[:latent], (((1,), (1,)), ((), ())), preferred_element_type=jnp.float32
            )
            * scale
            for weight, key, scale in zip(weights, keys, scales)
        ]
        lse_all = lse_buf[...]
        for i, lse in enumerate(lses):
            lse_all = jnp.where(lane == second * unroll + i, lse, lse_all)
        lse_buf[...] = lse_all
        rows_count = unroll * head_local
        for k in range(owners):
            both = jnp.concatenate(
                [one[k * head_local : (k + 1) * head_local] for one in mixed], axis=0
            ).astype(jnp.bfloat16)
            for p in range(latent // LANES):
                rows_at = pl.multiple_of(p * group * head_local + second * rows_count, rows_count)
                obuf[spots[k], pl.ds(rows_at, rows_count), :] = both[:, p * LANES : (p + 1) * LANES]
        return carry

    lax.fori_loop(0, SIDE, several, 0)
    tail = latent // LANES * group * head_local
    parts = lse_parts(lse_buf[...])
    for k in range(owners):
        own = slice(k * head_local, (k + 1) * head_local)
        obuf[spots[k], tail:, :] = jnp.concatenate(
            [one[own] for one in parts] + [jnp.zeros_like(parts[0][own])], axis=0
        ).astype(jnp.bfloat16)
    copies = [
        pltpu.make_async_copy(obuf.at[pl.ds(d * SIDE, SIDE)], outs[d], sems.at[d])
        for d in range(SIDE)
    ]
    for one in copies:
        one.start()
    for one in copies:
        one.wait()


def lse_parts(value):
    high = value.astype(jnp.bfloat16).astype(jnp.float32)
    mid = (value - high).astype(jnp.bfloat16).astype(jnp.float32)
    return [high, mid, value - high - mid]


def attend(code_own, code_other, lengths, q_all, pieces, ranks, latent, head_local):
    per, _, head_total = q_all[0].shape
    width, block_len = pieces[0].shape[1:]
    heads = head_total // CORES
    blocks = sum(one.shape[0] for one in pieces)
    chips = SIDE * SIDE
    out_rows = latent // LANES * chips * CORES * head_local + 16
    count = len(pieces)
    dims = (blocks // ranks // CORES, ranks, head_local, latent, count)
    return pl.pallas_call(
        functools.partial(attend_kernel, dims),
        out_shape=(pltpu.VMEM((SIDE, out_rows, LANES), jnp.bfloat16),) * SIDE,
        in_specs=[smem_spec] * 3 + [hbm_spec] * (SIDE + count),
        out_specs=(vmem_spec,) * SIDE,
        scratch_shapes=[
            pltpu.VMEM((blocks, width, block_len), jnp.bfloat16),
            pltpu.VMEM((chips, width, head_total), jnp.bfloat16),
            pltpu.VMEM((chips, out_rows, LANES), jnp.bfloat16),
            pltpu.VMEM((heads, LANES), jnp.float32),
            pltpu.SemaphoreType.DMA((count + SIDE,)),
        ],
        compiler_params=pltpu.CompilerParams(vmem_limit_bytes=22 * MIB),
        cost_estimate=moves(20000000),
        name="attend",
    )(code_own, code_other, lengths, *[in_hbm(one) for one in q_all], *pieces)


def combine_shares(lses, sets, rows, group, head_local):
    merged, scaled = [], [None] * len(lses)
    for one_set in sets:
        peak = functools.reduce(jnp.maximum, [lses[s] for s in one_set])
        shares = [jnp.exp(lses[s] - peak) for s in one_set]
        total = functools.reduce(jnp.add, shares)
        merged.append(peak + jnp.log(total))
        inverse = 1.0 / total
        for s, share in zip(one_set, shares):
            scaled[s] = share * inverse
    share_all = jnp.concatenate(scaled, axis=0)
    count = len(lses) * head_local
    pick_request = jnp.where(
        lax.broadcasted_iota(jnp.int32, (rows, LANES), 0) // head_local
        == lax.broadcasted_iota(jnp.int32, (rows, LANES), 1),
        1.0,
        0.0,
    )
    valid = lax.broadcasted_iota(jnp.int32, (count, LANES), 1) < group
    spread = lax.dot_general(
        pick_request,
        jnp.where(valid, share_all, 0.0),
        (((1,), (1,)), ((), ())),
        precision=lax.Precision.HIGHEST,
        preferred_element_type=jnp.float32,
    )
    own_head = (
        lax.broadcasted_iota(jnp.int32, (rows, count), 0) % head_local
        == lax.broadcasted_iota(jnp.int32, (rows, count), 1) % head_local
    )
    pick_source = jnp.where(
        lax.broadcasted_iota(jnp.int32, (count, LANES), 0) // head_local
        == lax.broadcasted_iota(jnp.int32, (count, LANES), 1),
        1.0,
        0.0,
    )
    share = jnp.dot(
        jnp.where(own_head, spread, 0.0),
        pick_source,
        precision=lax.Precision.HIGHEST,
        preferred_element_type=jnp.float32,
    )
    return share, merged


def read_lse(tile, head_local):
    three = tile.astype(jnp.float32)
    return functools.reduce(
        jnp.add, [three[i * head_local : (i + 1) * head_local] for i in range(3)]
    )


def merge_kernel(dims, *refs):
    group, head_local, latent = dims
    ins, outs = refs[:SIDE], refs[SIDE + 1 :]
    rows = group * head_local
    pieces = latent // LANES
    tail = pieces * rows
    lses = [read_lse(one[e, tail:, :], head_local) for e in range(SIDE) for one in ins]
    sets = [[e * SIDE + s for s in range(SIDE)] for e in range(SIDE)]
    share, merged = combine_shares(lses, sets, rows, group, head_local)
    for e in range(SIDE):
        totals = [None] * pieces
        for s in range(SIDE):
            at = e * SIDE + s
            factor = jnp.broadcast_to(share[:, at : at + 1], (rows, LANES))
            for p in range(pieces):
                term = ins[s][e, p * rows : (p + 1) * rows, :].astype(jnp.float32) * factor
                totals[p] = term if s == 0 else totals[p] + term
        for p in range(pieces):
            outs[e][p * rows : (p + 1) * rows, :] = totals[p].astype(jnp.bfloat16)
        parts = lse_parts(merged[e])
        outs[e][tail:, :] = jnp.concatenate(parts + [jnp.zeros_like(parts[0])], axis=0).astype(
            jnp.bfloat16
        )


def merge(arrived, after, group, head_local, latent):
    shape = arrived[0].shape[1:]
    return pl.pallas_call(
        functools.partial(merge_kernel, (group, head_local, latent)),
        out_shape=(pltpu.VMEM(shape, jnp.bfloat16),) * SIDE,
        in_specs=[vmem_spec] * (SIDE + 1),
        out_specs=(vmem_spec,) * SIDE,
        compiler_params=pltpu.CompilerParams(vmem_limit_bytes=8 * MIB),
        cost_estimate=moves(4500000),
        name="merge",
    )(*[in_vmem(one) for one in arrived], after)


def scatter_tiles(flat, value, first_tile, group, tiles):
    for n in range(value.shape[1] // LANES):
        flat[pl.ds(first_tile + n, group, stride=tiles), :] = value[:, n * LANES : (n + 1) * LANES]


def project_kernel(dims, *refs):
    group, head_local, latent, chunk = dims
    parts = refs[:SIDE]
    w_value, w_out, kept, passed, att_buf, flat = refs[SIDE:]
    rows = group * head_local
    pieces = latent // LANES
    tiles = w_out.shape[1] // LANES
    tail = pieces * rows
    lses = [read_lse(one[tail:, :], head_local) for one in parts]
    share, _ = combine_shares(lses, [list(range(SIDE))], rows, group, head_local)
    totals = [None] * pieces
    for s in range(SIDE):
        factor = jnp.broadcast_to(share[:, s : s + 1], (rows, LANES))
        for p in range(pieces):
            term = parts[s][p * rows : (p + 1) * rows, :].astype(jnp.float32) * factor
            totals[p] = term if s == 0 else totals[p] + term
    for p in range(pieces):
        att_buf[p] = totals[p]
    heads = []
    for j in range(head_local):
        attended = jnp.concatenate(
            [att_buf[p, pl.ds(j, group, stride=head_local), :] for p in range(pieces)], axis=1
        ).astype(jnp.bfloat16)
        heads.append(
            jnp.dot(attended, w_value[j], preferred_element_type=jnp.float32).astype(jnp.bfloat16)
        )
    per_head = jnp.concatenate(heads, axis=1)
    for c in range(w_out.shape[1] // chunk):
        value = jnp.dot(
            per_head, w_out[:, c * chunk : (c + 1) * chunk], preferred_element_type=jnp.float32
        )
        scatter_tiles(flat, value, c * chunk // LANES, group, tiles)
    core = lax.axis_index("tensor") % CORES
    for chip in range(SIDE * SIDE):
        pair = jnp.where(core == 0, chip, chip % SIDE * SIDE + chip // SIDE)
        for out, side in ((kept, core), (passed, 1 - core)):
            at = pl.multiple_of((pair * CORES + side) * tiles, 8)
            out[chip] = flat[pl.ds(at, tiles), :].astype(jnp.bfloat16)


def project(parts, w_value, w_out, group):
    head_local, latent, _ = w_value.shape
    features = w_out.shape[1]
    tiles = features // LANES
    dims = (group, head_local, latent, features // 7)
    return pl.pallas_call(
        functools.partial(project_kernel, dims),
        out_shape=(pltpu.VMEM((group // CORES, tiles, LANES), jnp.bfloat16),) * CORES,
        in_specs=[vmem_spec] * (SIDE + 2),
        out_specs=(vmem_spec,) * CORES,
        scratch_shapes=[
            pltpu.VMEM((latent // LANES, group * head_local, LANES), jnp.float32),
            pltpu.VMEM((group * tiles, LANES), jnp.float32),
        ],
        compiler_params=pltpu.CompilerParams(vmem_limit_bytes=12 * MIB),
        cost_estimate=moves(9000000),
        name="project",
    )(*[in_vmem(one) for one in parts], w_value, w_out)


def add_kernel(one, other, out):
    for s in range(out.shape[0]):
        out[s] = (one[s].astype(jnp.float32) + other[s].astype(jnp.float32)).astype(out.dtype)


def add(one, other):
    return pl.pallas_call(
        add_kernel,
        out_shape=pltpu.VMEM(one.shape, one.dtype),
        in_specs=[vmem_spec] * 2,
        out_specs=vmem_spec,
        compiler_params=pltpu.CompilerParams(vmem_limit_bytes=4 * MIB),
        cost_estimate=moves(700000),
        name="add",
    )(in_vmem(one), in_vmem(other))


def norm_kernel(got, residual, gain, kept, normed):
    total = residual[...]
    for s in range(got.shape[0]):
        total = total + got[s].astype(jnp.float32)
    kept[...] = total
    mean = jnp.sum(total * total) * (1.0 / total.size)
    value = (total * lax.rsqrt(mean + norm_eps) * gain[...]).astype(jnp.bfloat16)
    for s in range(normed.shape[0]):
        normed[s] = value


def norm(got, residual, gain):
    return pl.pallas_call(
        norm_kernel,
        out_shape=(pltpu.VMEM(residual.shape, jnp.float32), pltpu.VMEM(got.shape, got.dtype)),
        in_specs=[vmem_spec] * 3,
        out_specs=(vmem_spec, vmem_spec),
        compiler_params=pltpu.CompilerParams(vmem_limit_bytes=8 * MIB),
        cost_estimate=moves(700000),
        name="norm",
    )(in_vmem(got), in_vmem(residual), in_vmem(gain))


def ffn_kernel(chunk, *refs):
    normed, (w_gate, w_up, w_down) = refs[:CORES], refs[CORES : CORES + 3]
    outs, (flat, wide) = refs[CORES + 3 : 2 * CORES + 3], refs[2 * CORES + 3 :]
    half, tiles, _ = normed[0].shape
    group = CORES * half
    for c in range(CORES):
        for r in range(half):
            at = (c * half + r) * tiles
            flat[at : at + tiles, :] = normed[c][r].astype(jnp.float32)
    for n in range(tiles):
        wide[:, n * LANES : (n + 1) * LANES] = flat[pl.ds(n, group, stride=tiles), :].astype(
            jnp.bfloat16
        )
    gate = jnp.dot(wide[...], w_gate[...], preferred_element_type=jnp.float32)
    up = jnp.dot(wide[...], w_up[...], preferred_element_type=jnp.float32)
    activated = (gate / (1.0 + jnp.exp(-gate)) * up).astype(jnp.bfloat16)
    for c in range(w_down.shape[1] // chunk):
        value = jnp.dot(
            activated, w_down[:, c * chunk : (c + 1) * chunk], preferred_element_type=jnp.float32
        )
        scatter_tiles(flat, value, c * chunk // LANES, group, tiles)
    for c in range(CORES):
        for r in range(half):
            at = (c * half + r) * tiles
            outs[c][r] = flat[at : at + tiles, :].astype(jnp.bfloat16)


def ffn(normed, w_gate, w_up, w_down):
    half, tiles, _ = normed[0].shape
    group, features = CORES * half, tiles * LANES
    return pl.pallas_call(
        functools.partial(ffn_kernel, features // 7),
        out_shape=(pltpu.VMEM(normed[0].shape, jnp.bfloat16),) * CORES,
        in_specs=[vmem_spec] * (CORES + 3),
        out_specs=(vmem_spec,) * CORES,
        scratch_shapes=[
            pltpu.VMEM((group * tiles, LANES), jnp.float32),
            pltpu.VMEM((group, features), jnp.bfloat16),
        ],
        compiler_params=pltpu.CompilerParams(vmem_limit_bytes=12 * MIB),
        cost_estimate=moves(17000000),
        name="ffn",
    )(*[in_vmem(one) for one in normed], w_gate, w_up, w_down)


def body(
    queries,
    cache_pool,
    holder,
    slot_ids,
    lengths,
    residual,
    w_value,
    w_out,
    norm_gain,
    w_gate,
    w_up,
    w_down,
):
    ranks = lax.axis_size("dp")
    tensors = lax.axis_size("tensor")
    column = lax.axis_index("tensor")
    group = residual.shape[0]
    slots = cache_pool.shape[0]
    head_local, latent, _ = w_value.shape
    features = residual.shape[1]
    tiles = features // LANES
    requests = lengths.shape[0]
    swap = [(i, i ^ 1) for i in range(tensors)]
    from_next = [((i + 1) % ranks, i) for i in range(ranks)]
    from_prev = [((i - 1) % ranks, i) for i in range(ranks)]

    def swapped(value):
        return lax.ppermute(value, "tensor", swap)

    def along(value, first, distance):
        return lax.ppermute(value, "tensor", shifts(tensors, first, distance))

    own_queries = queries[0]
    other_queries = swapped(own_queries)
    q_pair = turn(own_queries, other_queries)
    following = lax.ppermute(cache_pool, "dp", from_next)
    previous = lax.ppermute(cache_pool, "dp", from_prev)
    q_line = join([q_pair] + [along(q_pair, True, d) for d in range(1, SIDE)])
    q_all = [q_line] + [along(q_line, False, e) for e in range(1, SIDE)]
    far_low = lax.ppermute(cut(following, 0), "dp", from_next)
    far_high = lax.ppermute(cut(previous, slots // 2), "dp", from_prev)
    mine = [following, far_low, far_high, previous]
    moved = [in_vmem(swapped(one)) for one in mine]
    mine = [in_vmem(one) for one in mine]
    pieces = [in_hbm(cache_pool)] + mine + [in_hbm(swapped(cache_pool))] + moved
    code = (holder * slots + slot_ids).reshape(1, requests)
    code_other = swapped(code)
    own_residual = (
        lax.dynamic_index_in_dim(residual, column, 0, keepdims=False)
        .astype(jnp.float32)
        .reshape(tiles, LANES)
    )
    gain = norm_gain.reshape(tiles, LANES)
    q_all, own_residual, gain = lax.optimization_barrier((q_all, own_residual, gain))
    w_value, w_gate, w_up, w_down = [
        in_vmem(one) for one in (w_value, w_gate, w_up, w_down)
    ]
    partial = attend(
        code,
        code_other,
        lengths.reshape(1, requests),
        q_all,
        pieces,
        ranks,
        latent,
        head_local,
    )
    w_out = fetch(w_out, partial[0])
    opposite = along(partial[2], True, 2)
    one_on, one_back = along(partial[1], True, 1), along(partial[3], True, 3)
    arrived = [partial[0], opposite, one_on, one_back]
    merged = merge(arrived, w_out, group, head_local, latent)
    opposite = along(merged[2], False, 2)
    parts = [merged[0], opposite, along(merged[1], False, 1), along(merged[3], False, 3)]

    chips = SIDE * SIDE
    same_core = [[c + CORES * k for k in range(chips)] for c in range(CORES)]

    def exchange(value):
        return lax.all_to_all(
            value, "tensor", split_axis=0, concat_axis=0, tiled=True, axis_index_groups=same_core
        )

    def to_rows(kept, passed):
        return exchange(add(kept, swapped(passed)))

    residual_sum, normed = norm(
        to_rows(*project(parts, w_value, w_out, group)), own_residual, gain
    )
    rows = exchange(normed)
    down = to_rows(*ffn((rows, swapped(rows)), w_gate, w_up, w_down))
    return (residual_sum + jnp.sum(down.astype(jnp.float32), axis=0)).reshape(1, features)


def solution(mesh):
    in_specs = (
        P(("dp", "tensor"), None, None),
        P(("dp", "tensor"), None, None),
        P(None, "tensor"),
        P(None, "tensor"),
        P(),
        P("dp", None),
        P("tensor", None, None),
        P("tensor", None),
        P(),
        P(None, "tensor"),
        P(None, "tensor"),
        P("tensor", None),
    )
    out_specs = P(("dp", "tensor"), None)
    return jax.shard_map(body, mesh=mesh, in_specs=in_specs, out_specs=out_specs, check_vma=False)
```

```python
import functools

import jax
import jax.numpy as jnp
from jax import lax
from jax.experimental import pallas as pl
from jax.experimental.pallas import tpu as pltpu
from jax.sharding import PartitionSpec as P

score_scale = 192.0 ** (-0.5)
norm_eps = 1e-06
far_below = -1e30
CORES = 2
LANES = 128
HEAD_LOCAL = 4
SIDE = 4
MIB = 1024 * 1024
hbm_spec = pl.BlockSpec(memory_space=pl.ANY)
vmem_spec = pl.BlockSpec(memory_space=pltpu.VMEM)
smem_spec = pl.BlockSpec(memory_space=pltpu.SMEM)


def in_vmem(value):
    return pltpu.with_memory_space_constraint(value, pltpu.VMEM)


def moves(size):
    return pl.CostEstimate(flops=0, bytes_accessed=size, transcendentals=0)


def in_hbm(value):
    return pltpu.with_memory_space_constraint(value, pltpu.HBM)


def cut_kernel(first, blocks, out, sem):
    copy = pltpu.make_async_copy(blocks.at[pl.ds(first, out.shape[0])], out, sem)
    copy.start()
    copy.wait()


def cut(blocks, first):
    half = (blocks.shape[0] // 2,) + blocks.shape[1:]
    return pl.pallas_call(
        functools.partial(cut_kernel, first),
        out_shape=pltpu.VMEM(half, blocks.dtype),
        in_specs=[hbm_spec],
        out_specs=vmem_spec,
        scratch_shapes=[pltpu.SemaphoreType.DMA],
        compiler_params=pltpu.CompilerParams(vmem_limit_bytes=4 * MIB),
        cost_estimate=moves(1200000),
        name="cut",
    )(blocks)


def fetch_kernel(weight, _, out, sem):
    copy = pltpu.make_async_copy(weight, out, sem)
    copy.start()
    copy.wait()


def fetch(weight, after):
    return pl.pallas_call(
        fetch_kernel,
        out_shape=pltpu.VMEM(weight.shape, weight.dtype),
        in_specs=[hbm_spec, vmem_spec],
        out_specs=vmem_spec,
        scratch_shapes=[pltpu.SemaphoreType.DMA],
        compiler_params=pltpu.CompilerParams(vmem_limit_bytes=4 * MIB),
        cost_estimate=moves(2 * weight.size * weight.dtype.itemsize),
        name="fetch",
    )(in_hbm(weight), in_vmem(after))


def turn_kernel(own, other, out):
    width, head_total = own.shape
    heads = head_total // CORES
    head_local, tail = HEAD_LOCAL, width // LANES * LANES
    core = lax.axis_index("tensor") % CORES
    row = lax.broadcasted_iota(jnp.int32, (heads, head_total), 0)
    wanted = (row // head_local) * (CORES * head_local) + core * head_local + row % head_local
    hit = lax.broadcasted_iota(jnp.int32, (heads, head_total), 1) == wanted
    select = jnp.where(hit, 1.0, 0.0).astype(jnp.bfloat16)
    turned = [
        lax.dot_general(select, one[...], (((1,), (1,)), ((), ())), preferred_element_type=jnp.float32)
        for one in (own, other)
    ]
    pair = [
        jnp.where(core == 0, turned[0], turned[1]).astype(jnp.bfloat16),
        jnp.where(core == 0, turned[1], turned[0]).astype(jnp.bfloat16),
    ]
    rows = [
        pair[i][:, p * LANES : (p + 1) * LANES] for p in range(tail // LANES) for i in range(CORES)
    ]
    out[0] = jnp.concatenate(
        rows + [jnp.concatenate([one[:, tail:] for one in pair], axis=1)], axis=0
    )


def turn(own, other):
    return pl.pallas_call(
        turn_kernel,
        out_shape=jax.ShapeDtypeStruct((1,) + own.shape, own.dtype),
        in_specs=[vmem_spec] * 2,
        out_specs=vmem_spec,
        compiler_params=pltpu.CompilerParams(vmem_limit_bytes=4 * MIB),
        cost_estimate=moves(450000),
        name="turn",
    )(own, other)


def join_kernel(*refs):
    count = len(refs) - 2
    out, sems = refs[count:]
    copies = [
        pltpu.make_async_copy(one, out.at[pl.ds(i, 1)], sems.at[i])
        for i, one in enumerate(refs[:count])
    ]
    for one in copies:
        one.start()
    for one in copies:
        one.wait()


def join(pieces):
    count = len(pieces)
    return pl.pallas_call(
        join_kernel,
        out_shape=jax.ShapeDtypeStruct((count,) + pieces[0].shape[1:], pieces[0].dtype),
        in_specs=[hbm_spec] * count,
        out_specs=hbm_spec,
        scratch_shapes=[pltpu.SemaphoreType.DMA((count,))],
        compiler_params=pltpu.CompilerParams(vmem_limit_bytes=4 * MIB),
        cost_estimate=moves(1200000),
        name="join",
    )(*pieces)


def by_core(core, chip):
    x, y = chip % SIDE, chip // SIDE
    return jnp.where(core == 0, x, y), jnp.where(core == 0, y, x)


def shifts(tensors, first, distance):
    pairs = []
    for i in range(tensors):
        core, chip = i % CORES, i // CORES
        x, y = chip % SIDE, chip // SIDE
        if (core == 0) == first:
            x = (x + distance) % SIDE
        else:
            y = (y + distance) % SIDE
        pairs.append((i, (y * SIDE + x) * CORES + core))
    return pairs


def attend_kernel(dims, code_own, code_other, lengths, *refs):
    slots, ranks, head_local, latent, count = dims
    q_refs, pieces = refs[:SIDE], refs[SIDE : SIDE + count]
    outs = refs[SIDE + count : 2 * SIDE + count]
    kbuf, qbuf, obuf, lse_buf, sems = refs[2 * SIDE + count :]
    group = CORES * SIDE * SIDE
    heads = lse_buf.shape[0]
    block_len = kbuf.shape[2]
    owners = heads // head_local
    my_rank = lax.axis_index("dp")
    column = lax.axis_index("tensor")
    core = column % CORES
    own_first, own_second = by_core(core, column // CORES)
    first = my_rank * group
    q_copies = [
        pltpu.make_async_copy(one, qbuf.at[pl.ds(e * SIDE, SIDE)], sems.at[count + e])
        for e, one in enumerate(q_refs)
    ]
    copies, at = [], 0
    for i, one in enumerate(pieces):
        copies.append(pltpu.make_async_copy(one, kbuf.at[pl.ds(at, one.shape[0])], sems.at[i]))
        at += one.shape[0]
    for one in copies[:1] + copies[count // 2 : count // 2 + 1] + q_copies[:1]:
        one.start()
    for one in copies[1 : count // 2] + copies[count // 2 + 1 :] + q_copies[1:]:
        one.start()
    token = lax.broadcasted_iota(jnp.int32, (1, 2 * block_len), 1)
    partner = column + 1 - 2 * core
    position = jnp.where(
        token < block_len, token + column * block_len, token - block_len + partner * block_len
    )
    lane = lax.broadcasted_iota(jnp.int32, (heads, LANES), 1)
    lse_buf[...] = jnp.zeros_like(lse_buf)
    spots = []
    for k in range(owners):
        k_first, k_second = by_core(core, k)
        spots.append(
            (k_first - own_first + SIDE) % SIDE * SIDE + (k_second - own_second + SIDE) % SIDE
        )
    for one in copies:
        one.wait()

    def place(codes, r):
        code = codes[0, first + r]
        return ((code // slots - my_rank + ranks) % ranks) * slots + code % slots

    unroll = CORES * SIDE

    def several(e, carry):
        for i, one in enumerate(q_copies):
            pl.when(e == i)(one.wait)
        second = (own_second - e + SIDE) % SIDE
        rs, asked = [], []
        for i in range(SIDE):
            chip = jnp.where(core == 0, second * SIDE + i, i * SIDE + second)
            at = e * SIDE + (own_first - i + SIDE) % SIDE
            for side in range(CORES):
                rs.append(chip * CORES + side)
                rotary = qbuf[at, latent:, :]
                mine = (lane < LANES // CORES) if side == 0 else (lane >= LANES // CORES)
                rows = [
                    qbuf[at, (p * CORES + side) * heads : (p * CORES + side + 1) * heads, :]
                    for p in range(latent // LANES)
                ]
                asked.append(
                    jnp.concatenate(
                        rows + [jnp.where(mine, rotary, jnp.zeros_like(rotary))], axis=1
                    )
                )
        keys = [
            jnp.concatenate(
                [kbuf[place(code_own, r)], kbuf[ranks * slots + place(code_other, r)]], axis=1
            )
            for r in rs
        ]
        scores = [
            jnp.dot(
                q,
                jnp.concatenate([key, key[latent:]], axis=0),
                preferred_element_type=jnp.float32,
            )
            * score_scale
            for q, key in zip(asked, keys)
        ]
        weights, scales, lses = [], [], []
        for r, score in zip(rs, scores):
            live = position < lengths[0, first + r]
            masked = jnp.where(live, score, far_below)
            top = jnp.max(masked, axis=1, keepdims=True)
            weight = jnp.where(live, jnp.exp(masked - top), 0.0)
            total = jnp.sum(weight, axis=1, keepdims=True)
            some = total > 0.0
            safe = jnp.where(some, total, 1.0)
            weights.append(weight.astype(jnp.bfloat16))
            scales.append(jnp.where(some, 1.0 / safe, 0.0))
            lses.append(jnp.where(some, top + jnp.log(safe), far_below))
        mixed = [
            lax.dot_general(
                weight, key[:latent], (((1,), (1,)), ((), ())), preferred_element_type=jnp.float32
            )
            * scale
            for weight, key, scale in zip(weights, keys, scales)
        ]
        lse_all = lse_buf[...]
        for i, lse in enumerate(lses):
            lse_all = jnp.where(lane == second * unroll + i, lse, lse_all)
        lse_buf[...] = lse_all
        rows_count = unroll * head_local
        for k in range(owners):
            both = jnp.concatenate(
                [one[k * head_local : (k + 1) * head_local] for one in mixed], axis=0
            ).astype(jnp.bfloat16)
            for p in range(latent // LANES):
                rows_at = pl.multiple_of(p * group * head_local + second * rows_count, rows_count)
                obuf[spots[k], pl.ds(rows_at, rows_count), :] = both[:, p * LANES : (p + 1) * LANES]
        return carry

    lax.fori_loop(0, SIDE, several, 0)
    tail = latent // LANES * group * head_local
    parts = lse_parts(lse_buf[...])
    for k in range(owners):
        own = slice(k * head_local, (k + 1) * head_local)
        obuf[spots[k], tail:, :] = jnp.concatenate(
            [one[own] for one in parts] + [jnp.zeros_like(parts[0][own])], axis=0
        ).astype(jnp.bfloat16)
    copies = [
        pltpu.make_async_copy(obuf.at[pl.ds(d * SIDE, SIDE)], outs[d], sems.at[d])
        for d in range(SIDE)
    ]
    for one in copies:
        one.start()
    for one in copies:
        one.wait()


def lse_parts(value):
    high = value.astype(jnp.bfloat16).astype(jnp.float32)
    mid = (value - high).astype(jnp.bfloat16).astype(jnp.float32)
    return [high, mid, value - high - mid]


def attend(code_own, code_other, lengths, q_all, pieces, ranks, latent, head_local):
    per, _, head_total = q_all[0].shape
    width, block_len = pieces[0].shape[1:]
    heads = head_total // CORES
    blocks = sum(one.shape[0] for one in pieces)
    chips = SIDE * SIDE
    out_rows = latent // LANES * chips * CORES * head_local + 16
    count = len(pieces)
    dims = (blocks // ranks // CORES, ranks, head_local, latent, count)
    return pl.pallas_call(
        functools.partial(attend_kernel, dims),
        out_shape=(pltpu.VMEM((SIDE, out_rows, LANES), jnp.bfloat16),) * SIDE,
        in_specs=[smem_spec] * 3 + [hbm_spec] * (SIDE + count),
        out_specs=(vmem_spec,) * SIDE,
        scratch_shapes=[
            pltpu.VMEM((blocks, width, block_len), jnp.bfloat16),
            pltpu.VMEM((chips, width, head_total), jnp.bfloat16),
            pltpu.VMEM((chips, out_rows, LANES), jnp.bfloat16),
            pltpu.VMEM((heads, LANES), jnp.float32),
            pltpu.SemaphoreType.DMA((count + SIDE,)),
        ],
        compiler_params=pltpu.CompilerParams(vmem_limit_bytes=22 * MIB),
        cost_estimate=moves(20000000),
        name="attend",
    )(code_own, code_other, lengths, *[in_hbm(one) for one in q_all], *pieces)


def combine_shares(lses, sets, rows, group, head_local):
    merged, scaled = [], [None] * len(lses)
    for one_set in sets:
        peak = functools.reduce(jnp.maximum, [lses[s] for s in one_set])
        shares = [jnp.exp(lses[s] - peak) for s in one_set]
        total = functools.reduce(jnp.add, shares)
        merged.append(peak + jnp.log(total))
        inverse = 1.0 / total
        for s, share in zip(one_set, shares):
            scaled[s] = share * inverse
    share_all = jnp.concatenate(scaled, axis=0)
    count = len(lses) * head_local
    pick_request = jnp.where(
        lax.broadcasted_iota(jnp.int32, (rows, LANES), 0) // head_local
        == lax.broadcasted_iota(jnp.int32, (rows, LANES), 1),
        1.0,
        0.0,
    )
    valid = lax.broadcasted_iota(jnp.int32, (count, LANES), 1) < group
    spread = lax.dot_general(
        pick_request,
        jnp.where(valid, share_all, 0.0),
        (((1,), (1,)), ((), ())),
        precision=lax.Precision.HIGHEST,
        preferred_element_type=jnp.float32,
    )
    own_head = (
        lax.broadcasted_iota(jnp.int32, (rows, count), 0) % head_local
        == lax.broadcasted_iota(jnp.int32, (rows, count), 1) % head_local
    )
    pick_source = jnp.where(
        lax.broadcasted_iota(jnp.int32, (count, LANES), 0) // head_local
        == lax.broadcasted_iota(jnp.int32, (count, LANES), 1),
        1.0,
        0.0,
    )
    share = jnp.dot(
        jnp.where(own_head, spread, 0.0),
        pick_source,
        precision=lax.Precision.HIGHEST,
        preferred_element_type=jnp.float32,
    )
    return share, merged


def read_lse(tile, head_local):
    three = tile.astype(jnp.float32)
    return functools.reduce(
        jnp.add, [three[i * head_local : (i + 1) * head_local] for i in range(3)]
    )


def merge_kernel(dims, *refs):
    group, head_local, latent = dims
    ins, outs = refs[:SIDE], refs[SIDE + 1 :]
    rows = group * head_local
    pieces = latent // LANES
    tail = pieces * rows
    lses = [read_lse(one[e, tail:, :], head_local) for e in range(SIDE) for one in ins]
    sets = [[e * SIDE + s for s in range(SIDE)] for e in range(SIDE)]
    share, merged = combine_shares(lses, sets, rows, group, head_local)
    for e in range(SIDE):
        totals = [None] * pieces
        for s in range(SIDE):
            at = e * SIDE + s
            factor = jnp.broadcast_to(share[:, at : at + 1], (rows, LANES))
            for p in range(pieces):
                term = ins[s][e, p * rows : (p + 1) * rows, :].astype(jnp.float32) * factor
                totals[p] = term if s == 0 else totals[p] + term
        for p in range(pieces):
            outs[e][p * rows : (p + 1) * rows, :] = totals[p].astype(jnp.bfloat16)
        parts = lse_parts(merged[e])
        outs[e][tail:, :] = jnp.concatenate(parts + [jnp.zeros_like(parts[0])], axis=0).astype(
            jnp.bfloat16
        )


def merge(arrived, after, group, head_local, latent):
    shape = arrived[0].shape[1:]
    return pl.pallas_call(
        functools.partial(merge_kernel, (group, head_local, latent)),
        out_shape=(pltpu.VMEM(shape, jnp.bfloat16),) * SIDE,
        in_specs=[vmem_spec] * (SIDE + 1),
        out_specs=(vmem_spec,) * SIDE,
        compiler_params=pltpu.CompilerParams(vmem_limit_bytes=8 * MIB),
        cost_estimate=moves(4500000),
        name="merge",
    )(*[in_vmem(one) for one in arrived], after)


def scatter_tiles(flat, value, first_tile, group, tiles):
    for n in range(value.shape[1] // LANES):
        flat[pl.ds(first_tile + n, group, stride=tiles), :] = value[:, n * LANES : (n + 1) * LANES]


def project_kernel(dims, *refs):
    group, head_local, latent, chunk = dims
    parts = refs[:SIDE]
    w_value, w_out, kept, passed, att_buf, flat = refs[SIDE:]
    rows = group * head_local
    pieces = latent // LANES
    tiles = w_out.shape[1] // LANES
    tail = pieces * rows
    lses = [read_lse(one[tail:, :], head_local) for one in parts]
    share, _ = combine_shares(lses, [list(range(SIDE))], rows, group, head_local)
    totals = [None] * pieces
    for s in range(SIDE):
        factor = jnp.broadcast_to(share[:, s : s + 1], (rows, LANES))
        for p in range(pieces):
            term = parts[s][p * rows : (p + 1) * rows, :].astype(jnp.float32) * factor
            totals[p] = term if s == 0 else totals[p] + term
    for p in range(pieces):
        att_buf[p] = totals[p]
    heads = []
    for j in range(head_local):
        attended = jnp.concatenate(
            [att_buf[p, pl.ds(j, group, stride=head_local), :] for p in range(pieces)], axis=1
        ).astype(jnp.bfloat16)
        heads.append(
            jnp.dot(attended, w_value[j], preferred_element_type=jnp.float32).astype(jnp.bfloat16)
        )
    per_head = jnp.concatenate(heads, axis=1)
    for c in range(w_out.shape[1] // chunk):
        value = jnp.dot(
            per_head, w_out[:, c * chunk : (c + 1) * chunk], preferred_element_type=jnp.float32
        )
        scatter_tiles(flat, value, c * chunk // LANES, group, tiles)
    core = lax.axis_index("tensor") % CORES
    for chip in range(SIDE * SIDE):
        pair = jnp.where(core == 0, chip, chip % SIDE * SIDE + chip // SIDE)
        for out, side in ((kept, core), (passed, 1 - core)):
            at = pl.multiple_of((pair * CORES + side) * tiles, 8)
            out[chip] = flat[pl.ds(at, tiles), :].astype(jnp.bfloat16)


def project(parts, w_value, w_out, group):
    head_local, latent, _ = w_value.shape
    features = w_out.shape[1]
    tiles = features // LANES
    dims = (group, head_local, latent, features // 7)
    return pl.pallas_call(
        functools.partial(project_kernel, dims),
        out_shape=(pltpu.VMEM((group // CORES, tiles, LANES), jnp.bfloat16),) * CORES,
        in_specs=[vmem_spec] * (SIDE + 2),
        out_specs=(vmem_spec,) * CORES,
        scratch_shapes=[
            pltpu.VMEM((latent // LANES, group * head_local, LANES), jnp.float32),
            pltpu.VMEM((group * tiles, LANES), jnp.float32),
        ],
        compiler_params=pltpu.CompilerParams(vmem_limit_bytes=12 * MIB),
        cost_estimate=moves(9000000),
        name="project",
    )(*[in_vmem(one) for one in parts], w_value, w_out)


def add_kernel(one, other, out):
    for s in range(out.shape[0]):
        out[s] = (one[s].astype(jnp.float32) + other[s].astype(jnp.float32)).astype(out.dtype)


def add(one, other):
    return pl.pallas_call(
        add_kernel,
        out_shape=pltpu.VMEM(one.shape, one.dtype),
        in_specs=[vmem_spec] * 2,
        out_specs=vmem_spec,
        compiler_params=pltpu.CompilerParams(vmem_limit_bytes=4 * MIB),
        cost_estimate=moves(700000),
        name="add",
    )(in_vmem(one), in_vmem(other))


def norm_kernel(got, residual, gain, kept, normed):
    total = residual[...]
    for s in range(got.shape[0]):
        total = total + got[s].astype(jnp.float32)
    kept[...] = total
    mean = jnp.sum(total * total) * (1.0 / total.size)
    value = (total * lax.rsqrt(mean + norm_eps) * gain[...]).astype(jnp.bfloat16)
    for s in range(normed.shape[0]):
        normed[s] = value


def norm(got, residual, gain):
    return pl.pallas_call(
        norm_kernel,
        out_shape=(pltpu.VMEM(residual.shape, jnp.float32), pltpu.VMEM(got.shape, got.dtype)),
        in_specs=[vmem_spec] * 3,
        out_specs=(vmem_spec, vmem_spec),
        compiler_params=pltpu.CompilerParams(vmem_limit_bytes=8 * MIB),
        cost_estimate=moves(700000),
        name="norm",
    )(in_vmem(got), in_vmem(residual), in_vmem(gain))


def ffn_kernel(chunk, *refs):
    normed, (w_gate, w_up, w_down) = refs[:CORES], refs[CORES : CORES + 3]
    outs, (flat, wide) = refs[CORES + 3 : 2 * CORES + 3], refs[2 * CORES + 3 :]
    half, tiles, _ = normed[0].shape
    group = CORES * half
    for c in range(CORES):
        for r in range(half):
            at = (c * half + r) * tiles
            flat[at : at + tiles, :] = normed[c][r].astype(jnp.float32)
    for n in range(tiles):
        wide[:, n * LANES : (n + 1) * LANES] = flat[pl.ds(n, group, stride=tiles), :].astype(
            jnp.bfloat16
        )
    gate = jnp.dot(wide[...], w_gate[...], preferred_element_type=jnp.float32)
    up = jnp.dot(wide[...], w_up[...], preferred_element_type=jnp.float32)
    activated = (gate / (1.0 + jnp.exp(-gate)) * up).astype(jnp.bfloat16)
    for c in range(w_down.shape[1] // chunk):
        value = jnp.dot(
            activated, w_down[:, c * chunk : (c + 1) * chunk], preferred_element_type=jnp.float32
        )
        scatter_tiles(flat, value, c * chunk // LANES, group, tiles)
    for c in range(CORES):
        for r in range(half):
            at = (c * half + r) * tiles
            outs[c][r] = flat[at : at + tiles, :].astype(jnp.bfloat16)


def ffn(normed, w_gate, w_up, w_down):
    half, tiles, _ = normed[0].shape
    group, features = CORES * half, tiles * LANES
    return pl.pallas_call(
        functools.partial(ffn_kernel, features // 7),
        out_shape=(pltpu.VMEM(normed[0].shape, jnp.bfloat16),) * CORES,
        in_specs=[vmem_spec] * (CORES + 3),
        out_specs=(vmem_spec,) * CORES,
        scratch_shapes=[
            pltpu.VMEM((group * tiles, LANES), jnp.float32),
            pltpu.VMEM((group, features), jnp.bfloat16),
        ],
        compiler_params=pltpu.CompilerParams(vmem_limit_bytes=12 * MIB),
        cost_estimate=moves(17000000),
        name="ffn",
    )(*[in_vmem(one) for one in normed], w_gate, w_up, w_down)


def finish_kernel(kept, got, out):
    total = kept[...]
    for s in range(got.shape[0]):
        total = total + got[s].astype(jnp.float32)
    for n in range(total.shape[0]):
        out[:, n * LANES : (n + 1) * LANES] = total[n : n + 1, :]


def finish(kept, got):
    return pl.pallas_call(
        finish_kernel,
        out_shape=jax.ShapeDtypeStruct((1, kept.size), jnp.float32),
        in_specs=[vmem_spec] * 2,
        out_specs=vmem_spec,
        compiler_params=pltpu.CompilerParams(vmem_limit_bytes=4 * MIB),
        cost_estimate=moves(300000),
        name="finish",
    )(in_vmem(kept), in_vmem(got))


def body(
    queries,
    cache_pool,
    holder,
    slot_ids,
    lengths,
    residual,
    w_value,
    w_out,
    norm_gain,
    w_gate,
    w_up,
    w_down,
):
    ranks = lax.axis_size("dp")
    tensors = lax.axis_size("tensor")
    column = lax.axis_index("tensor")
    group = residual.shape[0]
    slots = cache_pool.shape[0]
    head_local, latent, _ = w_value.shape
    features = residual.shape[1]
    tiles = features // LANES
    requests = lengths.shape[0]
    swap = [(i, i ^ 1) for i in range(tensors)]
    from_next = [((i + 1) % ranks, i) for i in range(ranks)]
    from_prev = [((i - 1) % ranks, i) for i in range(ranks)]

    def swapped(value):
        return lax.ppermute(value, "tensor", swap)

    def along(value, first, distance):
        return lax.ppermute(value, "tensor", shifts(tensors, first, distance))

    own_queries = queries[0]
    other_queries = swapped(own_queries)
    q_pair = turn(own_queries, other_queries)
    following = lax.ppermute(cache_pool, "dp", from_next)
    previous = lax.ppermute(cache_pool, "dp", from_prev)
    q_line = join([q_pair] + [along(q_pair, True, d) for d in range(1, SIDE)])
    q_all = [q_line] + [along(q_line, False, e) for e in range(1, SIDE)]
    far_low = lax.ppermute(cut(following, 0), "dp", from_next)
    far_high = lax.ppermute(cut(previous, slots // 2), "dp", from_prev)
    mine = [following, far_low, far_high, previous]
    moved = [in_vmem(swapped(one)) for one in mine]
    mine = [in_vmem(one) for one in mine]
    pieces = [in_hbm(cache_pool)] + mine + [in_hbm(swapped(cache_pool))] + moved
    code = (holder * slots + slot_ids).reshape(1, requests)
    code_other = swapped(code)
    own_residual = (
        lax.dynamic_index_in_dim(residual, column, 0, keepdims=False)
        .astype(jnp.float32)
        .reshape(tiles, LANES)
    )
    gain = norm_gain.reshape(tiles, LANES)
    q_all, own_residual, gain = lax.optimization_barrier((q_all, own_residual, gain))
    w_value, w_gate, w_up, w_down = [
        in_vmem(one) for one in (w_value, w_gate, w_up, w_down)
    ]
    partial = attend(
        code,
        code_other,
        lengths.reshape(1, requests),
        q_all,
        pieces,
        ranks,
        latent,
        head_local,
    )
    w_out = fetch(w_out, partial[0])
    opposite = along(partial[2], True, 2)
    one_on, one_back = along(partial[1], True, 1), along(partial[3], True, 3)
    arrived = [partial[0], opposite, one_on, one_back]
    merged = merge(arrived, w_out, group, head_local, latent)
    opposite = along(merged[2], False, 2)
    parts = [merged[0], opposite, along(merged[1], False, 1), along(merged[3], False, 3)]

    chips = SIDE * SIDE
    same_core = [[c + CORES * k for k in range(chips)] for c in range(CORES)]

    def exchange(value):
        return lax.all_to_all(
            value, "tensor", split_axis=0, concat_axis=0, tiled=True, axis_index_groups=same_core
        )

    def to_rows(kept, passed):
        return exchange(add(kept, swapped(passed)))

    residual_sum, normed = norm(
        to_rows(*project(parts, w_value, w_out, group)), own_residual, gain
    )
    rows = exchange(normed)
    down = to_rows(*ffn((rows, swapped(rows)), w_gate, w_up, w_down))
    return finish(residual_sum, down)


def solution(mesh):
    in_specs = (
        P(("dp", "tensor"), None, None),
        P(("dp", "tensor"), None, None),
        P(None, "tensor"),
        P(None, "tensor"),
        P(),
        P("dp", None),
        P("tensor", None, None),
        P("tensor", None),
        P(),
        P(None, "tensor"),
        P(None, "tensor"),
        P("tensor", None),
    )
    out_specs = P(("dp", "tensor"), None)
    return jax.shard_map(body, mesh=mesh, in_specs=in_specs, out_specs=out_specs, check_vma=False)
```
